32 devices in a mesh: ctx: 8 (over z, x), wsh: 4 (over y, core).
Axes of the slice: x: 2, y: 2, z: 4, core: 2. Of those that a mesh axis runs over, the one named last changes fastest.
Arguments:
- tokens: bfloat16 [4, 2048, 1024], P('wsh', 'ctx'), may hold values from -6 to 6
- segments: int32 [4, 2048], P('wsh', 'ctx'), may hold values from 0 to 3, never falling along the last dimension, each value on 1 to 1024 neighbouring positions
- routes: int32 [4, 2048, 8], P('wsh', 'ctx'), may hold values from 0 to 15, all different within a row; in each aligned block of 256 rows (0 to 255, 256 to 511, ..., all dimensions but the last counted through in order) at most 192 rows name the same one
- gate_weights: float32 [4, 2048, 8], P('wsh', 'ctx'), may hold values from 0.05 to 0.25
- cotangent: bfloat16 [4, 2048, 1024], P('wsh', 'ctx'), may hold values from -6 to 6
- owners: int32 [54], replicated, may hold values from 0 to 79, as said below
- masters: float32 [80, 1024, 512], P('wsh', 'ctx'), may hold values from -8 to 8
- first_moments: float32 [80, 1024, 512], P('wsh', 'ctx'), may hold values from -16384 to 16384
- second_moments: float32 [80, 1024, 512], P('wsh', 'ctx'), may hold values from 0 to 32768, as said below
- norm_gains: float32 [2, 1024], replicated, may hold values from 0.5 to 1.5
- gain_first: float32 [2, 1024], replicated, may hold values from -32768 to 32768
- gain_second: float32 [2, 1024], replicated, may hold values from 0 to 131072, as said below
Outputs:
- output: bfloat16 [4, 2048, 1024], P('wsh', 'ctx')
- input_grad: float32 [4, 2048, 1024], P('wsh', 'ctx')
- new_masters: float32 [80, 1024, 512], P('wsh', 'ctx')
- new_first: float32 [80, 1024, 512], P('wsh', 'ctx')
- new_second: float32 [80, 1024, 512], P('wsh', 'ctx')
- new_gains: float32 [2, 1024], replicated
- new_gain_first: float32 [2, 1024], replicated
- new_gain_second: float32 [2, 1024], replicated
The draws below stay inside these ranges and needn't reach their ends.
Inputs may be any that keep to these rules, and one draw needn't show every extreme that they name: `owners`: the entries are distinct; slot s belongs to index s // 20 of wsh; one index of wsh holds exactly 20 of the matrices. `segments`: documents are numbered in order within each sequence; each has at most 1024 positions and one of each sequence has exactly 1024. `routes`: the 8 experts of a position are distinct; among the 256 positions of one device no expert is named more than 192 times, and some expert is named 192 times. `second_moments`: every entry is positive. `gain_second`: every entry is positive.
All inputs are finite; a program needn't handle non-finite values.
Results may differ from the reference program's by a relative error of at most 0.024.
Values may be sent and summed in bfloat16 or wider, within the bound.
No kernel may reach another device: no remote copies, remote signals or barrier semaphores. Data moves between devices by JAX's collectives and lax.ppermute only.
A program may use at most 256 MiB of HBM per device.

```python
import math
import jax
import jax.numpy as jnp
import numpy as np
from jax import lax

D = 1024
QH = 16
KVH = 8
HD = 64
EH = 512
TOPK = 8
SEG = 256
REACH = 4
SLOTS = 20
STEP = 7
EXPERTS = 16
LEN = 2048
SEQ_TOT = 4
DOC_MAX = 1024
DOCS = 4
CAP = 192
N_CTX = 8
N_WSH = 4


def slot_layout(key):
    matrix_count = 6 + 3 * EXPERTS
    slot_total = N_WSH * SLOTS
    k_busy, k_order, k_own, k_rest = jax.random.split(jax.random.fold_in(key, 7), 4)
    busiest = jax.random.randint(k_busy, (), 0, N_WSH)
    order = jax.random.permutation(k_order, matrix_count)
    own_slots = busiest * SLOTS + jax.random.permutation(k_own, SLOTS)
    rest_slots = jnp.arange(slot_total - SLOTS)
    rest_slots = rest_slots + jnp.where(rest_slots >= busiest * SLOTS, SLOTS, 0)
    rest_slots = jax.random.permutation(k_rest, rest_slots)
    chosen = jnp.concatenate([own_slots, rest_slots[:matrix_count - SLOTS]]).astype(jnp.int32)
    return jnp.zeros((matrix_count,), jnp.int32).at[order].set(chosen)


def slot_kind(key):
    owners = slot_layout(key)
    table = jnp.array([0, 0, 1, 2, 3, 3] + [4, 5, 6] * EXPERTS, jnp.int32)
    return jnp.full((N_WSH * SLOTS,), 7, jnp.int32).at[owners].set(table)


def init_scale():
    base_scale = D ** (-0.5)
    return jnp.array([base_scale, base_scale, base_scale, 4.0 * (2 * EH) ** (-0.5), base_scale, base_scale, 6.0 * EH ** (-0.5), base_scale], jnp.float32)


def grad_scale():
    positions = SEQ_TOT * LEN
    routed = positions * TOPK / EXPERTS
    full_root = math.sqrt(positions)
    routed_root = math.sqrt(routed)
    return jnp.array([0.5 * full_root, 0.7 * full_root, 0.7 * full_root, 0.2 * full_root, 0.5 * routed_root, 0.5 * routed_root, 0.07 * routed_root, 0.5 * full_root], jnp.float32)


def draw_owners(key, part):
    return slot_layout(key)


def draw_masters(key, part):
    kinds = slot_kind(key)
    normal_vals = jax.random.truncated_normal(jax.random.fold_in(key, 21), -4.0, 4.0, (N_WSH * SLOTS, D, EH), jnp.float32)
    return normal_vals * init_scale()[kinds][:, None, None]


def draw_first_moments(key, part):
    kinds = slot_kind(key)
    spread = jax.random.uniform(jax.random.fold_in(key, 31), (N_WSH * SLOTS, D, EH), jnp.float32, -1.5, 1.5)
    return spread * grad_scale()[kinds][:, None, None]


def draw_second_moments(key, part):
    kinds = slot_kind(key)
    factor = jnp.exp(jax.random.uniform(jax.random.fold_in(key, 41), (N_WSH * SLOTS, D, EH), jnp.float32, 0.0, math.log(4.0)))
    sizes = grad_scale()[kinds][:, None, None]
    return factor * sizes * sizes * (0.4 / 0.6)


def gain_scale():
    return math.sqrt(SEQ_TOT * LEN) * jnp.array([1.0, 2.0], jnp.float32)[:, None]


def draw_gain_first(key, part):
    spread = jax.random.uniform(jax.random.fold_in(key, 51), (2, D), jnp.float32, -1.5, 1.5)
    return spread * gain_scale()


def draw_gain_second(key, part):
    factor = jnp.exp(jax.random.uniform(jax.random.fold_in(key, 61), (2, D), jnp.float32, 0.0, math.log(4.0)))
    sizes = gain_scale()
    return factor * sizes * sizes * (0.4 / 0.6)


def levels(key, dims, pieces, least, largest):
    gain = 1.0
    for axis_at, parts in pieces:
        steps = jax.random.uniform(jax.random.fold_in(jax.random.fold_in(key, 6), axis_at), (parts,), jnp.float32, least / len(pieces), largest / len(pieces))
        gain = gain * jnp.repeat(jnp.exp(steps), dims[axis_at] // parts).reshape((-1,) + (1,) * (len(dims) - 1 - axis_at))
    return gain


def profile(amount, total, reach, lean):
    loads = [(1 << 20) // math.isqrt(grade ** lean) + 1 for grade in range(2, amount + 1)]
    spare, holding = total - reach - (amount - 1), [1] * (amount - 1)
    while spare > 0:
        candidates = [i for i in range(amount - 1) if holding[i] < reach]
        pool, left = sum([loads[i] for i in candidates]), spare
        for i in candidates:
            more = min(reach - holding[i], max(1, left * loads[i] // pool), spare)
            holding[i] = holding[i] + more
            spare = spare - more
    return np.array([reach] + holding)


def ragged(stream_key, count, total, reach, slope):
    if count == 2:
        one = jax.random.randint(stream_key, (), max(1, total - reach), min(reach, total - 1) + 1)
        return jnp.stack([one, total - one])
    sizes = jnp.asarray(profile(count, total, reach, slope), jnp.int32)
    couples = (count - 1) // 2
    donor, receiver = sizes[1:1 + 2 * couples:2], sizes[2:2 + 2 * couples:2]
    room = jnp.minimum(donor - 1, reach - receiver)
    passed = jax.random.randint(jax.random.fold_in(stream_key, 1), (couples,), 0, 1 << 20) % (room + 1)
    sizes = sizes.at[1:1 + 2 * couples:2].set(donor - passed).at[2:2 + 2 * couples:2].set(receiver + passed)
    return sizes[jax.random.permutation(jax.random.fold_in(stream_key, 2), count)]


def routed_block(stream_key, own, number, rows, count, top, bound, lean):
    ranking = jax.random.permutation(stream_key, count)
    heavy_load, ordinary = portions_of(count, rows * top, bound, lean, True), portions_of(count, rows * top, bound, lean, False)
    places = jnp.arange(count)

    def named(sizes, rotation):
        used = int((sizes > 0).sum())
        fixed = max(1, used // 4)
        passed = fixed + (places - fixed + rotation * (used - fixed)) % max(1, count - fixed)
        return jnp.zeros((count,), jnp.int32).at[ranking[jnp.where(places < fixed, places, passed)]].set(jnp.asarray(sizes, jnp.int32))

    sizes = jnp.where(number % 4 == 0, named(heavy_load, number // 4), named(ordinary, number - number // 4 - 1))
    mixed = jax.random.permutation(jax.random.fold_in(own, 3), count)
    source_of, receiver = mixed[0:count // 2 * 2:2], mixed[1:count // 2 * 2:2]
    room = jnp.minimum(sizes[source_of] - 1, bound - sizes[receiver]) // 2
    room = jnp.where((source_of == ranking[0]) | (receiver == ranking[0]) | (sizes[receiver] == 0), 0, jnp.maximum(room, 0))
    passed = jax.random.randint(jax.random.fold_in(own, 4), (count // 2,), 0, 1 << 20) % (room + 1)
    sizes = sizes.at[source_of].add(-passed).at[receiver].add(passed)
    items = jnp.searchsorted(jnp.cumsum(sizes), jnp.arange(rows * top), side="right").astype(jnp.int32)
    listing = items.reshape(top, rows).T
    listing = listing[jax.random.permutation(jax.random.fold_in(own, 1), rows)]
    rotation = jax.random.randint(jax.random.fold_in(own, 2), (rows, 1), 0, top)
    return jnp.take_along_axis(listing, (jnp.arange(top)[None, :] + rotation) % top, axis=1)


def portions_of(count, total, limit, skew, full):
    loads = [(1 << 20) // math.isqrt(grade ** skew) + 1 for grade in range(1, count + 1)]
    largest = limit if full else min(limit, max(-(-total // count), total * loads[0] // sum(loads)))
    least = 1 if total - largest >= count - 1 else 0
    counts, surplus = [largest] + [least] * (count - 1), total - largest - least * (count - 1)
    while surplus > 0:
        candidates = [i for i in range(1, count) if counts[i] < largest] or [i for i in range(1, count) if counts[i] < limit]
        mass, budget = sum([loads[i] for i in candidates]), surplus
        for i in candidates:
            extra = min(limit - counts[i], max(1, budget * loads[i] // mass), surplus)
            counts[i] = counts[i] + extra
            surplus = surplus - extra
    return np.array(counts)


def scatter_about(own_key, extent, scale, limit, pieces=(), kind=jnp.bfloat16):
    values = jax.random.normal(own_key, extent, jnp.float32) * scale
    if len(pieces) > 0:
        values = levels(own_key, extent, pieces, -0.22, 0.18) * values
    return jnp.clip(values, min=-limit, max=limit).astype(kind)


def setup_inputs(seed: int = 0) -> dict:
    seeds = jax.random.split(jax.random.key(seed), 13)
    tokens = scatter_about(seeds[0], (SEQ_TOT, LEN, D), 1.0, 6.0, ((0, 4), (1, 8)))
    segments = jax.vmap(lambda own: jnp.searchsorted(jnp.cumsum(ragged(own, DOCS, LEN, DOC_MAX, 2)), jnp.arange(LEN), side="right"))(jax.random.split(seeds[1], SEQ_TOT)).reshape((SEQ_TOT, LEN)).astype(jnp.int32)
    routes_keys = jax.random.split(jax.random.fold_in(seeds[2], 1), SEQ_TOT * LEN // SEG)
    routes_turns = jax.random.permutation(jax.random.fold_in(seeds[2], 3), SEQ_TOT * LEN // SEG)
    routes = jax.vmap(lambda own, number: routed_block(jax.random.fold_in(seeds[2], 2), own, number, SEG, EXPERTS, TOPK, CAP, 1))(routes_keys, routes_turns).reshape((SEQ_TOT, LEN, TOPK))
    gate_weights = jnp.clip(jnp.exp(math.log(0.25) - 1.609438 * jax.random.uniform(seeds[3], (SEQ_TOT, LEN, TOPK), jnp.float32) ** levels(seeds[3], (SEQ_TOT, LEN, TOPK), ((0, 4), (1, 8)), -0.2, 0.2)), 0.05, 0.25)
    cotangent = scatter_about(seeds[4], (SEQ_TOT, LEN, D), 1.0, 6.0, ((0, 4), (1, 8)))
    owners = draw_owners(jax.random.fold_in(seeds[12], 71), 0)
    masters = draw_masters(jax.random.fold_in(seeds[12], 71), 0)
    first_moments = draw_first_moments(jax.random.fold_in(seeds[12], 71), 0)
    second_moments = draw_second_moments(jax.random.fold_in(seeds[12], 71), 0)
    norm_gains = jnp.clip(1.0 + 0.1 * jax.random.normal(seeds[9], (2, D), jnp.float32), 0.5, 1.5)
    gain_first = draw_gain_first(jax.random.fold_in(seeds[12], 71), 0)
    gain_second = draw_gain_second(jax.random.fold_in(seeds[12], 71), 0)
    return {"tokens": tokens, "segments": segments, "routes": routes, "gate_weights": gate_weights, "cotangent": cotangent, "owners": owners, "masters": masters, "first_moments": first_moments, "second_moments": second_moments, "norm_gains": norm_gains, "gain_first": gain_first, "gain_second": gain_second}


@jax.custom_vjp
def low(v):
    return lax.optimization_barrier(v.astype(jnp.bfloat16)).astype(jnp.float32)

@jax.custom_vjp
def low_back(v):
    return v

def low_keep(v):
    return (low(v), None)

def low_pass(kept, grad):
    return (grad,)

def back_keep(v):
    return (v, None)

def back_low(kept, grad):
    return (low(grad),)
low.defvjp(low_keep, low_pass)
low_back.defvjp(back_keep, back_low)
EPS_NORM = 1e-05
THETA = 10000.0
BETA_ONE = 0.5
BETA_TWO = 0.6
ADAM_EPS = 1e-08
DECAY = 0.1
GAIN_RATE = 0.3
NEG_BIG = -1e+30
HIGH = lax.Precision.HIGHEST

def matmul(left, right):
    return jnp.dot(left, right, precision=HIGH, preferred_element_type=jnp.float32)

def normalize(values, gain_row):
    scale_row = lax.rsqrt(lax.optimization_barrier(jnp.mean(values * values, axis=-1, keepdims=True)) + EPS_NORM)
    return values * scale_row * gain_row

def rotate_half(vector):
    half_width = vector.shape[-1] // 2
    return jnp.concatenate([-vector[..., half_width:], vector[..., :half_width]], axis=-1)

def rotary_tables(positions):
    inverse = THETA ** (-(jnp.arange(HD // 2, dtype=jnp.float32) * 2.0 / HD))
    angles = positions.astype(jnp.float32)[:, None] * inverse[None, :]
    cosine = jnp.concatenate([jnp.cos(angles), jnp.cos(angles)], axis=-1)[:, None, :]
    sine_table = jnp.concatenate([jnp.sin(angles), jnp.sin(angles)], axis=-1)[:, None, :]
    return (cosine, sine_table)

def rotary(vector, cosine, sine_table):
    return vector * cosine + rotate_half(vector) * sine_table

def kind_rates(width, hidden):
    base_rate = 0.5 * width ** (-0.5)
    return jnp.array([base_rate, base_rate, base_rate, 2.0 * (2 * hidden) ** (-0.5), base_rate, base_rate, 3.0 * hidden ** (-0.5), base_rate], jnp.float32)

def slot_kinds(owners, slot_total):
    count = (owners.shape[0] - 6) // 3
    table = jnp.asarray(np.array([0, 0, 1, 2, 3, 3] + [4, 5, 6] * count, np.int32))
    return jnp.full((slot_total,), 7, jnp.int32).at[owners].set(table)

def adamw(weight, first, second, grad, rate, decay):
    first_new = BETA_ONE * first + (1.0 - BETA_ONE) * grad
    second_new = BETA_TWO * second + (1.0 - BETA_TWO) * grad * grad
    first_hat = first_new / (1.0 - BETA_ONE ** STEP)
    second_hat = second_new / (1.0 - BETA_TWO ** STEP)
    weight_new = weight - rate * (first_hat / (jnp.sqrt(second_hat) + ADAM_EPS) + decay * weight)
    return (weight_new, first_new, second_new)

def attend(queries_turned, keys_turned, values_low, seg_ids):
    margin = REACH * SEG
    window = (REACH + 1) * SEG
    scale_score = HD ** (-0.5)
    keys_pad = jnp.pad(keys_turned, ((margin, 0), (0, 0), (0, 0)))
    values_pad = jnp.pad(values_low, ((margin, 0), (0, 0), (0, 0)))
    seg_pad = jnp.pad(seg_ids, (margin, 0), constant_values=-1)

    def block_out(index):
        start = (index * SEG).astype(jnp.int32)
        query_blk = lax.dynamic_slice_in_dim(queries_turned, start, SEG, 0)
        key_blk = lax.dynamic_slice_in_dim(keys_pad, start, window, 0)
        value_blk = lax.dynamic_slice_in_dim(values_pad, start, window, 0)
        key_seg = lax.dynamic_slice_in_dim(seg_pad, start, window, 0)
        query_seg = lax.dynamic_slice_in_dim(seg_ids, start, SEG, 0)
        query_pos = start + jnp.arange(SEG, dtype=jnp.int32)
        key_pos = start - margin + jnp.arange(window, dtype=jnp.int32)
        allowed = (key_pos[None, :] <= query_pos[:, None]) & (key_seg[None, :] == query_seg[:, None])
        scores = low_back(jnp.einsum('qgrd,kgd->grqk', query_blk, key_blk, precision=HIGH)) * scale_score
        scores = jnp.where(allowed, scores, NEG_BIG)
        probs_low = low(jax.nn.softmax(scores, axis=-1))
        mixed = jnp.einsum('grqk,kgd->qgrd', probs_low, value_blk, precision=HIGH)
        return mixed.reshape(SEG, QH * HD)
    blocks = lax.map(jax.checkpoint(block_out), jnp.arange(N_CTX, dtype=jnp.int32))
    return blocks.reshape(N_CTX * SEG, QH * HD)

def forward_seq(tokens_f, seg_ids, route_ids, gate_vals, norm_gains, matrices):
    weights_low = low(matrices)
    w_query = jnp.concatenate([weights_low[0], weights_low[1]], axis=1)
    w_key = weights_low[2]
    w_value = weights_low[3]
    w_out = jnp.concatenate([weights_low[4], weights_low[5]], axis=1)
    attn_in = low(normalize(tokens_f, norm_gains[0]))
    queries = low_back(matmul(attn_in, w_query))
    keys_raw = low_back(matmul(attn_in, w_key))
    values_low = low(low_back(matmul(attn_in, w_value)))
    cosine, sine_table = rotary_tables(jnp.arange(N_CTX * SEG, dtype=jnp.int32))
    queries_turned = low(rotary(queries.reshape(-1, QH, HD), cosine, sine_table)).reshape(-1, KVH, 2, HD)
    keys_turned = low(rotary(keys_raw.reshape(-1, KVH, HD), cosine, sine_table))
    attn_mix = low(low_back(attend(queries_turned, keys_turned, values_low.reshape(-1, KVH, HD), seg_ids)))
    attn_out = low_back(matmul(attn_mix, w_out.T))
    resid_one = tokens_f + attn_out
    expert_in = low(normalize(resid_one, norm_gains[1]))
    hits = (route_ids[:, :, None] == jnp.arange(EXPERTS, dtype=jnp.int32)[None, None, :]).astype(jnp.float32)
    combine = lax.optimization_barrier(jnp.sum(gate_vals[:, :, None] * hits, axis=1))
    stacked = weights_low[6:].reshape(EXPERTS, 3, D, EH)

    def one_expert(total, inputs):
        w_gate, w_up, w_down, share = inputs
        gate_pre = low_back(matmul(expert_in, w_gate))
        up_pre = low_back(matmul(expert_in, w_up))
        hidden_low = low(jax.nn.silu(gate_pre) * up_pre)
        result = low(low_back(matmul(hidden_low, w_down.T)))
        return (total + share[:, None] * result, None)
    mixed_sum, unused = lax.scan(jax.checkpoint(one_expert), jnp.zeros_like(resid_one), (stacked[:, 0], stacked[:, 1], stacked[:, 2], combine.T))
    return resid_one + mixed_sum

def reference(tokens, segments, routes, gate_weights, cotangent, owners, masters, first_moments, second_moments, norm_gains, gain_first, gain_second):
    matrices = jnp.take(masters, owners, axis=0)

    def one_sequence(carry, inputs):
        seq_tokens, seq_segs, seq_routes, seq_gates, seq_cot = inputs

        def forward(tokens_f, gains_f, mats_f):
            return forward_seq(tokens_f, seq_segs, seq_routes, seq_gates, gains_f, mats_f)
        result, pullback = jax.vjp(forward, seq_tokens.astype(jnp.float32), norm_gains, matrices)
        grad_tokens, grad_gains, grad_mats = pullback(seq_cot.astype(jnp.float32))
        return ((carry[0] + grad_gains, carry[1] + grad_mats), (result.astype(jnp.bfloat16), grad_tokens))
    start_carry = (jnp.zeros_like(norm_gains), jnp.zeros_like(matrices))
    (gain_grad, mat_grad), (output, input_grad) = lax.scan(one_sequence, start_carry, (tokens, segments, routes, gate_weights, cotangent))
    slot_grad = jnp.zeros_like(masters).at[owners].set(mat_grad)
    rates = kind_rates(D, EH)[slot_kinds(owners, masters.shape[0])][:, None, None]
    new_masters, new_first, new_second = adamw(masters, first_moments, second_moments, slot_grad, rates, DECAY)
    new_gains, new_gain_first, new_gain_second = adamw(norm_gains, gain_first, gain_second, gain_grad, GAIN_RATE, 0.0)
    return (output, input_grad, new_masters, new_first, new_second, new_gains, new_gain_first, new_gain_second)
```

```python
import jax
import jax.numpy as jnp
import numpy as np
from jax import lax
from jax.experimental import pallas as pl
from jax.experimental.pallas import tpu as pltpu
from jax.sharding import Mesh
from jax.sharding import PartitionSpec as P

QH = 16
KVH = 8
HD = 64
STEP = 7

EPS_NORM = 1e-05
THETA = 10000.0
BETA_ONE = 0.5
BETA_TWO = 0.6
ADAM_EPS = 1e-08
DECAY = 0.1
GAIN_RATE = 0.3
NEG_BIG = -1e30
PLANE = ("x", "y", "c")
WSH = ("y", "c")
BF = jnp.bfloat16
F32 = jnp.float32


def swap(value, axis):
    return lax.ppermute(value, axis, [(0, 1), (1, 0)])


def shift(value, by):
    count = lax.axis_size("z")
    pairs = [(i, i + by) for i in range(count) if 0 <= i + by < count]
    return lax.ppermute(value, "z", pairs)


def plane_gather(rows):
    half = rows.shape[0] // 2
    over_x = swap(rows, "x")
    over_y = swap(rows, "y")
    corner_top = swap(over_x[:half], "y")
    corner_low = swap(over_y[half:], "x")
    mine = jnp.concatenate([rows, over_x, over_y, corner_top, corner_low], axis=0)
    other = swap(mine, "c")
    return jnp.concatenate([mine, other], axis=0)


def plane_reduce(part):
    whole = part.shape[0]
    step = whole // 8
    half = step // 2
    got = swap(part[whole // 2 :], "c")
    total = part[: whole // 2].astype(F32) + got.astype(F32)
    own = total[:step]
    to_x = total[step : 2 * step]
    to_y = total[2 * step : 3 * step]
    corner = total[3 * step :].astype(BF)
    for_x = swap(corner[:half], "y").astype(F32)
    for_y = swap(corner[half:], "x").astype(F32)
    to_x = jnp.concatenate([to_x[:half] + for_x, to_x[half:]], axis=0).astype(BF)
    to_y = jnp.concatenate([to_y[:half], to_y[half:] + for_y], axis=0).astype(BF)
    return own + swap(to_x, "x").astype(F32) + swap(to_y, "y").astype(F32)


def sum_everywhere(value):
    for axis in ("c", "x", "y"):
        value = value + swap(value, axis)
    count = lax.axis_size("z")
    if count & (count - 1):
        return lax.psum(value, "z")
    stride = 1
    while stride < count:
        value = value + lax.ppermute(value, "z", [(i, i ^ stride) for i in range(count)])
        stride *= 2
    return value


def norm_scale(values):
    return lax.rsqrt(jnp.mean(values * values, axis=-1, keepdims=True) + EPS_NORM)


def norm_back(values, scale_row, gain_row, grad_out):
    gain_grad = jnp.sum(grad_out * values * scale_row, axis=0)
    weighted = grad_out * gain_row
    grad_in = scale_row * weighted - values * scale_row**3 * jnp.mean(
        values * weighted, axis=-1, keepdims=True
    )
    return (grad_in, gain_grad)


def kind_rates(width, hidden):
    base_rate = 0.5 * width ** (-0.5)
    return [
        base_rate,
        base_rate,
        base_rate,
        2.0 * (2 * hidden) ** (-0.5),
        base_rate,
        base_rate,
        3.0 * hidden ** (-0.5),
        base_rate,
    ]


def adamw(weight, first, second, grad, rate, decay):
    first_new = BETA_ONE * first + (1.0 - BETA_ONE) * grad
    second_new = BETA_TWO * second + (1.0 - BETA_TWO) * grad * grad
    first_hat = first_new / (1.0 - BETA_ONE**STEP)
    second_hat = second_new / (1.0 - BETA_TWO**STEP)
    weight_new = weight - rate * (first_hat / (jnp.sqrt(second_hat) + ADAM_EPS) + decay * weight)
    return (weight_new, first_new, second_new)


def dot_nn(left, right):
    return lax.dot_general(left, right, (((1,), (0,)), ((), ())), preferred_element_type=F32)


def dot_nt(left, right):
    return lax.dot_general(left, right, (((1,), (1,)), ((), ())), preferred_element_type=F32)


def dot_tn(left, right):
    return lax.dot_general(left, right, (((0,), (0,)), ((), ())), preferred_element_type=F32)


def turn(value, lane):
    low = (lane % HD) < (HD // 2)
    return jnp.where(
        low, -pltpu.roll(value, 2 * HD - HD // 2, 1), pltpu.roll(value, HD // 2, 1)
    )


def project_kernel(x_ref, w_ref, cos_ref, sin_ref, q_ref, kv_ref):
    both = dot_nn(x_ref[...], w_ref[...])
    cosine = cos_ref[0]
    sine = sin_ref[0]
    lane = lax.broadcasted_iota(jnp.int32, cosine.shape, 1)
    query = both[:, : 2 * HD]
    pair = both[:, 2 * HD :]
    q_ref[...] = (query * cosine + turn(query, lane) * sine).astype(BF)
    turned = pair * cosine + turn(pair, lane) * sine
    kv_ref[...] = jnp.where(lane < HD, turned, pair).astype(BF)


def project(x_rows, w_pair, cosine, sine, block):
    rows = x_rows.shape[0]
    width = w_pair.shape[0]
    table = pl.BlockSpec((1, block, 2 * HD), lambda i: (i % 2, 0, 0))
    return pl.pallas_call(
        project_kernel,
        grid=(rows // block,),
        in_specs=[
            pl.BlockSpec((block, width), lambda i: (i, 0)),
            pl.BlockSpec((width, 4 * HD), lambda i: (0, 0)),
            table,
            table,
        ],
        out_specs=[pl.BlockSpec((block, 2 * HD), lambda i: (i, 0))] * 2,
        out_shape=[jax.ShapeDtypeStruct((rows, 2 * HD), BF)] * 2,
        compiler_params=pltpu.CompilerParams(vmem_limit_bytes=32 * 2**20),
    )(x_rows, w_pair, cosine, sine)


def head_rows(rows, head, lane, high):
    if (head == 1) != high:
        rows = pltpu.roll(rows, HD, 1)
    keep = (lane >= HD) if high else (lane < HD)
    return jnp.where(keep, rows, jnp.zeros_like(rows))


def masks(info_ref, qseg_ref, kseg_ref, block, span):
    flip = info_ref[0]
    chunk = pl.program_id(1)
    key_at = lax.broadcasted_iota(jnp.int32, (span, 1), 0)
    query_at = lax.broadcasted_iota(jnp.int32, (1, block), 1)
    swapped = jnp.where(flip == 1, key_at ^ block, key_at)
    key_pos = jnp.where(key_at < 2 * block, swapped, -1)
    query_pos = query_at + block * jnp.where(flip == 1, 1 - chunk, chunk)
    return (key_pos <= query_pos) & (kseg_ref[0] == qseg_ref[0])


def attend_kernel(info_ref, q_ref, k0_ref, k1_ref, k2_ref, qseg_ref, kseg_ref, w_ref,
                  mix_ref, stat_ref, out_ref, kv_all):
    block = q_ref.shape[0]
    span = kv_all.shape[0]
    third = span // 3
    kv_all[:third] = k0_ref[...]
    kv_all[third : 2 * third] = k1_ref[...]
    kv_all[2 * third :] = k2_ref[...]
    pair = kv_all[...]
    allowed = masks(info_ref, qseg_ref, kseg_ref, block, span)
    lane = lax.broadcasted_iota(jnp.int32, (block, 2 * HD), 1)
    query = q_ref[...]
    mixed = []
    for head in range(2):
        scores = dot_nt(pair, head_rows(query, head, lane, False)) * HD ** (-0.5)
        scores = jnp.where(allowed, scores, NEG_BIG)
        top = jnp.max(scores, axis=0, keepdims=True)
        powers = jnp.exp(scores - top)
        total = jnp.sum(powers, axis=0, keepdims=True)
        stat_ref[0, 0, head : head + 1, :] = top + jnp.log(total)
        probs = (powers * (1.0 / total)).astype(BF)
        mixed.append(dot_tn(probs, pair))
    mix = jnp.where(lane < HD, pltpu.roll(mixed[0], HD, 1), mixed[1]).astype(BF)
    mix_ref[...] = mix
    out_ref[...] = dot_nt(mix, w_ref[...]).astype(BF)


def attend(info, query, kv, qseg, kseg, w_out, block):
    rows = query.shape[0]
    seqs = rows // (2 * block)
    width = w_out.shape[0]
    row_spec = pl.BlockSpec((block, 2 * HD), lambda s, i: (2 * s + i, 0))
    kv_spec = pl.BlockSpec((2 * block, 2 * HD), lambda s, i: (s, 0))
    return pl.pallas_call(
        attend_kernel,
        grid=(seqs, 2),
        in_specs=[
            pl.BlockSpec(memory_space=pltpu.SMEM),
            row_spec,
            kv_spec,
            kv_spec,
            kv_spec,
            pl.BlockSpec((1, 1, block), lambda s, i: (2 * s + i, 0, 0)),
            pl.BlockSpec((1, 6 * block, 1), lambda s, i: (s, 0, 0)),
            pl.BlockSpec((width, 2 * HD), lambda s, i: (0, 0)),
        ],
        out_specs=[
            row_spec,
            pl.BlockSpec((1, 1, 2, block), lambda s, i: (s, i, 0, 0)),
            pl.BlockSpec((block, width), lambda s, i: (2 * s + i, 0)),
        ],
        out_shape=[
            jax.ShapeDtypeStruct((rows, 2 * HD), BF),
            jax.ShapeDtypeStruct((seqs, 2, 2, block), F32),
            jax.ShapeDtypeStruct((rows, width), BF),
        ],
        scratch_shapes=[pltpu.VMEM((6 * block, 2 * HD), BF)],
        compiler_params=pltpu.CompilerParams(vmem_limit_bytes=48 * 2**20),
    )(info, query, *kv, qseg, kseg, w_out)


def attend_back_kernel(info_ref, q_ref, k0_ref, k1_ref, k2_ref, qseg_ref, kseg_ref, stat_ref,
                       dy_ref, w_ref, cos_ref, sin_ref,
                       dq_ref, dk0_ref, dk1_ref, dk2_ref, kv_all, sums):
    block = q_ref.shape[0]
    span = kv_all.shape[0]
    third = span // 3
    chunk = pl.program_id(1)

    @pl.when(chunk == 0)
    def _():
        sums[...] = jnp.zeros_like(sums)
        kv_all[:third] = k0_ref[...]
        kv_all[third : 2 * third] = k1_ref[...]
        kv_all[2 * third :] = k2_ref[...]

    pair = kv_all[...]
    allowed = masks(info_ref, qseg_ref, kseg_ref, block, span)
    lane = lax.broadcasted_iota(jnp.int32, (block, 2 * HD), 1)
    query = q_ref[...]
    grad_mix = dot_nn(dy_ref[...], w_ref[...]).astype(BF)
    grad_query = []
    for head in range(2):
        q_low = head_rows(query, head, lane, False)
        g_high = head_rows(grad_mix, head, lane, True)
        scores = dot_nt(pair, q_low) * HD ** (-0.5)
        stat = stat_ref[0, 0, head : head + 1, :]
        probs = jnp.where(allowed, jnp.exp(scores - stat), 0.0)
        grad_probs = dot_nt(pair, g_high)
        delta = jnp.sum(probs * grad_probs, axis=0, keepdims=True)
        grad_scores = (probs * (grad_probs - delta) * HD ** (-0.5)).astype(BF)
        sums[...] += dot_nn(grad_scores, q_low) + dot_nn(probs.astype(BF), g_high)
        grad_query.append(dot_tn(grad_scores, pair))
    grad_q = jnp.where(lane < HD, grad_query[0], pltpu.roll(grad_query[1], HD, 1))
    dq_ref[...] = (grad_q * cos_ref[0] - turn(grad_q * sin_ref[0], lane)).astype(BF)

    @pl.when(chunk == 1)
    def _():
        dk0_ref[...] = sums[:third]
        dk1_ref[...] = sums[third : 2 * third]
        dk2_ref[...] = sums[2 * third :].astype(BF)


def attend_back(info, query, kv, qseg, kseg, stat, grad_rows, w_out, cosine, sine, block):
    rows = query.shape[0]
    seqs = rows // (2 * block)
    width = w_out.shape[0]
    row_spec = pl.BlockSpec((block, 2 * HD), lambda s, i: (2 * s + i, 0))
    kv_spec = pl.BlockSpec((2 * block, 2 * HD), lambda s, i: (s, 0))
    table = pl.BlockSpec((1, block, 2 * HD), lambda s, i: (i, 0, 0))
    return pl.pallas_call(
        attend_back_kernel,
        grid=(seqs, 2),
        in_specs=[
            pl.BlockSpec(memory_space=pltpu.SMEM),
            row_spec,
            kv_spec,
            kv_spec,
            kv_spec,
            pl.BlockSpec((1, 1, block), lambda s, i: (2 * s + i, 0, 0)),
            pl.BlockSpec((1, 6 * block, 1), lambda s, i: (s, 0, 0)),
            pl.BlockSpec((1, 1, 2, block), lambda s, i: (s, i, 0, 0)),
            pl.BlockSpec((block, width), lambda s, i: (2 * s + i, 0)),
            pl.BlockSpec((width, 2 * HD), lambda s, i: (0, 0)),
            table,
            table,
        ],
        out_specs=[row_spec, kv_spec, kv_spec, kv_spec],
        out_shape=[
            jax.ShapeDtypeStruct((rows, 2 * HD), BF),
            jax.ShapeDtypeStruct((rows, 2 * HD), F32),
            jax.ShapeDtypeStruct((rows, 2 * HD), F32),
            jax.ShapeDtypeStruct((rows, 2 * HD), BF),
        ],
        scratch_shapes=[
            pltpu.VMEM((6 * block, 2 * HD), BF),
            pltpu.VMEM((6 * block, 2 * HD), F32),
        ],
        compiler_params=pltpu.CompilerParams(vmem_limit_bytes=56 * 2**20),
    )(info, query, *kv, qseg, kseg, stat, grad_rows, w_out, cosine, sine)


def key_back_kernel(a_ref, b_ref, cos_ref, sin_ref, out_ref):
    grad = a_ref[...] + b_ref[...].astype(F32)
    lane = lax.broadcasted_iota(jnp.int32, grad.shape, 1)
    turned = grad * cos_ref[0] - turn(grad * sin_ref[0], lane)
    out_ref[...] = jnp.where(lane < HD, turned, grad).astype(BF)


def key_back(here, arrived, cosine, sine, block):
    rows = here.shape[0]
    spec = pl.BlockSpec((block, 2 * HD), lambda i: (i, 0))
    table = pl.BlockSpec((1, block, 2 * HD), lambda i: (i % 2, 0, 0))
    return pl.pallas_call(
        key_back_kernel,
        grid=(rows // block,),
        in_specs=[spec, spec, table, table],
        out_specs=spec,
        out_shape=jax.ShapeDtypeStruct((rows, 2 * HD), BF),
    )(here, arrived, cosine, sine)


def shards(
    tokens,
    segments,
    routes,
    gate_weights,
    cotangent,
    owners,
    masters,
    first_moments,
    second_moments,
    norm_gains,
    gain_first,
    gain_second,
):
    z_index = lax.axis_index("z")
    x_index = lax.axis_index("x")
    w_index = lax.axis_index("y") * 2 + lax.axis_index("c")
    slot_count, row_count, hidden = masters.shape
    slot_total = slot_count * 4
    seg_len = tokens.shape[1]
    width = tokens.shape[2]
    matrix_count = owners.shape[0]
    experts = (matrix_count - 6) // 3
    group = experts // 2
    part = hidden // 4
    x_even = x_index == 0

    slot_ids = jnp.arange(slot_total, dtype=jnp.int32)
    hits = owners[None, :] == slot_ids[:, None]
    held = jnp.sum(hits * (jnp.arange(matrix_count, dtype=jnp.int32) + 1)[None, :], axis=1) - 1

    masters_low = masters.astype(BF)
    local_at = owners[:6] - slot_count * w_index
    local_ok = (local_at >= 0) & (local_at < slot_count)
    attn_mats = jnp.where(
        local_ok[:, None, None],
        jnp.take(masters_low, jnp.clip(local_at, 0, slot_count - 1), axis=0),
        jnp.zeros((), BF),
    )

    def by_head(mat, lanes):
        return jnp.transpose(mat.reshape(row_count, -1, lanes), (1, 0, 2))

    q_parts = jnp.concatenate([by_head(attn_mats[0], part), by_head(attn_mats[1], part)], axis=0)
    o_parts = jnp.concatenate([by_head(attn_mats[4], part), by_head(attn_mats[5], part)], axis=0)
    kv_parts = jnp.concatenate([by_head(attn_mats[2], HD), by_head(attn_mats[3], HD)], axis=2)
    attn_send = jnp.stack([q_parts, kv_parts, o_parts], axis=1)
    attn_got = lax.all_to_all(attn_send, PLANE, split_axis=0, concat_axis=0, tiled=True)
    attn_mine = jnp.sum(attn_got.reshape(2, 4, 3, row_count, part).astype(F32), axis=1).astype(BF)
    attn_mine = jnp.transpose(attn_mine, (0, 2, 1, 3)).reshape(2 * row_count, 3 * part)
    attn_w = lax.all_gather(attn_mine, "z", axis=0, tiled=True)
    w_pair = attn_w[:, : 2 * part]
    w_out = attn_w[:, 2 * part :]

    tokens_f = tokens[0].astype(F32)
    scale_one = norm_scale(tokens_f)
    attn_in = (tokens_f * scale_one * norm_gains[0]).astype(BF)
    expert_ids = jnp.arange(experts, dtype=jnp.int32)
    gates = jnp.sum(
        jnp.where(routes[0][:, :, None] == expert_ids[None, None, :], gate_weights[0][:, :, None], 0.0),
        axis=1,
    )
    gates_high = gates.astype(BF)
    gates_low = (gates - gates_high.astype(F32)).astype(BF)
    marks = (segments[0] + 1).astype(BF)[:, None]
    spare = jnp.zeros((seg_len, 128 - 2 * experts - 1), BF)
    packed = jnp.concatenate([attn_in, gates_high, gates_low, marks, spare], axis=1)
    packed_all = plane_gather(packed)
    x_all = packed_all[:, :width]
    gates_all = packed_all[:, width : width + experts].astype(F32) + packed_all[
        :, width + experts : width + 2 * experts
    ].astype(F32)
    my_gates = jnp.where(x_even, gates_all[:, :group], gates_all[:, group:])
    marks_all = packed_all[:, width + 2 * experts].astype(F32).reshape(-1, 128)
    marks_one = shift(marks_all, 1)
    marks_two = shift(marks_one, 1)
    seqs = 4
    qseg = marks_all.reshape(2 * seqs, 1, seg_len)
    kseg = jnp.concatenate(
        [m.reshape(seqs, 2 * seg_len) for m in (marks_all, marks_one, marks_two)], axis=1
    )[:, :, None]
    g_all = plane_gather(cotangent[0])

    bulk_send = jnp.transpose(masters_low.reshape(slot_count, row_count, 4, part), (2, 0, 1, 3))
    bulk_got = lax.all_to_all(bulk_send, WSH, split_axis=0, concat_axis=0, tiled=True).reshape(
        slot_total, row_count, part
    )
    order = np.array([[6 + 3 * (group * g + e) + k for k in range(3) for e in range(group)] for g in range(2)])
    picks = jnp.take(owners, jnp.asarray(order))
    picks_mine = jnp.where(x_even, picks[0], picks[1])
    picks_other = jnp.where(x_even, picks[1], picks[0])

    def pick(which):
        return jnp.transpose(jnp.take(bulk_got, which, axis=0), (1, 0, 2)).reshape(row_count, -1)

    rows_mine = pick(picks_mine)
    rows_got = swap(pick(picks_other), "x")
    pair_rows = jnp.where(
        x_even,
        jnp.concatenate([rows_mine, rows_got], axis=0),
        jnp.concatenate([rows_got, rows_mine], axis=0),
    )
    expert_w = lax.all_gather(pair_rows, "z", axis=0, tiled=True)
    cols = group * part
    w_gate = expert_w[:, :cols]
    w_up = expert_w[:, cols : 2 * cols]
    w_down = expert_w[:, 2 * cols :]

    inverse = THETA ** (-(jnp.arange(HD // 2, dtype=F32) * 2.0 / HD))
    at = jnp.arange(seg_len, dtype=jnp.int32)
    first_pos = z_index * 2 * seg_len + x_index * seg_len + at
    second_pos = z_index * 2 * seg_len + (1 - x_index) * seg_len + at
    positions = jnp.stack([first_pos, second_pos])
    angles = positions.astype(F32)[:, :, None] * inverse[None, None, :]
    cosine = jnp.tile(jnp.cos(angles), (1, 1, 4))
    sine = jnp.tile(jnp.sin(angles), (1, 1, 4))
    info = x_index.reshape(1).astype(jnp.int32)

    query, kv_zero = project(packed_all, w_pair, cosine, sine, seg_len)
    kv_one = shift(kv_zero, 1)
    kv_two = shift(kv_one, 1)
    kv = (kv_zero, kv_one, kv_two)
    attn_mix, stat, out_part = attend(info, query, kv, qseg, kseg, w_out, seg_len)
    resid_one = tokens_f + plane_reduce(out_part)
    scale_two = norm_scale(resid_one)
    expert_in = (resid_one * scale_two * norm_gains[1]).astype(BF)
    e_all = plane_gather(expert_in)

    gate_wide = jnp.broadcast_to(my_gates[:, :, None], (my_gates.shape[0], group, part)).reshape(
        -1, cols
    )
    gate_pre = dot_nn(e_all, w_gate)
    up_pre = dot_nn(e_all, w_up)
    logistic = jax.nn.sigmoid(gate_pre)
    active = gate_pre * logistic
    hidden_low = (active * up_pre * gate_wide).astype(BF)
    grad_hidden = dot_nn(g_all, w_down) * gate_wide
    grad_gate_low = (grad_hidden * up_pre * logistic * (1.0 + gate_pre * (1.0 - logistic))).astype(BF)
    grad_up_low = (grad_hidden * active).astype(BF)
    grad_in_part = (dot_nt(grad_gate_low, w_gate) + dot_nt(grad_up_low, w_up)).astype(BF)
    expert_grads = jnp.concatenate(
        [
            dot_tn(e_all, grad_gate_low).astype(BF),
            dot_tn(e_all, grad_up_low).astype(BF),
            dot_tn(g_all, hidden_low).astype(BF),
        ],
        axis=1,
    )
    expert_sum = lax.psum_scatter(expert_grads, "z", scatter_dimension=0, tiled=True)
    out_moe = dot_nt(hidden_low, w_down).astype(BF)
    grad_expert_in = plane_reduce(grad_in_part)
    resid_two = resid_one + plane_reduce(out_moe)
    output = resid_two.astype(BF)

    cot_rows = cotangent[0].astype(F32)
    norm_grad_two, gain_grad_two = norm_back(resid_one, scale_two, norm_gains[1], grad_expert_in)
    grad_resid = cot_rows + norm_grad_two
    dy_all = plane_gather(grad_resid.astype(BF))
    grad_w_out = dot_tn(dy_all, attn_mix)
    grad_q_low, dkv_zero, dkv_one, dkv_two = attend_back(
        info, query, kv, qseg, kseg, stat, dy_all, w_out, cosine, sine, seg_len
    )
    passed = shift(dkv_two, -1)
    passed = shift((dkv_one + passed.astype(F32)).astype(BF), -1)
    grad_kv_low = key_back(dkv_zero, passed, cosine, sine, seg_len)
    grad_both = jnp.concatenate([grad_q_low, grad_kv_low], axis=1)
    grad_w_pair = dot_tn(x_all, grad_both)
    grad_in_one = plane_reduce(dot_nt(grad_both, w_pair).astype(BF))
    norm_grad_one, gain_grad_one = norm_back(tokens_f, scale_one, norm_gains[0], grad_in_one)
    input_grad = grad_resid + norm_grad_one

    attn_grads = jnp.concatenate([grad_w_pair.astype(BF), grad_w_out.astype(BF)], axis=1)
    attn_sum = lax.psum_scatter(attn_grads, "z", scatter_dimension=0, tiled=True)
    attn_rows = jnp.broadcast_to(
        attn_sum.reshape(2, 1, row_count, 3 * part), (2, 4, row_count, 3 * part)
    ).reshape(8, row_count, 3 * part)
    attn_back = lax.all_to_all(attn_rows, PLANE, split_axis=0, concat_axis=0, tiled=True)
    q_back = jnp.transpose(attn_back[:, :, :part].reshape(2, 4, row_count, part), (0, 2, 1, 3)).reshape(2, row_count, hidden)
    o_back = jnp.transpose(attn_back[:, :, 2 * part :].reshape(2, 4, row_count, part), (0, 2, 1, 3)).reshape(2, row_count, hidden)
    k_back = jnp.transpose(attn_back[:, :, part : part + HD], (1, 0, 2)).reshape(1, row_count, hidden)
    v_back = jnp.transpose(attn_back[:, :, part + HD : 2 * part], (1, 0, 2)).reshape(1, row_count, hidden)
    attn_six = jnp.concatenate([q_back, k_back, v_back, o_back], axis=0)

    keep = lax.dynamic_slice_in_dim(expert_sum, x_index * row_count, row_count, axis=0)
    give = lax.dynamic_slice_in_dim(expert_sum, (1 - x_index) * row_count, row_count, axis=0)
    came = swap(give, "x")
    both_groups = jnp.stack([keep, came]).reshape(2, row_count, 3 * group, part)
    both_groups = jnp.transpose(both_groups, (0, 2, 1, 3)).reshape(6 * group, row_count, part)
    expert_of = (held - 6) // 3
    kind_of = (held - 6) % 3
    side = (expert_of // group) ^ x_index
    place = side * 3 * group + kind_of * group + expert_of % group
    is_expert = held >= 6
    slot_send = jnp.where(
        is_expert[:, None, None],
        jnp.take(both_groups, jnp.clip(place, 0, 6 * group - 1), axis=0),
        jnp.zeros((), BF),
    )
    slot_got = lax.all_to_all(slot_send, WSH, split_axis=0, concat_axis=0, tiled=True)
    expert_slot = jnp.transpose(
        slot_got.reshape(4, slot_count, row_count, part), (1, 2, 0, 3)
    ).reshape(slot_count, row_count, hidden)
    held_mine = lax.dynamic_slice_in_dim(held, w_index * slot_count, slot_count)
    attn_slot = jnp.take(attn_six, jnp.clip(held_mine, 0, 5), axis=0)
    is_attn = (held_mine >= 0) & (held_mine < 6)
    slot_grad = jnp.where(is_attn[:, None, None], attn_slot, expert_slot).astype(F32)
    table = jnp.asarray(np.array([7, 0, 0, 1, 2, 3, 3] + [4, 5, 6] * experts, np.int32))
    rates = jnp.take(jnp.asarray(kind_rates(width, hidden), F32), jnp.take(table, held_mine + 1))
    new_masters, new_first, new_second = adamw(
        masters, first_moments, second_moments, slot_grad, rates[:, None, None], DECAY
    )
    gain_grad = sum_everywhere(jnp.stack([gain_grad_one, gain_grad_two]))
    new_gains, new_gain_first, new_gain_second = adamw(
        norm_gains, gain_first, gain_second, gain_grad, GAIN_RATE, 0.0
    )
    return (
        output[None],
        input_grad[None],
        new_masters,
        new_first,
        new_second,
        new_gains,
        new_gain_first,
        new_gain_second,
    )


def solution(mesh):
    ctx, wsh = mesh.devices.shape
    fine = Mesh(mesh.devices.reshape(ctx // 2, 2, wsh // 2, 2), ("z", "x", "y", "c"))
    rows = P(WSH, ("z", "x"), None)
    marks = P(WSH, ("z", "x"))
    return jax.shard_map(
        shards,
        mesh=fine,
        in_specs=(rows, marks, rows, rows, rows, P(), rows, rows, rows, P(), P(), P()),
        out_specs=(rows, rows, rows, rows, rows, P(), P(), P()),
        check_vma=False,
    )
```

```python
import jax
import jax.numpy as jnp
import numpy as np
from jax import lax
from jax.experimental import pallas as pl
from jax.experimental.pallas import tpu as pltpu
from jax.sharding import Mesh
from jax.sharding import PartitionSpec as P

QH = 16
KVH = 8
HD = 64
STEP = 7

EPS_NORM = 1e-05
THETA = 10000.0
BETA_ONE = 0.5
BETA_TWO = 0.6
ADAM_EPS = 1e-08
DECAY = 0.1
GAIN_RATE = 0.3
NEG_BIG = -1e30
PLANE = ("x", "y", "c")
WSH = ("y", "c")
BF = jnp.bfloat16
F32 = jnp.float32


def swap(value, axis):
    return lax.ppermute(value, axis, [(0, 1), (1, 0)])


def shift(value, by):
    count = lax.axis_size("z")
    pairs = [(i, i + by) for i in range(count) if 0 <= i + by < count]
    return lax.ppermute(value, "z", pairs)


def took(us):
    return pl.CostEstimate(flops=int(us * 1e9), bytes_accessed=2**20, transcendentals=0)


def vmem(mib):
    return pltpu.CompilerParams(vmem_limit_bytes=mib * 2**20)


def whole(shape):
    return pl.BlockSpec(shape, lambda *_: (0,) * len(shape))


def half_specs(block, width, rows, at):
    low = pl.BlockSpec((block, width), lambda *g: (jnp.minimum(at(*g), rows // 2 // block - 1), 0))
    high = pl.BlockSpec((block, width), lambda *g: (jnp.maximum(at(*g) - rows // 2 // block, 0), 0))
    return [low, high]


def after(value, *first):
    return lax.optimization_barrier((value, *first))[0]


def stack_kernel(*refs):
    at = 0
    for ref in refs[:-1]:
        refs[-1][at : at + ref.shape[0]] = ref[...]
        at += ref.shape[0]


def stack(pieces):
    shape = (sum(piece.shape[0] for piece in pieces), pieces[0].shape[1])
    return pl.pallas_call(
        stack_kernel,
        grid=(1,),
        in_specs=[whole(piece.shape) for piece in pieces],
        out_specs=whole(shape),
        out_shape=jax.ShapeDtypeStruct(shape, BF),
        cost_estimate=took(2),
        compiler_params=vmem(32),
    )(*pieces)


def plane_gather(rows, wait=lambda value: value, last=lambda value: value):
    half = rows.shape[0] // 2
    over_x = swap(rows, "x")
    over_y = swap(rows, "y")
    first, second = wait((over_x[:half], over_y[half:]))
    corner_top = swap(first, "y")
    corner_low = swap(second, "x")
    mine = stack([rows, over_x, over_y, corner_top, corner_low])
    return mine, swap(last(mine), "c")


def corner_kernel(kept_ref, got_ref, out_ref):
    out_ref[...] = (kept_ref[...].astype(F32) + got_ref[...].astype(F32)).astype(BF)


def corner_rows(kept, got):
    rows, width = kept.shape
    spec = pl.BlockSpec((rows // 4, width), lambda i: (3, 0))
    return pl.pallas_call(
        corner_kernel,
        grid=(1,),
        in_specs=[spec, spec],
        out_specs=whole((rows // 4, width)),
        out_shape=jax.ShapeDtypeStruct((rows // 4, width), BF),
        cost_estimate=took(2),
        compiler_params=vmem(32),
    )(kept, got)


def edge_kernel(kx_ref, gx_ref, ky_ref, gy_ref, fx_ref, fy_ref, x_ref, y_ref):
    half = fx_ref.shape[0]
    for kept, got, extra, out_ref, at in ((kx_ref, gx_ref, fx_ref, x_ref, 0), (ky_ref, gy_ref, fy_ref, y_ref, 1)):
        total = kept[...].astype(F32) + got[...].astype(F32)
        mine, rest = slice(at * half, (at + 1) * half), slice((1 - at) * half, (2 - at) * half)
        out_ref[mine] = (total[mine] + extra[...].astype(F32)).astype(BF)
        out_ref[rest] = total[rest].astype(BF)


def edge_rows(kept, got, for_x, for_y):
    rows, width = kept.shape
    step = rows // 4
    one, two = (pl.BlockSpec((step, width), lambda i, b=b: (b, 0)) for b in (1, 2))
    half = whole((step // 2, width))
    return pl.pallas_call(
        edge_kernel,
        grid=(1,),
        in_specs=[one, one, two, two, half, half],
        out_specs=[whole((step, width))] * 2,
        out_shape=[jax.ShapeDtypeStruct((step, width), BF)] * 2,
        cost_estimate=took(2),
        compiler_params=vmem(32),
    )(kept, got, kept, got, for_x, for_y)


def plane_reduce(kept, sent, waits=(None, None, None)):
    hold = [wait or (lambda value: value) for wait in waits]
    step = kept.shape[0] // 4
    half = step // 2
    got = swap(hold[0](sent), "c")
    corner = hold[1](corner_rows(kept, got))
    for_x = swap(corner[:half], "y")
    for_y = swap(corner[half:], "x")
    to_x, to_y = hold[2](edge_rows(kept, got, for_x, for_y))
    own = kept[:step].astype(F32) + got[:step].astype(F32)
    return own + swap(to_x, "x").astype(F32) + swap(to_y, "y").astype(F32)


def sum_everywhere(value):
    for axis in ("c", "x", "y"):
        value = value + swap(value, axis)
    count = lax.axis_size("z")
    if count & (count - 1):
        return lax.psum(value, "z")
    stride = 1
    while stride < count:
        value = value + lax.ppermute(value, "z", [(i, i ^ stride) for i in range(count)])
        stride *= 2
    return value


def norm_scale(values):
    return lax.rsqrt(jnp.mean(values * values, axis=-1, keepdims=True) + EPS_NORM)


def norm_back(values, scale_row, gain_row, grad_out):
    weighted = grad_out * gain_row
    grad_in = scale_row * weighted - values * scale_row**3 * jnp.mean(
        values * weighted, axis=-1, keepdims=True
    )
    return grad_in


def kind_rates(width, hidden):
    base_rate = 0.5 * width ** (-0.5)
    return [
        base_rate,
        base_rate,
        base_rate,
        2.0 * (2 * hidden) ** (-0.5),
        base_rate,
        base_rate,
        3.0 * hidden ** (-0.5),
        base_rate,
    ]


def adamw(weight, first, second, grad, rate, decay):
    first_new = BETA_ONE * first + (1.0 - BETA_ONE) * grad
    second_new = BETA_TWO * second + (1.0 - BETA_TWO) * grad * grad
    first_hat = first_new / (1.0 - BETA_ONE**STEP)
    second_hat = second_new / (1.0 - BETA_TWO**STEP)
    weight_new = weight - rate * (first_hat / (jnp.sqrt(second_hat) + ADAM_EPS) + decay * weight)
    return (weight_new, first_new, second_new)


def dot_nn(left, right):
    return lax.dot_general(left, right, (((1,), (0,)), ((), ())), preferred_element_type=F32)


def dot_nt(left, right):
    return lax.dot_general(left, right, (((1,), (1,)), ((), ())), preferred_element_type=F32)


def dot_tn(left, right):
    return lax.dot_general(left, right, (((0,), (0,)), ((), ())), preferred_element_type=F32)


def turn(value, lane):
    low = (lane % HD) < (HD // 2)
    return jnp.where(
        low, -pltpu.roll(value, 2 * HD - HD // 2, 1), pltpu.roll(value, HD // 2, 1)
    )

def choose(early, low_ref, high_ref):
    return jnp.where(early, low_ref[...], high_ref[...])


def attn_send_kernel(at_ref, ok_ref, *refs):
    mats, out_ref = refs[:6], refs[6]

    def read(m):
        return jnp.where(ok_ref[m] == 1, mats[m][0], 0.0).astype(BF)

    part = out_ref.shape[3]
    for side in range(2):
        for kind, m in ((0, side), (2, 4 + side)):
            mat = read(m)
            for j in range(4):
                out_ref[4 * side + j, kind] = mat[:, j * part : (j + 1) * part]
    keys, values = read(2), read(3)
    for h in range(8):
        both = (keys[:, h * HD : (h + 1) * HD], values[:, h * HD : (h + 1) * HD])
        out_ref[h, 1] = jnp.concatenate(both, axis=1)


def attn_send(masters, at, ok):
    _, rows, hidden = masters.shape
    part = hidden // 4
    specs = [pl.BlockSpec((1, rows, hidden), lambda i, at, ok, m=m: (at[m], 0, 0)) for m in range(6)]
    return pl.pallas_call(
        attn_send_kernel,
        grid_spec=pltpu.PrefetchScalarGridSpec(
            num_scalar_prefetch=2,
            grid=(1,),
            in_specs=specs,
            out_specs=pl.BlockSpec((8, 3, rows, part), lambda i, at, ok: (0, 0, 0, 0)),
        ),
        out_shape=jax.ShapeDtypeStruct((8, 3, rows, part), BF),
        cost_estimate=took(3),
        compiler_params=vmem(62),
    )(at, ok, *([masters] * 6))


def bulk_send_kernel(in_ref, *outs):
    part = outs[0].shape[3]
    rows = outs[0].shape[2]
    for h, out_ref in enumerate(outs):
        for j in range(4):
            piece = in_ref[:, h * rows : (h + 1) * rows, j * part : (j + 1) * part]
            out_ref[j] = piece.astype(BF)


def bulk_send(masters, halves):
    slots, rows, hidden = masters.shape
    step, part, piece = 5 if slots % 5 == 0 else 1, hidden // 4, rows // halves
    return pl.pallas_call(
        bulk_send_kernel,
        grid=(slots // step,),
        in_specs=[pl.BlockSpec((step, rows, hidden), lambda i: (i, 0, 0))],
        out_specs=[pl.BlockSpec((4, step, piece, part), lambda i: (0, i, 0, 0))] * halves,
        out_shape=[jax.ShapeDtypeStruct((4, slots, piece, part), BF)] * halves,
        cost_estimate=took(4),
        compiler_params=vmem(62),
    )(masters)


def pick_kernel(mine_ref, other_ref, in_ref, keep_ref, give_ref):
    part = in_ref.shape[2]
    for k in range(keep_ref.shape[1] // part):
        keep_ref[:, k * part : (k + 1) * part] = in_ref[mine_ref[k]]
        give_ref[:, k * part : (k + 1) * part] = in_ref[other_ref[k]]


def pick(mine, other, slots):
    total, rows, part = slots.shape
    count = mine.shape[0]
    wide = (rows, count * part)
    return pl.pallas_call(
        pick_kernel,
        grid_spec=pltpu.PrefetchScalarGridSpec(
            num_scalar_prefetch=2,
            grid=(1,),
            in_specs=[pl.BlockSpec((total, rows, part), lambda i, a, b: (0, 0, 0))],
            out_specs=[pl.BlockSpec(wide, lambda i, a, b: (0, 0))] * 2,
        ),
        out_shape=[jax.ShapeDtypeStruct(wide, BF)] * 2,
        cost_estimate=took(3),
        compiler_params=vmem(32),
    )(mine, other, slots)


def join_kernel(info_ref, *refs):
    out_ref = refs[-1]
    rows = refs[0].shape[0]
    half = out_ref.shape[0] // 2
    first = info_ref[0] == 0
    for h in range(len(refs) // 2):
        keep, got = refs[2 * h][...], refs[2 * h + 1][...]
        out_ref[h * rows : (h + 1) * rows] = jnp.where(first, keep, got)
        out_ref[half + h * rows : half + (h + 1) * rows] = jnp.where(first, got, keep)


def join(info, pieces):
    rows, wide = pieces[0].shape
    total = rows * len(pieces)
    return pl.pallas_call(
        join_kernel,
        grid=(1,),
        in_specs=[pl.BlockSpec(memory_space=pltpu.SMEM)] + [whole((rows, wide))] * len(pieces),
        out_specs=whole((total, wide)),
        out_shape=jax.ShapeDtypeStruct((total, wide), BF),
        cost_estimate=took(2),
        compiler_params=vmem(32),
    )(info, *pieces)


def pack_kernel(place_ref, side_ref, info_ref, total_ref, got_ref, out_ref):
    part = out_ref.shape[2]
    rows = out_ref.shape[1]
    mine = pl.ds(pl.multiple_of(info_ref[0] * rows, rows), rows)

    def one(s, carry):
        start = pl.multiple_of(place_ref[s] * part, part)

        @pl.when(side_ref[s] == 0)
        def _():
            out_ref[s] = total_ref[mine, pl.ds(start, part)]

        @pl.when(side_ref[s] == 1)
        def _():
            out_ref[s] = got_ref[:, pl.ds(start, part)]

        @pl.when(side_ref[s] == 2)
        def _():
            out_ref[s] = jnp.zeros((rows, part), BF)

        return carry

    lax.fori_loop(0, out_ref.shape[0], one, 0)


def pack(place, side, info, summed, got, part):
    rows, wide = got.shape
    total = place.shape[0]
    return pl.pallas_call(
        pack_kernel,
        grid_spec=pltpu.PrefetchScalarGridSpec(
            num_scalar_prefetch=3,
            grid=(1,),
            in_specs=[
                pl.BlockSpec((2 * rows, wide), lambda i, a, b, c: (0, 0)),
                pl.BlockSpec((rows, wide), lambda i, a, b, c: (0, 0)),
            ],
            out_specs=pl.BlockSpec((total, rows, part), lambda i, a, b, c: (0, 0, 0)),
        ),
        out_shape=jax.ShapeDtypeStruct((total, rows, part), BF),
        cost_estimate=took(3),
        compiler_params=vmem(32),
    )(place, side, info, summed, got)


def update_kernel(halves, held_ref, rate_ref, attn_ref, *refs):
    grads, (w_ref, m_ref, v_ref, w_out, m_out, v_out) = refs[:halves], refs[halves:]
    part = grads[0].shape[3]
    rows = grads[0].shape[2]
    everything = slice(0, halves * rows)

    def one(s, carry):
        slot = pl.program_id(0) * w_ref.shape[0] + s
        held = held_ref[slot]
        rate = rate_ref[slot]

        def write(at, lanes, grad):
            new_w, new_m, new_v = adamw(
                w_ref[s, at, lanes], m_ref[s, at, lanes], v_ref[s, at, lanes], grad, rate, DECAY
            )
            w_out[s, at, lanes] = new_w
            m_out[s, at, lanes] = new_m
            v_out[s, at, lanes] = new_v

        @pl.when((held < 0) | (held >= 6))
        def _():
            for h in range(halves):
                for j in range(4):
                    at, lanes = slice(h * rows, (h + 1) * rows), slice(j * part, (j + 1) * part)
                    write(at, lanes, grads[h][j, s].astype(F32))

        for m, side, kind in ((0, 0, 0), (1, 1, 0), (4, 0, 2), (5, 1, 2)):

            @pl.when(held == m)
            def _():
                for j in range(4):
                    grad = attn_ref[4 * side + j, :, kind * part : (kind + 1) * part]
                    write(everything, slice(j * part, (j + 1) * part), grad.astype(F32))

        for m, start in ((2, part), (3, part + HD)):

            @pl.when(held == m)
            def _():
                for j in range(4):
                    pieces = [attn_ref[2 * j + i, :, start : start + HD] for i in range(2)]
                    grad = jnp.concatenate(pieces, axis=1)
                    write(everything, slice(j * part, (j + 1) * part), grad.astype(F32))

        return carry

    lax.fori_loop(0, w_ref.shape[0], one, 0)


def update(held, rates, attn_back, grads, masters, first, second):
    slots, rows, hidden = masters.shape
    halves = len(grads)
    step = 4 if slots % 4 == 0 else 1
    smem = pl.BlockSpec(memory_space=pltpu.SMEM)
    spec = pl.BlockSpec((step, rows, hidden), lambda i: (i, 0, 0))
    grad_spec = pl.BlockSpec((4, step, rows // halves, hidden // 4), lambda i: (0, i, 0, 0))
    return pl.pallas_call(
        lambda *refs: update_kernel(halves, *refs),
        grid=(slots // step,),
        in_specs=[smem, smem, whole(attn_back.shape)] + [grad_spec] * halves + [spec] * 3,
        out_specs=[spec] * 3,
        out_shape=[jax.ShapeDtypeStruct(masters.shape, F32)] * 3,
        cost_estimate=took(12),
        compiler_params=vmem(62),
    )(held, rates, attn_back, *grads, masters, first, second)


def project_kernel(low_ref, high_ref, w_ref, cos_ref, sin_ref, q_ref, kv_ref):
    early = pl.program_id(0) < pl.num_programs(0) // 2
    both = dot_nn(choose(early, low_ref, high_ref), w_ref[...])
    cosine = cos_ref[0]
    sine = sin_ref[0]
    lane = lax.broadcasted_iota(jnp.int32, cosine.shape, 1)
    query = both[:, : 2 * HD]
    pair = both[:, 2 * HD :]
    q_ref[...] = (query * cosine + turn(query, lane) * sine).astype(BF)
    turned = pair * cosine + turn(pair, lane) * sine
    kv_ref[...] = jnp.where(lane < HD, turned, pair).astype(BF)


def project(x_low, x_high, w_pair, cosine, sine, block):
    rows = 2 * x_low.shape[0]
    width = w_pair.shape[0]
    table = pl.BlockSpec((1, block, 2 * HD), lambda i: (i % 2, 0, 0))
    return pl.pallas_call(
        project_kernel,
        grid=(rows // block,),
        in_specs=[
            *half_specs(block, width, rows, lambda i: i),
            whole((width, 4 * HD)),
            table,
            table,
        ],
        out_specs=[pl.BlockSpec((block, 2 * HD), lambda i: (i, 0))] * 2,
        out_shape=[jax.ShapeDtypeStruct((rows, 2 * HD), BF)] * 2,
        cost_estimate=took(6),
        compiler_params=vmem(32),
    )(x_low, x_high, w_pair, cosine, sine)


def head_rows(rows, head, lane, high):
    if (head == 1) != high:
        rows = pltpu.roll(rows, HD, 1)
    keep = (lane >= HD) if high else (lane < HD)
    return jnp.where(keep, rows, jnp.zeros_like(rows))


def masks(info_ref, qseg_ref, kseg, block, span):
    flip = info_ref[0]
    chunk = pl.program_id(1)
    key_at = lax.broadcasted_iota(jnp.int32, (span, 1), 0)
    query_at = lax.broadcasted_iota(jnp.int32, (1, block), 1)
    swapped = jnp.where(flip == 1, key_at ^ block, key_at)
    key_pos = jnp.where(key_at < 2 * block, swapped, -1)
    query_pos = query_at + block * jnp.where(flip == 1, 1 - chunk, chunk)
    return (key_pos <= query_pos) & (kseg == qseg_ref[0])


def load_pairs(refs, tails, kv_all, kv_turned, marks, kseg):
    third = kv_all.shape[0] // 3
    for i, (ref, tail) in enumerate(zip(refs, tails)):
        kv_all[i * third : (i + 1) * third] = ref[...]
        marks[i] = tail[...].astype(F32).reshape(marks.shape[1:])
        columns = marks[i, pl.program_id(0)].T
        for j in range(third // 128):
            at = i * third + j * 128
            kseg[at : at + 128] = columns[:, j : j + 1]
    kv_turned[...] = kv_all[...].T


def attend_kernel(info_ref, q_ref, k0_ref, k1_ref, k2_ref, t0_ref, t1_ref, t2_ref, qseg_ref,
                  w_ref, mix_ref, stat_ref, low_ref, high_ref, kv_all, kv_turned, marks, kseg):
    block = q_ref.shape[0]
    span = kv_all.shape[0]

    @pl.when(pl.program_id(1) == 0)
    def _():
        load_pairs((k0_ref, k1_ref, k2_ref), (t0_ref, t1_ref, t2_ref), kv_all, kv_turned, marks, kseg)

    allowed = masks(info_ref, qseg_ref, kseg[...], block, span)
    lane = lax.broadcasted_iota(jnp.int32, (block, 2 * HD), 1)
    query = q_ref[...] * jnp.asarray(HD**-0.5, BF)
    mixed = []
    for head in range(2):
        scores = dot_nt(kv_all[...], head_rows(query, head, lane, False))
        scores = jnp.where(allowed, scores, NEG_BIG)
        top = jnp.max(scores, axis=0, keepdims=True)
        powers = jnp.exp(scores - top)
        total = jnp.sum(powers, axis=0, keepdims=True)
        stat_ref[0, 0, head : head + 1, :] = top + jnp.log(total)
        probs = (powers * (1.0 / total)).astype(BF)
        mixed.append(dot_nn(kv_turned[...], probs)[HD:])
    mix = jnp.concatenate(mixed, axis=0).T.astype(BF)
    mix_ref[...] = mix
    out = dot_nt(mix, w_ref[...]).astype(BF)
    early = pl.program_id(0) < pl.num_programs(0) // 2

    @pl.when(early)
    def _():
        low_ref[...] = out

    @pl.when(jnp.logical_not(early))
    def _():
        high_ref[...] = out


def attend(info, query, kv, qseg, w_out, block):
    rows = query.shape[0]
    seqs = rows // (2 * block)
    width = w_out.shape[0]
    row_spec = pl.BlockSpec((block, 2 * HD), lambda s, i: (2 * s + i, 0))
    kv_spec = pl.BlockSpec((2 * block, 2 * HD), lambda s, i: (s, 0))
    tail_spec = pl.BlockSpec((8 * seqs, 2 * HD), lambda s, i: (rows // (8 * seqs), 0))
    return pl.pallas_call(
        attend_kernel,
        grid=(seqs, 2),
        in_specs=[
            pl.BlockSpec(memory_space=pltpu.SMEM),
            row_spec,
            kv_spec,
            kv_spec,
            kv_spec,
            tail_spec,
            tail_spec,
            tail_spec,
            pl.BlockSpec((1, 1, block), lambda s, i: (2 * s + i, 0, 0)),
            whole((width, 2 * HD)),
        ],
        out_specs=[
            row_spec,
            pl.BlockSpec((1, 1, 2, block), lambda s, i: (s, i, 0, 0)),
            *half_specs(block, width, rows, lambda s, i: 2 * s + i),
        ],
        out_shape=[
            jax.ShapeDtypeStruct((rows, 2 * HD), BF),
            jax.ShapeDtypeStruct((seqs, 2, 2, block), F32),
            *[jax.ShapeDtypeStruct((rows // 2, width), BF)] * 2,
        ],
        scratch_shapes=[
            pltpu.VMEM((6 * block, 2 * HD), BF),
            pltpu.VMEM((2 * HD, 6 * block), BF),
            pltpu.VMEM((3, seqs, 8, 128), F32),
            pltpu.VMEM((6 * block, 1), F32),
        ],
        cost_estimate=took(24),
        compiler_params=vmem(48),
    )(info, query, *kv, *kv, qseg, w_out)


def attend_back_kernel(info_ref, q_ref, k0_ref, k1_ref, k2_ref, t0_ref, t1_ref, t2_ref, qseg_ref,
                       stat_ref, dy_low, dy_high, mix_ref, w_ref, cos_ref, sin_ref,
                       dq_ref, dk0_ref, dk1_ref, dk2_ref, dw_ref,
                       kv_all, kv_turned, marks, kseg, sums, dw_sum):
    block = q_ref.shape[0]
    span = kv_all.shape[0]
    third = span // 3
    seq = pl.program_id(0)
    chunk = pl.program_id(1)

    @pl.when((chunk == 0) & (seq == 0))
    def _():
        dw_sum[...] = jnp.zeros_like(dw_sum)

    @pl.when(chunk == 0)
    def _():
        sums[...] = jnp.zeros_like(sums)
        load_pairs((k0_ref, k1_ref, k2_ref), (t0_ref, t1_ref, t2_ref), kv_all, kv_turned, marks, kseg)

    allowed = masks(info_ref, qseg_ref, kseg[...], block, span)
    lane = lax.broadcasted_iota(jnp.int32, (block, 2 * HD), 1)
    query = q_ref[...] * jnp.asarray(HD**-0.5, BF)
    grad_rows = choose(seq < pl.num_programs(0) // 2, dy_low, dy_high)
    dw_sum[...] += dot_tn(mix_ref[...], grad_rows)
    grad_mix = dot_nn(grad_rows, w_ref[...]).astype(BF)
    grad_query = []
    for head in range(2):
        q_low = head_rows(query, head, lane, False)
        g_high = head_rows(grad_mix, head, lane, True)
        scores = dot_nt(kv_all[...], q_low)
        stat = stat_ref[0, 0, head : head + 1, :]
        probs = jnp.where(allowed, jnp.exp(scores - stat), 0.0)
        grad_probs = dot_nt(kv_all[...], g_high)
        delta = jnp.sum(probs * grad_probs, axis=0, keepdims=True)
        grad_scores = (probs * (grad_probs - delta)).astype(BF)
        sums[...] += dot_nn(grad_scores, q_low) + dot_nn(probs.astype(BF), g_high)
        grad_query.append(dot_nn(kv_turned[...], grad_scores)[:HD])
    grad_q = jnp.concatenate(grad_query, axis=0).T * HD**-0.5
    dq_ref[...] = (grad_q * cos_ref[0] - turn(grad_q * sin_ref[0], lane)).astype(BF)

    @pl.when(chunk == 1)
    def _():
        dk0_ref[...] = sums[:third]
        dk1_ref[...] = sums[third : 2 * third]
        dk2_ref[...] = sums[2 * third :].astype(BF)

    @pl.when((chunk == 1) & (seq == pl.num_programs(0) - 1))
    def _():
        dw_ref[...] = dw_sum[...].T.astype(BF)


def attend_back(info, query, kv, qseg, stat, grad_rows, mix, w_out, cosine, sine, block):
    rows = query.shape[0]
    seqs = rows // (2 * block)
    width = w_out.shape[0]
    row_spec = pl.BlockSpec((block, 2 * HD), lambda s, i: (2 * s + i, 0))
    kv_spec = pl.BlockSpec((2 * block, 2 * HD), lambda s, i: (s, 0))
    tail_spec = pl.BlockSpec((8 * seqs, 2 * HD), lambda s, i: (rows // (8 * seqs), 0))
    table = pl.BlockSpec((1, block, 2 * HD), lambda s, i: (i, 0, 0))
    return pl.pallas_call(
        attend_back_kernel,
        grid=(seqs, 2),
        in_specs=[
            pl.BlockSpec(memory_space=pltpu.SMEM),
            row_spec,
            kv_spec,
            kv_spec,
            kv_spec,
            tail_spec,
            tail_spec,
            tail_spec,
            pl.BlockSpec((1, 1, block), lambda s, i: (2 * s + i, 0, 0)),
            pl.BlockSpec((1, 1, 2, block), lambda s, i: (s, i, 0, 0)),
            *half_specs(block, width, rows, lambda s, i: 2 * s + i),
            row_spec,
            whole((width, 2 * HD)),
            table,
            table,
        ],
        out_specs=[row_spec, kv_spec, kv_spec, kv_spec, whole((width, 2 * HD))],
        out_shape=[
            jax.ShapeDtypeStruct((rows, 2 * HD), BF),
            jax.ShapeDtypeStruct((rows, 2 * HD), F32),
            jax.ShapeDtypeStruct((rows, 2 * HD), F32),
            jax.ShapeDtypeStruct((rows, 2 * HD), BF),
            jax.ShapeDtypeStruct((width, 2 * HD), BF),
        ],
        scratch_shapes=[
            pltpu.VMEM((6 * block, 2 * HD), BF),
            pltpu.VMEM((2 * HD, 6 * block), BF),
            pltpu.VMEM((3, seqs, 8, 128), F32),
            pltpu.VMEM((6 * block, 1), F32),
            pltpu.VMEM((6 * block, 2 * HD), F32),
            pltpu.VMEM((2 * HD, width), F32),
        ],
        cost_estimate=took(28),
        compiler_params=vmem(56),
    )(info, query, *kv, *kv, qseg, stat, *grad_rows, mix, w_out, cosine, sine)


def project_back_kernel(dq_ref, a_ref, b_ref, x_low, x_high, w_ref, cos_ref, sin_ref, dout_ref,
                        low_ref, high_ref, dw_ref, gain_ref, dw_sum):
    step = pl.program_id(0)

    @pl.when(step == 0)
    def _():
        dw_sum[...] = jnp.zeros_like(dw_sum)
        gain_ref[...] = jnp.zeros_like(gain_ref)

    grad = a_ref[...] + b_ref[...].astype(F32)
    lane = lax.broadcasted_iota(jnp.int32, grad.shape, 1)
    turned = grad * cos_ref[0] - turn(grad * sin_ref[0], lane)
    pair = jnp.where(lane < HD, turned, grad).astype(BF)
    both = jnp.concatenate([dq_ref[...], pair], axis=1)
    grad_in = dot_nt(both, w_ref[...])
    early = step < pl.num_programs(0) // 2

    @pl.when(early)
    def _():
        low_ref[...] = grad_in.astype(BF)

    @pl.when(jnp.logical_not(early))
    def _():
        high_ref[...] = grad_in.astype(BF)

    x_rows = choose(early, x_low, x_high)
    dw_sum[...] += dot_tn(both, x_rows)
    weighted = grad_in * x_rows.astype(F32)
    gain_ref[...] += jnp.sum(weighted.reshape(-1, 8, weighted.shape[1]), axis=0)

    @pl.when(step == pl.num_programs(0) - 1)
    def _():
        dw_ref[:, : 4 * HD] = dw_sum[...].T.astype(BF)
        dw_ref[:, 4 * HD :] = dout_ref[...]


def project_back(grad_q, here, arrived, x_rows, w_pair, cosine, sine, grad_out, block):
    rows = here.shape[0]
    width, cols = w_pair.shape
    spec = pl.BlockSpec((block, 2 * HD), lambda i: (i, 0))
    table = pl.BlockSpec((1, block, 2 * HD), lambda i: (i % 2, 0, 0))
    return pl.pallas_call(
        project_back_kernel,
        grid=(rows // block,),
        in_specs=[
            *[spec] * 3,
            *half_specs(block, width, rows, lambda i: i),
            whole((width, cols)),
            table,
            table,
            whole(grad_out.shape),
        ],
        out_specs=[
            *half_specs(block, width, rows, lambda i: i),
            whole((width, 6 * HD)),
            whole((8, width)),
        ],
        out_shape=[
            *[jax.ShapeDtypeStruct((rows // 2, width), BF)] * 2,
            jax.ShapeDtypeStruct((width, 6 * HD), BF),
            jax.ShapeDtypeStruct((8, width), F32),
        ],
        scratch_shapes=[pltpu.VMEM((cols, width), F32)],
        cost_estimate=took(7),
        compiler_params=vmem(32),
    )(grad_q, here, arrived, *x_rows, w_pair, cosine, sine, grad_out)


def expert_kernel(part, e_low, e_high, g_low, g_high, gate_ref, w_ref,
                  act_ref, low_ref, high_ref, et_ref, gt_ref, e_ref, g_ref):
    rows = e_ref.shape[0]
    early = pl.program_id(0) < pl.num_programs(0) // 2
    e_ref[...] = choose(early, e_low, e_high)
    g_ref[...] = choose(early, g_low, g_high)
    cols = w_ref.shape[1] // 3
    step = 2 * part
    lane = lax.broadcasted_iota(jnp.int32, (rows, step), 1)
    for j in range(cols // step):
        at = j * step
        gate = jnp.where(lane < part, gate_ref[:, 2 * j : 2 * j + 1], gate_ref[:, 2 * j + 1 : 2 * j + 2])
        pre = dot_nn(e_ref[...], w_ref[:, at : at + step])
        up = dot_nn(e_ref[...], w_ref[:, cols + at : cols + at + step])
        grad = dot_nn(g_ref[...], w_ref[:, 2 * cols + at : 2 * cols + at + step]) * gate
        logistic = 1.0 / (1.0 + jnp.exp(-pre))
        active = pre * logistic
        act_ref[:, at : at + step] = (
            grad * up * logistic * (1.0 + pre * (1.0 - logistic))
        ).astype(BF)
        act_ref[:, cols + at : cols + at + step] = (grad * active).astype(BF)
        act_ref[:, 2 * cols + at : 2 * cols + at + step] = (active * up * gate).astype(BF)
    et_ref[...] = e_ref[...].T
    gt_ref[...] = g_ref[...].T
    dx = dot_nt(act_ref[:, : 2 * cols], w_ref[:, : 2 * cols]).astype(BF)

    @pl.when(early)
    def _():
        low_ref[...] = dx

    @pl.when(jnp.logical_not(early))
    def _():
        high_ref[...] = dx


def expert_rows(e_rows, g_rows, gates, weights, part, block):
    rows, width = 2 * e_rows[0].shape[0], e_rows[0].shape[1]
    wide = weights.shape[1]
    return pl.pallas_call(
        lambda *refs: expert_kernel(part, *refs),
        grid=(rows // block,),
        in_specs=[
            *half_specs(block, width, rows, lambda i: i) * 2,
            pl.BlockSpec((block, gates.shape[1]), lambda i: (i, 0)),
            whole(weights.shape),
        ],
        out_specs=[
            pl.BlockSpec((block, wide), lambda i: (i, 0)),
            *half_specs(block, width, rows, lambda i: i),
            *[pl.BlockSpec((width, block), lambda i: (0, i))] * 2,
        ],
        out_shape=[
            jax.ShapeDtypeStruct((rows, wide), BF),
            *[jax.ShapeDtypeStruct((rows // 2, width), BF)] * 2,
            *[jax.ShapeDtypeStruct((width, rows), BF)] * 2,
        ],
        scratch_shapes=[pltpu.VMEM((block, width), BF)] * 2,
        cost_estimate=took(28),
        compiler_params=vmem(56),
    )(*e_rows, *g_rows, gates, weights)


def expert_grad_kernel(e_ref, g_ref, act_ref, out_ref):
    step = pl.program_id(0)
    count = 2 * (pl.num_programs(0) // 3)

    @pl.when(step < count)
    def _():
        out_ref[...] = dot_nn(e_ref[...].reshape(-1, act_ref.shape[0]), act_ref[...]).astype(BF)

    @pl.when(step >= count)
    def _():
        out_ref[...] = dot_nn(g_ref[...].reshape(-1, act_ref.shape[0]), act_ref[...]).astype(BF)


def expert_grads(e_turned, g_turned, act, half, halves, piece, step):
    width, rows = e_turned.shape
    wide = act.shape[1]
    count = width // halves // piece
    spec = pl.BlockSpec((count, 1, piece, rows), lambda i: (0, half, 0, 0))
    split = (count, halves, piece, rows)
    return pl.pallas_call(
        expert_grad_kernel,
        grid=(wide // step,),
        in_specs=[spec, spec, pl.BlockSpec((rows, step), lambda i: (0, i))],
        out_specs=pl.BlockSpec((count * piece, step), lambda i: (0, i)),
        out_shape=jax.ShapeDtypeStruct((count * piece, wide), BF),
        cost_estimate=took(9),
        compiler_params=vmem(48),
    )(e_turned.reshape(split), g_turned.reshape(split), act)


def expert_out_kernel(act_ref, w_ref, low_ref, high_ref):
    out = dot_nt(act_ref[...], w_ref[...]).astype(BF)
    early = pl.program_id(0) < pl.num_programs(0) // 2

    @pl.when(early)
    def _():
        low_ref[...] = out

    @pl.when(jnp.logical_not(early))
    def _():
        high_ref[...] = out


def expert_out(act, weights, block):
    rows, wide = act.shape
    width = weights.shape[0]
    cols = wide // 3
    return pl.pallas_call(
        expert_out_kernel,
        grid=(rows // block,),
        in_specs=[
            pl.BlockSpec((block, cols), lambda i: (i, 2)),
            pl.BlockSpec((width, cols), lambda i: (0, 2)),
        ],
        out_specs=half_specs(block, width, rows, lambda i: i),
        out_shape=[jax.ShapeDtypeStruct((rows // 2, width), BF)] * 2,
        cost_estimate=took(7),
        compiler_params=vmem(48),
    )(act, weights)


def shards(
    tokens,
    segments,
    routes,
    gate_weights,
    cotangent,
    owners,
    masters,
    first_moments,
    second_moments,
    norm_gains,
    gain_first,
    gain_second,
):
    z_index = lax.axis_index("z")
    x_index = lax.axis_index("x")
    w_index = lax.axis_index("y") * 2 + lax.axis_index("c")
    slot_count, row_count, hidden = masters.shape
    slot_total = slot_count * 4
    seg_len = tokens.shape[1]
    width = tokens.shape[2]
    ctx_count = width // row_count
    matrix_count = owners.shape[0]
    experts = (matrix_count - 6) // 3
    group = experts // 2
    part = hidden // 4
    halves = 2 if row_count % 32 == 0 else 1
    piece = row_count // halves
    x_even = x_index == 0
    info = x_index.reshape(1).astype(jnp.int32)

    slot_ids = jnp.arange(slot_total, dtype=jnp.int32)
    hits = owners[None, :] == slot_ids[:, None]
    held = jnp.sum(hits * (jnp.arange(matrix_count, dtype=jnp.int32) + 1)[None, :], axis=1) - 1

    local_at = owners[:6] - slot_count * w_index
    local_ok = (local_at >= 0) & (local_at < slot_count)
    attn_sent = attn_send(masters, jnp.clip(local_at, 0, slot_count - 1), local_ok.astype(jnp.int32))
    bulk = bulk_send(masters, halves)
    attn_got = lax.all_to_all(attn_sent, PLANE, split_axis=0, concat_axis=0, tiled=True)
    attn_got = after(attn_got, *bulk)
    attn_mine = jnp.sum(attn_got.reshape(2, 4, 3, row_count, part).astype(F32), axis=1).astype(BF)
    attn_mine = jnp.transpose(attn_mine, (0, 2, 1, 3)).reshape(2 * row_count, 3 * part)
    attn_w = lax.all_gather(attn_mine, "z", axis=0, tiled=True)
    w_pair = attn_w[:, : 2 * part]
    w_out = attn_w[:, 2 * part :]

    order = np.array([[6 + 3 * (group * g + e) + k for k in range(3) for e in range(group)] for g in range(2)])
    picks = jnp.take(owners, jnp.asarray(order))
    picks_mine = jnp.where(x_even, picks[0], picks[1])
    picks_other = jnp.where(x_even, picks[1], picks[0])
    pieces = []
    arrived = []
    got = attn_got
    for send in bulk:
        got = lax.all_to_all(after(send, got), WSH, split_axis=0, concat_axis=0, tiled=True)
        arrived.append(got)
        keep, give = pick(picks_mine, picks_other, got.reshape(slot_total, piece, part))
        pieces += [keep, swap(give, "x")]
    joined = join(info, pieces)
    expert_w = lax.all_gather(after(joined, attn_w), "z", axis=0, tiled=True)

    gains = norm_gains
    tokens_f = tokens[0].astype(F32)
    cot_low = cotangent[0]
    scale_one = norm_scale(tokens_f)
    attn_in = (tokens_f * scale_one * gains[0]).astype(BF)
    expert_ids = jnp.arange(experts, dtype=jnp.int32)
    gates = jnp.sum(
        jnp.where(routes[0][:, :, None] == expert_ids[None, None, :], gate_weights[0][:, :, None], 0.0),
        axis=1,
    )
    gates_high = gates.astype(BF)
    gates_low = (gates - gates_high.astype(F32)).astype(BF)
    marks = (segments[0] + 1).astype(BF)[:, None]
    spare = jnp.zeros((seg_len, 128 - 2 * experts - 1), BF)
    packed = jnp.concatenate([attn_in, gates_high, gates_low, marks, spare], axis=1)
    packed_all = plane_gather(
        after(packed, attn_got), lambda sent: after(sent, attn_w, arrived[0])
    )
    extras = jnp.concatenate([rows[:, width:] for rows in packed_all], axis=0)
    gates_all = extras[:, :experts].astype(F32) + extras[:, experts : 2 * experts].astype(F32)
    my_gates = jnp.where(x_even, gates_all[:, :group], gates_all[:, group:])
    seqs = 4
    rows_all = seqs * 2 * seg_len
    marks_all = extras[:, 2 * experts].reshape(seqs, -1, 128)
    marks_tail = jnp.pad(marks_all, ((0, 0), (0, 8 - marks_all.shape[1]), (0, 0))).reshape(-1, 128)

    inverse = THETA ** (-(jnp.arange(HD // 2, dtype=F32) * 2.0 / HD))
    at = jnp.arange(seg_len, dtype=jnp.int32)
    first_pos = z_index * 2 * seg_len + x_index * seg_len + at
    second_pos = z_index * 2 * seg_len + (1 - x_index) * seg_len + at
    positions = jnp.stack([first_pos, second_pos])
    angles = positions.astype(F32)[:, :, None] * inverse[None, None, :]
    cosine = jnp.tile(jnp.cos(angles), (1, 1, 4))
    sine = jnp.tile(jnp.sin(angles), (1, 1, 4))

    query, kv_low = project(*packed_all, w_pair, cosine, sine, seg_len)
    kv_zero = jnp.concatenate([kv_low, marks_tail], axis=0)
    g_all = plane_gather(after(cot_low, kv_zero))
    kv_one = shift(kv_zero, 1)
    kv_two = shift(kv_one, 1)
    kv = (kv_zero, kv_one, kv_two)
    qseg = marks_all.astype(F32).reshape(2 * seqs, 1, seg_len)
    attn_mix, stat, out_low, out_high = attend(
        info, after(query, joined), kv, qseg, w_out, seg_len
    )
    resid_one = tokens_f + plane_reduce(out_low, out_high)
    scale_two = norm_scale(resid_one)
    expert_in = (resid_one * scale_two * gains[1]).astype(BF)
    e_all = plane_gather(expert_in)

    act, grad_in_low, grad_in_high, e_turned, g_turned = expert_rows(e_all, g_all, my_gates, expert_w, part, 2 * seg_len)
    parts = []

    def weight_grads(h, then):
        grads = expert_grads(e_turned, g_turned, after(act, then), h, halves, piece, 4 * part)
        parts.append(grads)
        return after(then, grads)

    waits = [None, lambda sent: weight_grads(0, sent), None]
    if halves == 2:
        waits[2] = lambda sent: (weight_grads(1, sent[0]), sent[1])
    grad_expert_in = plane_reduce(grad_in_low, grad_in_high, waits)

    cot_rows = cot_low.astype(F32)
    norm_grad_two = norm_back(resid_one, scale_two, gains[1], grad_expert_in)
    gain_grad_two = jnp.sum(grad_expert_in * resid_one * scale_two, axis=0)
    grad_resid = cot_rows + norm_grad_two
    expert_of = (held - 6) // 3
    kind_of = (held - 6) % 3
    place = jnp.where(held >= 6, kind_of * group + expert_of % group, 0)
    side = jnp.where(held >= 6, (expert_of // group) ^ x_index, 2)

    def pack_slots(total, *first):
        give = lax.dynamic_slice_in_dim(total, (1 - x_index) * piece, piece, axis=0)
        return pack(place, side, info, total, after(swap(give, "x"), *first), part)

    def to_owners(send):
        got = lax.all_to_all(send, WSH, split_axis=0, concat_axis=0, tiled=True)
        return got.reshape(4, slot_count, piece, part)

    sums = [lax.psum_scatter(parts[0], "z", scatter_dimension=0, tiled=True)]
    dy_all = after(plane_gather(grad_resid.astype(BF)), *sums)
    if halves == 2:
        sums.append(lax.psum_scatter(after(parts[1], *sums), "z", scatter_dimension=0, tiled=True))
    grad_q_low, dkv_zero, dkv_one, dkv_two, grad_w_out = attend_back(
        info, query, kv, qseg, stat, dy_all, attn_mix, w_out, cosine, sine, seg_len
    )
    passed_one = shift(dkv_two, -1)
    packs = [pack_slots(sums[0], grad_q_low)]
    slot_grads = [to_owners(packs[0])]
    moe_low, moe_high = expert_out(after(act, grad_q_low, packs[0]), expert_w, 2 * seg_len)
    passed_one = after(passed_one, moe_high, *sums)
    passed = shift((dkv_one + passed_one.astype(F32)).astype(BF), -1)
    resid_two = resid_one + plane_reduce(
        moe_low,
        moe_high,
        (None, lambda sent: after(sent, passed_one), None),
    )
    output = (resid_two.astype(BF))
    if halves == 2:
        packs.append(pack_slots(after(sums[1], slot_grads[0])))
        slot_grads.append(to_owners(packs[1]))
    grad_one_low, grad_one_high, attn_grads, gain_part = project_back(
        grad_q_low, after(dkv_zero, *packs), passed, packed_all, w_pair, cosine, sine, grad_w_out, seg_len
    )
    grad_in_one = plane_reduce(
        grad_one_low, grad_one_high, (None, lambda sent: after(sent, *slot_grads), None)
    )
    gain_grad_one = jnp.sum(gain_part, axis=0) / gains[0]
    norm_grad_one = norm_back(tokens_f, scale_one, gains[0], grad_in_one)
    input_grad = (grad_resid + norm_grad_one)

    attn_sum = lax.psum_scatter(attn_grads, "z", scatter_dimension=0, tiled=True)
    attn_rows = jnp.broadcast_to(
        after(attn_sum, *slot_grads).reshape(2, 1, row_count, 3 * part), (2, 4, row_count, 3 * part)
    ).reshape(8, row_count, 3 * part)
    attn_back = lax.all_to_all(attn_rows, PLANE, split_axis=0, concat_axis=0, tiled=True)

    held_mine = lax.dynamic_slice_in_dim(held, w_index * slot_count, slot_count)
    table = jnp.asarray(np.array([7, 0, 0, 1, 2, 3, 3] + [4, 5, 6] * experts, np.int32))
    rates = jnp.take(jnp.asarray(kind_rates(width, hidden), F32), jnp.take(table, held_mine + 1))
    new_masters, new_first, new_second = update(
        held_mine, rates, attn_back, slot_grads, masters, first_moments, second_moments
    )
    gain_grad = (sum_everywhere(after(jnp.stack([gain_grad_one, gain_grad_two]), attn_sum)))
    new_gains, new_gain_first, new_gain_second = adamw(
        norm_gains, gain_first, gain_second, gain_grad, GAIN_RATE, 0.0
    )
    return (
        output[None],
        input_grad[None],
        new_masters,
        new_first,
        new_second,
        new_gains,
        new_gain_first,
        new_gain_second,
    )


def solution(mesh):
    ctx, wsh = mesh.devices.shape
    fine = Mesh(mesh.devices.reshape(ctx // 2, 2, wsh // 2, 2), ("z", "x", "y", "c"))
    rows = P(WSH, ("z", "x"), None)
    marks = P(WSH, ("z", "x"))
    return jax.shard_map(
        shards,
        mesh=fine,
        in_specs=(rows, marks, rows, rows, rows, P(), rows, rows, rows, P(), P(), P()),
        out_specs=(rows, rows, rows, rows, rows, P(), P(), P()),
        check_vma=False,
    )
```

```python
import jax
import jax.numpy as jnp
import numpy as np
from jax import lax
from jax.experimental import pallas as pl
from jax.experimental.pallas import tpu as pltpu
from jax.sharding import Mesh
from jax.sharding import PartitionSpec as P

QH = 16
KVH = 8
HD = 64
STEP = 7

EPS_NORM = 1e-05
THETA = 10000.0
BETA_ONE = 0.5
BETA_TWO = 0.6
ADAM_EPS = 1e-08
DECAY = 0.1
GAIN_RATE = 0.3
NEG_BIG = -1e30
PLANE = ("x", "y", "c")
WSH = ("y", "c")
BF = jnp.bfloat16
F32 = jnp.float32


def swap(value, axis):
    return lax.ppermute(value, axis, [(0, 1), (1, 0)])


def shift(value, by):
    count = lax.axis_size("z")
    pairs = [(i, i + by) for i in range(count) if 0 <= i + by < count]
    return lax.ppermute(value, "z", pairs)


def took(us):
    return pl.CostEstimate(flops=int(us * 1e9), bytes_accessed=2**20, transcendentals=0)


def vmem(mib):
    return pltpu.CompilerParams(vmem_limit_bytes=mib * 2**20)


def whole(shape):
    return pl.BlockSpec(shape, lambda *_: (0,) * len(shape))


def half_specs(block, width, rows, at):
    low = pl.BlockSpec((block, width), lambda *g: (jnp.minimum(at(*g), rows // 2 // block - 1), 0))
    high = pl.BlockSpec((block, width), lambda *g: (jnp.maximum(at(*g) - rows // 2 // block, 0), 0))
    return [low, high]


def together(*values):
    return lax.optimization_barrier(values)


def after(value, *first):
    return lax.optimization_barrier((value, *first))[0]


def stack_kernel(*refs):
    at = 0
    for ref in refs[:-1]:
        refs[-1][at : at + ref.shape[0]] = ref[...]
        at += ref.shape[0]


def stack(pieces):
    shape = (sum(piece.shape[0] for piece in pieces), pieces[0].shape[1])
    return pl.pallas_call(
        stack_kernel,
        grid=(1,),
        in_specs=[whole(piece.shape) for piece in pieces],
        out_specs=whole(shape),
        out_shape=jax.ShapeDtypeStruct(shape, BF),
        cost_estimate=took(2),
        compiler_params=vmem(32),
    )(*pieces)


def plane_gather(rows, wait=lambda value: value, last=lambda value: value):
    half = rows.shape[0] // 2
    over_x = swap(rows, "x")
    over_y = swap(rows, "y")
    first, second = wait((over_x[:half], over_y[half:]))
    corner_top = swap(first, "y")
    corner_low = swap(second, "x")
    mine = stack([rows, over_x, over_y, corner_top, corner_low])
    return mine, swap(last(mine), "c")


def corner_kernel(kept_ref, got_ref, out_ref):
    out_ref[...] = (kept_ref[...].astype(F32) + got_ref[...].astype(F32)).astype(BF)


def corner_rows(kept, got):
    rows, width = kept.shape
    spec = pl.BlockSpec((rows // 4, width), lambda i: (3, 0))
    return pl.pallas_call(
        corner_kernel,
        grid=(1,),
        in_specs=[spec, spec],
        out_specs=whole((rows // 4, width)),
        out_shape=jax.ShapeDtypeStruct((rows // 4, width), BF),
        cost_estimate=took(1),
        compiler_params=vmem(32),
    )(kept, got)


def edge_kernel(kx_ref, gx_ref, ky_ref, gy_ref, fx_ref, fy_ref, x_ref, y_ref):
    half = fx_ref.shape[0]
    for kept, got, extra, out_ref, at in ((kx_ref, gx_ref, fx_ref, x_ref, 0), (ky_ref, gy_ref, fy_ref, y_ref, 1)):
        total = kept[...].astype(F32) + got[...].astype(F32)
        mine, rest = slice(at * half, (at + 1) * half), slice((1 - at) * half, (2 - at) * half)
        out_ref[mine] = (total[mine] + extra[...].astype(F32)).astype(BF)
        out_ref[rest] = total[rest].astype(BF)


def edge_rows(kept, got, for_x, for_y):
    rows, width = kept.shape
    step = rows // 4
    one, two = (pl.BlockSpec((step, width), lambda i, b=b: (b, 0)) for b in (1, 2))
    half = whole((step // 2, width))
    return pl.pallas_call(
        edge_kernel,
        grid=(1,),
        in_specs=[one, one, two, two, half, half],
        out_specs=[whole((step, width))] * 2,
        out_shape=[jax.ShapeDtypeStruct((step, width), BF)] * 2,
        cost_estimate=took(2),
        compiler_params=vmem(32),
    )(kept, got, kept, got, for_x, for_y)


def plane_reduce(kept, sent, waits=(None, None, None)):
    hold = [wait or (lambda value: value) for wait in waits]
    step = kept.shape[0] // 4
    half = step // 2
    got = swap(hold[0](sent), "c")
    corner = hold[1](corner_rows(kept, got))
    for_x = swap(corner[:half], "y")
    for_y = swap(corner[half:], "x")
    to_x, to_y = hold[2](edge_rows(kept, got, for_x, for_y))
    own = kept[:step].astype(F32) + got[:step].astype(F32)
    return own + swap(to_x, "x").astype(F32) + swap(to_y, "y").astype(F32)


def norm_scale(values):
    return lax.rsqrt(jnp.mean(values * values, axis=-1, keepdims=True) + EPS_NORM)


def norm_back(values, scale_row, gain_row, grad_out):
    weighted = grad_out * gain_row
    grad_in = scale_row * weighted - values * scale_row**3 * jnp.mean(
        values * weighted, axis=-1, keepdims=True
    )
    return grad_in


def kind_rates(width, hidden):
    base_rate = 0.5 * width ** (-0.5)
    return [
        base_rate,
        base_rate,
        base_rate,
        2.0 * (2 * hidden) ** (-0.5),
        base_rate,
        base_rate,
        3.0 * hidden ** (-0.5),
        base_rate,
    ]


def adamw(weight, first, second, grad, rate, decay):
    first_new = BETA_ONE * first + (1.0 - BETA_ONE) * grad
    second_new = BETA_TWO * second + (1.0 - BETA_TWO) * grad * grad
    first_hat = first_new / (1.0 - BETA_ONE**STEP)
    second_hat = second_new / (1.0 - BETA_TWO**STEP)
    weight_new = weight - rate * (first_hat / (jnp.sqrt(second_hat) + ADAM_EPS) + decay * weight)
    return (weight_new, first_new, second_new)


def dot_nn(left, right):
    return lax.dot_general(left, right, (((1,), (0,)), ((), ())), preferred_element_type=F32)


def dot_nt(left, right):
    return lax.dot_general(left, right, (((1,), (1,)), ((), ())), preferred_element_type=F32)


def dot_tn(left, right):
    return lax.dot_general(left, right, (((0,), (0,)), ((), ())), preferred_element_type=F32)


def turn(value, lane):
    low = (lane % HD) < (HD // 2)
    return jnp.where(
        low, -pltpu.roll(value, 2 * HD - HD // 2, 1), pltpu.roll(value, HD // 2, 1)
    )

def choose(early, low_ref, high_ref):
    return jnp.where(early, low_ref[...], high_ref[...])


def attn_send_kernel(at_ref, ok_ref, *refs):
    mats, out_ref = refs[:6], refs[6]

    def read(m):
        return jnp.where(ok_ref[m] == 1, mats[m][0], 0.0).astype(BF)

    part = out_ref.shape[3]
    for side in range(2):
        for kind, m in ((0, side), (2, 4 + side)):
            mat = read(m)
            for j in range(4):
                out_ref[4 * side + j, kind] = mat[:, j * part : (j + 1) * part]
    keys, values = read(2), read(3)
    for h in range(8):
        both = (keys[:, h * HD : (h + 1) * HD], values[:, h * HD : (h + 1) * HD])
        out_ref[h, 1] = jnp.concatenate(both, axis=1)


def attn_send(masters, at, ok):
    _, rows, hidden = masters.shape
    part = hidden // 4
    specs = [pl.BlockSpec((1, rows, hidden), lambda i, at, ok, m=m: (at[m], 0, 0)) for m in range(6)]
    return pl.pallas_call(
        attn_send_kernel,
        grid_spec=pltpu.PrefetchScalarGridSpec(
            num_scalar_prefetch=2,
            grid=(1,),
            in_specs=specs,
            out_specs=pl.BlockSpec((8, 3, rows, part), lambda i, at, ok: (0, 0, 0, 0)),
        ),
        out_shape=jax.ShapeDtypeStruct((8, 3, rows, part), BF),
        cost_estimate=took(3),
        compiler_params=vmem(62),
    )(at, ok, *([masters] * 6))


def bulk_send_kernel(info_ref, in_ref, *outs):
    part = outs[0].shape[2]
    for d, out_ref in enumerate(outs):
        start = pl.multiple_of((info_ref[1] ^ d) * part, part)
        out_ref[...] = in_ref[:, :, pl.ds(start, part)].astype(BF)


def bulk_send(info, masters):
    slots, rows, hidden = masters.shape
    step, part = 5 if slots % 5 == 0 else 1, hidden // 4
    return pl.pallas_call(
        bulk_send_kernel,
        grid=(slots // step,),
        in_specs=[
            pl.BlockSpec(memory_space=pltpu.SMEM),
            pl.BlockSpec((step, rows, hidden), lambda i: (i, 0, 0)),
        ],
        out_specs=[pl.BlockSpec((step, rows, part), lambda i: (i, 0, 0))] * 4,
        out_shape=[jax.ShapeDtypeStruct((slots, rows, part), BF)] * 4,
        cost_estimate=took(4),
        compiler_params=vmem(62),
    )(info, masters)


def over_wsh(arrays):
    across = [(i, i ^ 3) for i in range(4)]
    return [arrays[0], swap(arrays[1], "c"), swap(arrays[2], "y"), lax.ppermute(arrays[3], WSH, across)]


def pick_kernel(at_ref, *refs):
    slots, outs, held = refs[:4], refs[4:-1], refs[-1]
    count = slots[0].shape[0]
    part = held.shape[2]
    for d in range(4):
        held[d * count : (d + 1) * count] = slots[d][...]
    for i, out_ref in enumerate(outs):
        number = out_ref.shape[1] // part
        for k in range(number):
            out_ref[:, k * part : (k + 1) * part] = held[at_ref[i * number + k]]


def pick(places, slots, parts):
    count, rows, part = slots[0].shape
    wide = (rows, places.shape[0] // parts * part)
    return pl.pallas_call(
        pick_kernel,
        grid_spec=pltpu.PrefetchScalarGridSpec(
            num_scalar_prefetch=1,
            grid=(1,),
            in_specs=[pl.BlockSpec((count, rows, part), lambda i, a: (0, 0, 0))] * 4,
            out_specs=[pl.BlockSpec(wide, lambda i, a: (0, 0))] * parts,
            scratch_shapes=[pltpu.VMEM((4 * count, rows, part), BF)],
        ),
        out_shape=[jax.ShapeDtypeStruct(wide, BF)] * parts,
        cost_estimate=took(3),
        compiler_params=vmem(62),
    )(places, *slots)


def join_kernel(info_ref, *refs):
    count = len(refs) // 2
    keeps, gots, out_ref = refs[:count], refs[count:-1], refs[-1]
    rows, wide = keeps[0].shape
    first = info_ref[0] == 0
    for i in range(count):
        keep, got, lanes = keeps[i][...], gots[i][...], slice(i * wide, (i + 1) * wide)
        out_ref[:rows, lanes] = jnp.where(first, keep, got)
        out_ref[rows:, lanes] = jnp.where(first, got, keep)


def join(info, keeps, gots):
    rows, wide = keeps[0].shape
    shape = (2 * rows, wide * len(keeps))
    return pl.pallas_call(
        join_kernel,
        grid=(1,),
        in_specs=[pl.BlockSpec(memory_space=pltpu.SMEM)] + [whole((rows, wide))] * (2 * len(keeps)),
        out_specs=whole(shape),
        out_shape=jax.ShapeDtypeStruct(shape, BF),
        cost_estimate=took(1.5),
        compiler_params=vmem(32),
    )(info, *keeps, *gots)


def pack_kernel(place_ref, side_ref, info_ref, total_ref, got_ref, *outs):
    count, rows, part = outs[0].shape
    mine = pl.ds(pl.multiple_of(info_ref[0] * rows, rows), rows)
    for d, out_ref in enumerate(outs):

        def one(j, carry):
            s = (info_ref[1] ^ d) * count + j
            lanes = pl.ds(pl.multiple_of(place_ref[s] * part, part), part)

            @pl.when(side_ref[s] == 0)
            def _():
                out_ref[j] = total_ref[mine, lanes]

            @pl.when(side_ref[s] == 1)
            def _():
                out_ref[j] = got_ref[:, lanes]

            @pl.when(side_ref[s] == 2)
            def _():
                out_ref[j] = jnp.zeros((rows, part), BF)

            return carry

        lax.fori_loop(0, count, one, 0)


def pack(place, side, info, summed, got, part):
    rows, wide = got.shape
    shape = (place.shape[0] // 4, rows, part)
    return pl.pallas_call(
        pack_kernel,
        grid_spec=pltpu.PrefetchScalarGridSpec(
            num_scalar_prefetch=3,
            grid=(1,),
            in_specs=[
                pl.BlockSpec((2 * rows, wide), lambda i, a, b, c: (0, 0)),
                pl.BlockSpec((rows, wide), lambda i, a, b, c: (0, 0)),
            ],
            out_specs=[pl.BlockSpec(shape, lambda i, a, b, c: (0, 0, 0))] * 4,
        ),
        out_shape=[jax.ShapeDtypeStruct(shape, BF)] * 4,
        cost_estimate=took(4),
        compiler_params=vmem(32),
    )(place, side, info, summed, got)


def update_kernel(info_ref, rate_ref, *refs):
    grads, (w_ref, m_ref, v_ref, w_out, m_out, v_out) = refs[:-6], refs[-6:]
    part = grads[0].shape[2]
    rows = grads[0].shape[1]

    def one(s, carry):
        rate = rate_ref[pl.program_id(0) * w_ref.shape[0] + s]
        for i, grad_ref in enumerate(grads):
            lanes = pl.ds(pl.multiple_of((info_ref[1] ^ (i % 4)) * part, part), part)
            at = slice((i // 4) * rows, (i // 4 + 1) * rows)
            w_out[s, at, lanes], m_out[s, at, lanes], v_out[s, at, lanes] = adamw(
                w_ref[s, at, lanes],
                m_ref[s, at, lanes],
                v_ref[s, at, lanes],
                grad_ref[s].astype(F32),
                rate,
                DECAY,
            )
        return carry

    lax.fori_loop(0, w_ref.shape[0], one, 0)


def update(info, rates, grads, masters, first, second):
    slots, rows, hidden = masters.shape
    step = 4 if slots % 4 == 0 else 1
    smem = pl.BlockSpec(memory_space=pltpu.SMEM)
    spec = pl.BlockSpec((step, rows, hidden), lambda i: (i, 0, 0))
    grad_spec = pl.BlockSpec((step, *grads[0].shape[1:]), lambda i: (i, 0, 0))
    return pl.pallas_call(
        update_kernel,
        grid=(slots // step,),
        in_specs=[smem, smem] + [grad_spec] * len(grads) + [spec] * 3,
        out_specs=[spec] * 3,
        out_shape=[jax.ShapeDtypeStruct(masters.shape, F32)] * 3,
        cost_estimate=took(14),
        compiler_params=vmem(62),
    )(info, rates, *grads, masters, first, second)


def update_attn_kernel(slot_ref, held_ref, rate_ref, attn_ref, *refs):
    (w_ref, m_ref, v_ref), olds, news = refs[:3], refs[3:6], refs[6:]
    step = pl.program_id(0)
    held = held_ref[step]
    rate = rate_ref[step]
    part = w_ref.shape[2] // 4

    def write(j, grad):
        lanes = slice(j * part, (j + 1) * part)
        results = adamw(
            w_ref[0, :, lanes], m_ref[0, :, lanes], v_ref[0, :, lanes], grad.astype(F32), rate, DECAY
        )
        for new_ref, result in zip(news, results):
            new_ref[0, :, lanes] = result

    @pl.when(held < 0)
    def _():
        for old_ref, new_ref in zip(olds, news):
            new_ref[...] = old_ref[...]

    for m, side, kind in ((0, 0, 0), (1, 1, 0), (4, 0, 2), (5, 1, 2)):

        @pl.when(held == m)
        def _():
            for j in range(4):
                write(j, attn_ref[4 * side + j, :, kind * part : (kind + 1) * part])

    for m, start in ((2, part), (3, part + HD)):

        @pl.when(held == m)
        def _():
            for j in range(4):
                pieces = [attn_ref[2 * j + i, :, start : start + HD] for i in range(2)]
                write(j, jnp.concatenate(pieces, axis=1))


def update_attn(slots, held, rates, attn_back, masters, first, second, new):
    _, rows, hidden = masters.shape
    spec = pl.BlockSpec((1, rows, hidden), lambda i, at, held: (at[i], 0, 0))
    return pl.pallas_call(
        update_attn_kernel,
        grid_spec=pltpu.PrefetchScalarGridSpec(
            num_scalar_prefetch=2,
            grid=(slots.shape[0],),
            in_specs=[
                pl.BlockSpec(memory_space=pltpu.SMEM),
                pl.BlockSpec(attn_back.shape, lambda i, at, held: (0, 0, 0)),
                *[spec] * 6,
            ],
            out_specs=[spec] * 3,
        ),
        out_shape=[jax.ShapeDtypeStruct(masters.shape, F32)] * 3,
        input_output_aliases={7: 0, 8: 1, 9: 2},
        cost_estimate=took(5),
        compiler_params=vmem(62),
    )(slots, held, rates, attn_back, masters, first, second, *new)


def project_kernel(low_ref, high_ref, w_ref, cos_ref, sin_ref, q_ref, kv_ref):
    early = pl.program_id(0) < pl.num_programs(0) // 2
    both = dot_nn(choose(early, low_ref, high_ref), w_ref[...])
    cosine = cos_ref[0]
    sine = sin_ref[0]
    lane = lax.broadcasted_iota(jnp.int32, cosine.shape, 1)
    query = both[:, : 2 * HD]
    pair = both[:, 2 * HD :]
    q_ref[...] = (query * cosine + turn(query, lane) * sine).astype(BF)
    turned = pair * cosine + turn(pair, lane) * sine
    kv_ref[...] = jnp.where(lane < HD, turned, pair).astype(BF)


def project(x_low, x_high, weights, cosine, sine, block):
    rows = 2 * x_low.shape[0]
    width = weights.shape[0]
    table = pl.BlockSpec((1, block, 2 * HD), lambda i: (i % 2, 0, 0))
    return pl.pallas_call(
        project_kernel,
        grid=(rows // block,),
        in_specs=[
            *half_specs(block, width, rows, lambda i: i),
            pl.BlockSpec((width, 4 * HD), lambda i: (0, 0)),
            table,
            table,
        ],
        out_specs=[pl.BlockSpec((block, 2 * HD), lambda i: (i, 0))] * 2,
        out_shape=[jax.ShapeDtypeStruct((rows, 2 * HD), BF)] * 2,
        cost_estimate=took(6),
        compiler_params=vmem(32),
    )(x_low, x_high, weights, cosine, sine)


def head_rows(rows, head, lane, high):
    if (head == 1) != high:
        rows = pltpu.roll(rows, HD, 1)
    keep = (lane >= HD) if high else (lane < HD)
    return jnp.where(keep, rows, jnp.zeros_like(rows))


def masks(info_ref, qseg_ref, kseg, block, span):
    flip = info_ref[0]
    chunk = pl.program_id(1)
    key_at = lax.broadcasted_iota(jnp.int32, (span, 1), 0)
    query_at = lax.broadcasted_iota(jnp.int32, (1, block), 1)
    swapped = jnp.where(flip == 1, key_at ^ block, key_at)
    key_pos = jnp.where(key_at < 2 * block, swapped, -1)
    query_pos = query_at + block * jnp.where(flip == 1, 1 - chunk, chunk)
    return (key_pos <= query_pos) & (kseg == qseg_ref[0])


def load_pairs(refs, tails, kv_all, kv_turned, marks, kseg):
    third = kv_all.shape[0] // 3
    for i, (ref, tail) in enumerate(zip(refs, tails)):
        kv_all[i * third : (i + 1) * third] = ref[...]
        marks[i] = tail[...].astype(F32).reshape(marks.shape[1:])
        columns = marks[i, pl.program_id(0)].T
        for j in range(third // 128):
            at = i * third + j * 128
            kseg[at : at + 128] = columns[:, j : j + 1]
    kv_turned[...] = kv_all[...].T


def attend_kernel(info_ref, q_ref, k0_ref, k1_ref, k2_ref, t0_ref, t1_ref, t2_ref, qseg_ref,
                  w_ref, mix_ref, stat_ref, low_ref, high_ref, kv_all, kv_turned, marks, kseg):
    block = q_ref.shape[0]
    span = kv_all.shape[0]

    @pl.when(pl.program_id(1) == 0)
    def _():
        load_pairs((k0_ref, k1_ref, k2_ref), (t0_ref, t1_ref, t2_ref), kv_all, kv_turned, marks, kseg)

    allowed = masks(info_ref, qseg_ref, kseg[...], block, span)
    lane = lax.broadcasted_iota(jnp.int32, (block, 2 * HD), 1)
    query = q_ref[...] * jnp.asarray(HD**-0.5, BF)
    mixed = []
    for head in range(2):
        scores = dot_nt(kv_all[...], head_rows(query, head, lane, False))
        scores = jnp.where(allowed, scores, NEG_BIG)
        top = jnp.max(scores, axis=0, keepdims=True)
        powers = jnp.exp(scores - top)
        total = jnp.sum(powers, axis=0, keepdims=True)
        stat_ref[0, 0, head : head + 1, :] = top + jnp.log(total)
        probs = (powers * (1.0 / total)).astype(BF)
        mixed.append(dot_nn(kv_turned[...], probs)[HD:])
    mix = jnp.concatenate(mixed, axis=0).T.astype(BF)
    mix_ref[...] = mix
    out = dot_nt(mix, w_ref[...]).astype(BF)
    early = pl.program_id(0) < pl.num_programs(0) // 2

    @pl.when(early)
    def _():
        low_ref[...] = out

    @pl.when(jnp.logical_not(early))
    def _():
        high_ref[...] = out


def attend(info, query, kv, qseg, weights, block):
    rows = query.shape[0]
    seqs = rows // (2 * block)
    width = weights.shape[0]
    row_spec = pl.BlockSpec((block, 2 * HD), lambda s, i: (2 * s + i, 0))
    kv_spec = pl.BlockSpec((2 * block, 2 * HD), lambda s, i: (s, 0))
    tail_spec = pl.BlockSpec((8 * seqs, 2 * HD), lambda s, i: (rows // (8 * seqs), 0))
    return pl.pallas_call(
        attend_kernel,
        grid=(seqs, 2),
        in_specs=[
            pl.BlockSpec(memory_space=pltpu.SMEM),
            row_spec,
            kv_spec,
            kv_spec,
            kv_spec,
            tail_spec,
            tail_spec,
            tail_spec,
            pl.BlockSpec((1, 1, block), lambda s, i: (2 * s + i, 0, 0)),
            pl.BlockSpec((width, 2 * HD), lambda s, i: (0, 2)),
        ],
        out_specs=[
            row_spec,
            pl.BlockSpec((1, 1, 2, block), lambda s, i: (s, i, 0, 0)),
            *half_specs(block, width, rows, lambda s, i: 2 * s + i),
        ],
        out_shape=[
            jax.ShapeDtypeStruct((rows, 2 * HD), BF),
            jax.ShapeDtypeStruct((seqs, 2, 2, block), F32),
            *[jax.ShapeDtypeStruct((rows // 2, width), BF)] * 2,
        ],
        scratch_shapes=[
            pltpu.VMEM((6 * block, 2 * HD), BF),
            pltpu.VMEM((2 * HD, 6 * block), BF),
            pltpu.VMEM((3, seqs, 8, 128), F32),
            pltpu.VMEM((6 * block, 1), F32),
        ],
        cost_estimate=took(24),
        compiler_params=vmem(62),
    )(info, query, *kv, *kv, qseg, weights)


def attend_back_kernel(info_ref, q_ref, k0_ref, k1_ref, k2_ref, t0_ref, t1_ref, t2_ref, qseg_ref,
                       stat_ref, dy_low, dy_high, mix_ref, w_ref, cos_ref, sin_ref,
                       dq_ref, dk0_ref, dk1_ref, dk2_ref, dw_ref,
                       kv_all, kv_turned, marks, kseg, sums, dw_sum):
    block = q_ref.shape[0]
    span = kv_all.shape[0]
    third = span // 3
    seq = pl.program_id(0)
    chunk = pl.program_id(1)

    @pl.when((chunk == 0) & (seq == 0))
    def _():
        dw_sum[...] = jnp.zeros_like(dw_sum)

    @pl.when(chunk == 0)
    def _():
        sums[...] = jnp.zeros_like(sums)
        load_pairs((k0_ref, k1_ref, k2_ref), (t0_ref, t1_ref, t2_ref), kv_all, kv_turned, marks, kseg)

    allowed = masks(info_ref, qseg_ref, kseg[...], block, span)
    lane = lax.broadcasted_iota(jnp.int32, (block, 2 * HD), 1)
    query = q_ref[...] * jnp.asarray(HD**-0.5, BF)
    grad_rows = choose(seq < pl.num_programs(0) // 2, dy_low, dy_high)
    dw_sum[...] += dot_tn(mix_ref[...], grad_rows)
    grad_mix = dot_nn(grad_rows, w_ref[...]).astype(BF)
    grad_query = []
    for head in range(2):
        q_low = head_rows(query, head, lane, False)
        g_high = head_rows(grad_mix, head, lane, True)
        scores = dot_nt(kv_all[...], q_low)
        stat = stat_ref[0, 0, head : head + 1, :]
        probs = jnp.where(allowed, jnp.exp(scores - stat), 0.0)
        grad_probs = dot_nt(kv_all[...], g_high)
        delta = jnp.sum(probs * grad_probs, axis=0, keepdims=True)
        grad_scores = (probs * (grad_probs - delta)).astype(BF)
        sums[...] += dot_nn(grad_scores, q_low) + dot_nn(probs.astype(BF), g_high)
        grad_query.append(dot_nn(kv_turned[...], grad_scores)[:HD])
    grad_q = jnp.concatenate(grad_query, axis=0).T * HD**-0.5
    dq_ref[...] = (grad_q * cos_ref[0] - turn(grad_q * sin_ref[0], lane)).astype(BF)

    @pl.when(chunk == 1)
    def _():
        dk0_ref[...] = sums[:third]
        dk1_ref[...] = sums[third : 2 * third]
        dk2_ref[...] = sums[2 * third :].astype(BF)

    @pl.when((chunk == 1) & (seq == pl.num_programs(0) - 1))
    def _():
        dw_ref[...] = dw_sum[...].T.astype(BF)


def attend_back(info, query, kv, qseg, stat, grad_rows, mix, weights, cosine, sine, block):
    rows = query.shape[0]
    seqs = rows // (2 * block)
    width = weights.shape[0]
    row_spec = pl.BlockSpec((block, 2 * HD), lambda s, i: (2 * s + i, 0))
    kv_spec = pl.BlockSpec((2 * block, 2 * HD), lambda s, i: (s, 0))
    tail_spec = pl.BlockSpec((8 * seqs, 2 * HD), lambda s, i: (rows // (8 * seqs), 0))
    table = pl.BlockSpec((1, block, 2 * HD), lambda s, i: (i, 0, 0))
    return pl.pallas_call(
        attend_back_kernel,
        grid=(seqs, 2),
        in_specs=[
            pl.BlockSpec(memory_space=pltpu.SMEM),
            row_spec,
            kv_spec,
            kv_spec,
            kv_spec,
            tail_spec,
            tail_spec,
            tail_spec,
            pl.BlockSpec((1, 1, block), lambda s, i: (2 * s + i, 0, 0)),
            pl.BlockSpec((1, 1, 2, block), lambda s, i: (s, i, 0, 0)),
            *half_specs(block, width, rows, lambda s, i: 2 * s + i),
            row_spec,
            pl.BlockSpec((width, 2 * HD), lambda s, i: (0, 2)),
            table,
            table,
        ],
        out_specs=[row_spec, kv_spec, kv_spec, kv_spec, whole((width, 2 * HD))],
        out_shape=[
            jax.ShapeDtypeStruct((rows, 2 * HD), BF),
            jax.ShapeDtypeStruct((rows, 2 * HD), F32),
            jax.ShapeDtypeStruct((rows, 2 * HD), F32),
            jax.ShapeDtypeStruct((rows, 2 * HD), BF),
            jax.ShapeDtypeStruct((width, 2 * HD), BF),
        ],
        scratch_shapes=[
            pltpu.VMEM((6 * block, 2 * HD), BF),
            pltpu.VMEM((2 * HD, 6 * block), BF),
            pltpu.VMEM((3, seqs, 8, 128), F32),
            pltpu.VMEM((6 * block, 1), F32),
            pltpu.VMEM((6 * block, 2 * HD), F32),
            pltpu.VMEM((2 * HD, width), F32),
        ],
        cost_estimate=took(28),
        compiler_params=vmem(62),
    )(info, query, *kv, *kv, qseg, stat, *grad_rows, mix, weights, cosine, sine)


def project_back_kernel(dq_ref, a_ref, b_ref, x_low, x_high, w_ref, cos_ref, sin_ref, dout_ref,
                        low_ref, high_ref, dw_ref, gain_ref, dw_sum):
    step = pl.program_id(0)

    @pl.when(step == 0)
    def _():
        dw_sum[...] = jnp.zeros_like(dw_sum)
        gain_ref[...] = jnp.zeros_like(gain_ref)

    grad = a_ref[...] + b_ref[...].astype(F32)
    lane = lax.broadcasted_iota(jnp.int32, grad.shape, 1)
    turned = grad * cos_ref[0] - turn(grad * sin_ref[0], lane)
    pair = jnp.where(lane < HD, turned, grad).astype(BF)
    both = jnp.concatenate([dq_ref[...], pair], axis=1)
    grad_in = dot_nt(both, w_ref[...])
    early = step < pl.num_programs(0) // 2

    @pl.when(early)
    def _():
        low_ref[...] = grad_in.astype(BF)

    @pl.when(jnp.logical_not(early))
    def _():
        high_ref[...] = grad_in.astype(BF)

    x_rows = choose(early, x_low, x_high)
    dw_sum[...] += dot_tn(both, x_rows)
    weighted = grad_in * x_rows.astype(F32)
    gain_ref[...] += jnp.sum(weighted.reshape(-1, 8, weighted.shape[1]), axis=0)

    @pl.when(step == pl.num_programs(0) - 1)
    def _():
        dw_ref[:, : 4 * HD] = dw_sum[...].T.astype(BF)
        dw_ref[:, 4 * HD :] = dout_ref[...]


def project_back(grad_q, here, arrived, x_rows, weights, cosine, sine, grad_out, block):
    rows = here.shape[0]
    width, cols = weights.shape[0], 4 * HD
    spec = pl.BlockSpec((block, 2 * HD), lambda i: (i, 0))
    table = pl.BlockSpec((1, block, 2 * HD), lambda i: (i % 2, 0, 0))
    return pl.pallas_call(
        project_back_kernel,
        grid=(rows // block,),
        in_specs=[
            *[spec] * 3,
            *half_specs(block, width, rows, lambda i: i),
            pl.BlockSpec((width, cols), lambda i: (0, 0)),
            table,
            table,
            whole(grad_out.shape),
        ],
        out_specs=[
            *half_specs(block, width, rows, lambda i: i),
            whole((width, 6 * HD)),
            whole((8, width)),
        ],
        out_shape=[
            *[jax.ShapeDtypeStruct((rows // 2, width), BF)] * 2,
            jax.ShapeDtypeStruct((width, 6 * HD), BF),
            jax.ShapeDtypeStruct((8, width), F32),
        ],
        scratch_shapes=[pltpu.VMEM((cols, width), F32)],
        cost_estimate=took(10),
        compiler_params=vmem(62),
    )(grad_q, here, arrived, *x_rows, weights, cosine, sine, grad_out)


def expert_kernel(part, piece, halves, e_low, e_high, g_low, g_high, gate_ref, w_ref, *refs):
    low_ref, high_ref, hidden_ref = refs[:3]
    grads, (e_ref, g_ref, act_ref, sums) = refs[3 : 3 + halves], refs[3 + halves :]
    rows, width = e_ref.shape
    step_id = pl.program_id(0)
    last = pl.num_programs(0) - 1
    early = step_id < pl.num_programs(0) // 2
    e_ref[...] = choose(early, e_low, e_high)
    g_ref[...] = choose(early, g_low, g_high)
    cols = w_ref.shape[1] // 3
    step = 2 * part
    lane = lax.broadcasted_iota(jnp.int32, (rows, step), 1)
    for j in range(cols // step):
        at = j * step
        gate = jnp.where(lane < part, gate_ref[:, 2 * j : 2 * j + 1], gate_ref[:, 2 * j + 1 : 2 * j + 2])
        pre = dot_nn(e_ref[...], w_ref[:, at : at + step])
        up = dot_nn(e_ref[...], w_ref[:, cols + at : cols + at + step])
        grad = dot_nn(g_ref[...], w_ref[:, 2 * cols + at : 2 * cols + at + step]) * gate
        logistic = 1.0 / (1.0 + jnp.exp(-pre))
        active = pre * logistic
        act_ref[:, at : at + step] = (
            grad * up * logistic * (1.0 + pre * (1.0 - logistic))
        ).astype(BF)
        act_ref[:, cols + at : cols + at + step] = (grad * active).astype(BF)
        act_ref[:, 2 * cols + at : 2 * cols + at + step] = (active * up * gate).astype(BF)
    hidden_ref[...] = act_ref[:, 2 * cols :]
    dx = dot_nt(act_ref[:, : 2 * cols], w_ref[:, : 2 * cols]).astype(BF)

    @pl.when(early)
    def _():
        low_ref[...] = dx

    @pl.when(jnp.logical_not(early))
    def _():
        high_ref[...] = dx

    e_turned = e_ref[...].T
    g_turned = g_ref[...].T
    chunk = 2 * step

    @pl.when(step_id == 0)
    def _():
        for at in range(0, 3 * cols, chunk):
            left = e_turned if at < 2 * cols else g_turned
            sums[:, at : at + chunk] = dot_nn(left, act_ref[:, at : at + chunk])

    @pl.when((step_id > 0) & (step_id < last))
    def _():
        for at in range(0, 3 * cols, chunk):
            left = e_turned if at < 2 * cols else g_turned
            sums[:, at : at + chunk] += dot_nn(left, act_ref[:, at : at + chunk])

    @pl.when(step_id == last)
    def _():
        for at in range(0, 3 * cols, chunk):
            left = e_turned if at < 2 * cols else g_turned
            total = (sums[:, at : at + chunk] + dot_nn(left, act_ref[:, at : at + chunk])).astype(BF)
            for i in range(width // piece):
                out_ref = grads[i % halves]
                to = (i // halves) * piece
                out_ref[to : to + piece, at : at + chunk] = total[i * piece : (i + 1) * piece]


def expert_rows(e_rows, g_rows, gates, weights, part, piece, halves, block):
    rows, width = 2 * e_rows[0].shape[0], e_rows[0].shape[1]
    wide = weights.shape[1]
    once = pl.Buffered(1)
    return pl.pallas_call(
        lambda *refs: expert_kernel(part, piece, halves, *refs),
        grid=(rows // block,),
        in_specs=[
            *half_specs(block, width, rows, lambda i: i) * 2,
            pl.BlockSpec((block, gates.shape[1]), lambda i: (i, 0)),
            pl.BlockSpec(weights.shape, lambda i: (0, 0), pipeline_mode=once),
        ],
        out_specs=[
            *half_specs(block, width, rows, lambda i: i),
            pl.BlockSpec((block, wide // 3), lambda i: (i, 0)),
            *[pl.BlockSpec((width // halves, wide), lambda i: (0, 0), pipeline_mode=once)] * halves,
        ],
        out_shape=[
            *[jax.ShapeDtypeStruct((rows // 2, width), BF)] * 2,
            jax.ShapeDtypeStruct((rows, wide // 3), BF),
            *[jax.ShapeDtypeStruct((width // halves, wide), BF)] * halves,
        ],
        scratch_shapes=[
            *[pltpu.VMEM((block, width), BF)] * 2,
            pltpu.VMEM((block, wide), BF),
            pltpu.VMEM((width, wide), F32),
        ],
        cost_estimate=took(45),
        compiler_params=vmem(62),
    )(*e_rows, *g_rows, gates, weights)


def expert_out_kernel(act_ref, w_ref, low_ref, high_ref):
    out = dot_nt(act_ref[...], w_ref[...]).astype(BF)
    early = pl.program_id(0) < pl.num_programs(0) // 2

    @pl.when(early)
    def _():
        low_ref[...] = out

    @pl.when(jnp.logical_not(early))
    def _():
        high_ref[...] = out


def expert_out(act, weights, block):
    rows, cols = act.shape
    width = weights.shape[0]
    return pl.pallas_call(
        expert_out_kernel,
        grid=(rows // block,),
        in_specs=[
            pl.BlockSpec((block, cols), lambda i: (i, 0)),
            pl.BlockSpec((width, cols), lambda i: (0, 2)),
        ],
        out_specs=half_specs(block, width, rows, lambda i: i),
        out_shape=[jax.ShapeDtypeStruct((rows // 2, width), BF)] * 2,
        cost_estimate=took(8),
        compiler_params=vmem(62),
    )(act, weights)


def shards(
    tokens,
    segments,
    routes,
    gate_weights,
    cotangent,
    owners,
    masters,
    first_moments,
    second_moments,
    norm_gains,
    gain_first,
    gain_second,
):
    z_index = lax.axis_index("z")
    x_index = lax.axis_index("x")
    w_index = lax.axis_index("y") * 2 + lax.axis_index("c")
    slot_count, row_count, hidden = masters.shape
    slot_total = slot_count * 4
    seg_len = tokens.shape[1]
    width = tokens.shape[2]
    ctx_count = width // row_count
    matrix_count = owners.shape[0]
    experts = (matrix_count - 6) // 3
    group = experts // 2
    part = hidden // 4
    halves = 2 if row_count % 32 == 0 else 1
    piece = row_count // halves
    x_even = x_index == 0
    info = jnp.stack([x_index, w_index]).astype(jnp.int32)

    slot_ids = jnp.arange(slot_total, dtype=jnp.int32)
    hits = owners[None, :] == slot_ids[:, None]
    held = jnp.sum(hits * (jnp.arange(matrix_count, dtype=jnp.int32) + 1)[None, :], axis=1) - 1

    local_at = owners[:6] - slot_count * w_index
    local_ok = (local_at >= 0) & (local_at < slot_count)
    attn_sent = attn_send(masters, jnp.clip(local_at, 0, slot_count - 1), local_ok.astype(jnp.int32))
    bulk = bulk_send(info, masters)
    attn_got = lax.all_to_all(attn_sent, PLANE, split_axis=0, concat_axis=0, tiled=True)
    attn_got, *bulk = together(attn_got, *bulk)
    attn_mine = jnp.sum(attn_got.reshape(2, 4, 3, row_count, part).astype(F32), axis=1).astype(BF)
    attn_mine = jnp.transpose(attn_mine, (0, 2, 1, 3)).reshape(2 * row_count, 3 * part)

    order = np.array([[6 + 3 * (group * g + e) + k for k in range(3) for e in range(group)] for g in range(2)])
    picks = jnp.take(owners, jnp.asarray(order))
    picks = jnp.stack([jnp.where(x_even, picks[0], picks[1]), jnp.where(x_even, picks[1], picks[0])])
    places = ((picks // slot_count) ^ w_index) * slot_count + picks % slot_count

    gains = norm_gains
    tokens_f = tokens[0].astype(F32)
    cot_low = cotangent[0]
    scale_one = norm_scale(tokens_f)
    attn_in = (tokens_f * scale_one * gains[0]).astype(BF)
    expert_ids = jnp.arange(experts, dtype=jnp.int32)
    gates = jnp.sum(
        jnp.where(routes[0][:, :, None] == expert_ids[None, None, :], gate_weights[0][:, :, None], 0.0),
        axis=1,
    )
    gates_high = gates.astype(BF)
    gates_low = (gates - gates_high.astype(F32)).astype(BF)
    marks = (segments[0] + 1).astype(BF)[:, None]
    spare = jnp.zeros((seg_len, 128 - 2 * experts - 1), BF)
    packed = jnp.concatenate([attn_in, gates_high, gates_low, marks, spare], axis=1)

    across = [(i, i ^ 3) for i in range(4)]
    half = seg_len // 2
    packed = after(packed, attn_got)
    over_x, over_y, from_y, attn_w = together(
        swap(packed, "x"),
        swap(packed, "y"),
        swap(bulk[2], "y"),
        lax.all_gather(attn_mine, "z", axis=0, tiled=True),
    )
    corner, from_c, from_corner = together(
        swap(over_y, "x"),
        swap(bulk[1], "c"),
        lax.ppermute(after(bulk[3], from_y), WSH, across),
    )
    mine = stack([packed, over_x, over_y, corner])
    other, *picked = together(
        swap(mine, "c"), *pick(places.reshape(-1), [bulk[0], from_c, from_y, from_corner], 2)
    )
    packed_all = (mine, other)
    extras = jnp.concatenate([rows[:, width:] for rows in packed_all], axis=0)
    gates_all = extras[:, :experts].astype(F32) + extras[:, experts : 2 * experts].astype(F32)
    my_gates = jnp.where(x_even, gates_all[:, :group], gates_all[:, group:])
    seqs = 4
    rows_all = seqs * 2 * seg_len
    marks_all = extras[:, 2 * experts].reshape(seqs, -1, 128)
    marks_tail = jnp.pad(marks_all, ((0, 0), (0, 8 - marks_all.shape[1]), (0, 0))).reshape(-1, 128)

    inverse = THETA ** (-(jnp.arange(HD // 2, dtype=F32) * 2.0 / HD))
    at = jnp.arange(seg_len, dtype=jnp.int32)
    first_pos = z_index * 2 * seg_len + x_index * seg_len + at
    second_pos = z_index * 2 * seg_len + (1 - x_index) * seg_len + at
    positions = jnp.stack([first_pos, second_pos])
    angles = positions.astype(F32)[:, :, None] * inverse[None, None, :]
    cosine = jnp.tile(jnp.cos(angles), (1, 1, 4))
    sine = jnp.tile(jnp.sin(angles), (1, 1, 4))

    query, kv_low = project(*packed_all, attn_w, cosine, sine, seg_len)
    kv_zero = jnp.concatenate([kv_low, marks_tail], axis=0)
    kv_one, got_rows = together(shift(kv_zero, 1), swap(picked[1], "x"))
    joined = join(info, picked[:1], [got_rows])
    expert_w = lax.all_gather(joined, "z", axis=0, tiled=True)
    kv_two = shift(after(kv_one, joined), 1)
    g_all = plane_gather(after(cot_low, joined))
    kv = (kv_zero, kv_one, kv_two)
    qseg = marks_all.astype(F32).reshape(2 * seqs, 1, seg_len)
    attn_mix, stat, out_low, out_high = attend(
        info, query, kv, qseg, attn_w, seg_len
    )
    resid_one = tokens_f + plane_reduce(out_low, out_high)
    scale_two = norm_scale(resid_one)
    expert_in = (resid_one * scale_two * gains[1]).astype(BF)
    e_all = plane_gather(expert_in)

    grad_in_low, grad_in_high, hidden_low, *parts = expert_rows(
        e_all, g_all, my_gates, expert_w, part, piece, halves, 2 * seg_len
    )
    grad_expert_in = plane_reduce(grad_in_low, grad_in_high)

    cot_rows = cot_low.astype(F32)
    norm_grad_two = norm_back(resid_one, scale_two, gains[1], grad_expert_in)
    gain_grad_two = jnp.sum(grad_expert_in * resid_one * scale_two, axis=0)
    grad_resid = cot_rows + norm_grad_two
    expert_of = (held - 6) // 3
    kind_of = (held - 6) % 3
    place = jnp.where(held >= 6, kind_of * group + expert_of % group, 0)
    side = jnp.where(held >= 6, (expert_of // group) ^ x_index, 2)

    def over(total):
        give = lax.dynamic_slice_in_dim(total, (1 - x_index) * piece, piece, axis=0)
        return swap(give, "x")

    held_mine = lax.dynamic_slice_in_dim(held, w_index * slot_count, slot_count)
    table = jnp.asarray(np.array([7, 0, 0, 1, 2, 3, 3] + [4, 5, 6] * experts, np.int32))
    rates = jnp.take(jnp.asarray(kind_rates(width, hidden), F32), jnp.take(table, held_mine + 1))

    sums = [lax.psum_scatter(parts[0], "z", scatter_dimension=0, tiled=True)]
    dy = grad_resid.astype(BF)
    over_x, over_y, moe = together(
        swap(dy, "x"), swap(dy, "y"), expert_out(after(hidden_low, dy), expert_w, 2 * seg_len)
    )
    corner_top, corner_low, moe_got = together(
        swap(over_x[:half], "y"), swap(over_y[half:], "x"), swap(moe[1], "c")
    )
    dy_mine = stack([dy, over_x, over_y, corner_top, corner_low])
    dy_other, moe_corner = together(swap(dy_mine, "c"), corner_rows(moe[0], moe_got))
    dy_all = after((dy_mine, dy_other), *sums)
    if halves == 2:
        sums.append(lax.psum_scatter(after(parts[1], *sums), "z", scatter_dimension=0, tiled=True))
    back = attend_back(info, query, kv, qseg, stat, dy_all, attn_mix, attn_w, cosine, sine, seg_len)
    (grad_q_low, dkv_zero, dkv_one, dkv_two, grad_w_out), got_rows, moe_x, moe_y = together(
        back, over(sums[0]), swap(moe_corner[:half], "y"), swap(moe_corner[half:], "x")
    )
    to_x, to_y = edge_rows(moe[0], moe_got, moe_x, moe_y)

    first_half = pack(place, side, info, sums[0], got_rows, part)
    passed_one, slot_grads, out_x, out_y = together(
        shift(dkv_two, -1), over_wsh(first_half), swap(to_x, "x"), swap(to_y, "y")
    )
    passing = (dkv_one + passed_one.astype(F32)).astype(BF)
    passed, *got_rows = together(shift(passing, -1), *[over(total) for total in sums[1:]])
    if halves == 2:
        second_half = pack(place, side, info, sums[1], got_rows[0], part)
        passed = after(passed, *second_half)
        slot_grads = slot_grads + over_wsh(second_half)
    grad_low, grad_high, attn_grads, gain_part = project_back(
        grad_q_low, dkv_zero, passed, packed_all, attn_w, cosine, sine, grad_w_out, seg_len
    )

    hops = [("x", 1), ("z", 0), *[("z", k) for k in range(1, lax.axis_size("z").bit_length() - 1)], ("y", 1), ("c", 1)]

    def hop(value, at):
        axis, k = hops[at]
        if axis != "z":
            return value + swap(value, axis)
        return value + lax.ppermute(value, "z", [(i, i ^ (1 << k)) for i in range(lax.axis_size("z"))])

    gain_grad = jnp.stack([jnp.sum(gain_part, axis=0) / gains[0], gain_grad_two])
    grad_got = swap(grad_high, "c")
    grad_corner = corner_rows(grad_low, grad_got)
    attn_sum, grad_x, grad_y, gain_grad, slot_grads = together(
        lax.psum_scatter(attn_grads, "z", scatter_dimension=0, tiled=True),
        swap(grad_corner[:half], "y"),
        swap(grad_corner[half:], "x"),
        hop(after(gain_grad, grad_corner), 0),
        slot_grads,
    )

    attn_rows = jnp.broadcast_to(
        attn_sum.reshape(2, 1, row_count, 3 * part), (2, 4, row_count, 3 * part)
    ).reshape(8, row_count, 3 * part)
    to_x, to_y = edge_rows(grad_low, grad_got, grad_x, grad_y)
    attn_back, last_x, last_y, gain_grad, new = together(
        lax.all_to_all(attn_rows, PLANE, split_axis=0, concat_axis=0, tiled=True),
        swap(to_x, "x"),
        swap(to_y, "y"),
        hop(hop(gain_grad, 1), 2),
        update(info, rates, slot_grads, masters, first_moments, second_moments),
    )
    for at in range(3, len(hops)):
        gain_grad = hop(gain_grad, at)

    def own(kept, got, *rest):
        total = kept[:seg_len].astype(F32) + got[:seg_len].astype(F32)
        return total + sum(value.astype(F32) for value in rest)

    output = (resid_one + own(moe[0], moe_got, out_x, out_y)).astype(BF)
    grad_in_one = own(grad_low, grad_got, last_x, last_y)
    input_grad = grad_resid + norm_back(tokens_f, scale_one, gains[0], grad_in_one)
    rank = jnp.cumsum(local_ok.astype(jnp.int32)) - 1
    count = rank[5] + 1
    wanted = jnp.minimum(jnp.arange(6, dtype=jnp.int32), count - 1)
    chosen = local_ok[None, :] & (rank[None, :] == wanted[:, None])
    attn_slots = jnp.sum(jnp.where(chosen, local_at[None, :], 0), axis=1)
    attn_held = jnp.sum(jnp.where(chosen, jnp.arange(6, dtype=jnp.int32)[None, :] + 1, 0), axis=1) - 1
    attn_rates = jnp.take(rates, attn_slots)
    new_masters, new_first, new_second = update_attn(
        attn_slots, attn_held, attn_rates, attn_back, masters, first_moments, second_moments, new
    )
    new_gains, new_gain_first, new_gain_second = adamw(
        norm_gains, gain_first, gain_second, gain_grad, GAIN_RATE, 0.0
    )
    return (
        output[None],
        input_grad[None],
        new_masters,
        new_first,
        new_second,
        new_gains,
        new_gain_first,
        new_gain_second,
    )


def solution(mesh):
    ctx, wsh = mesh.devices.shape
    fine = Mesh(mesh.devices.reshape(ctx // 2, 2, wsh // 2, 2), ("z", "x", "y", "c"))
    rows = P(WSH, ("z", "x"), None)
    marks = P(WSH, ("z", "x"))
    return jax.shard_map(
        shards,
        mesh=fine,
        in_specs=(rows, marks, rows, rows, rows, P(), rows, rows, rows, P(), P(), P()),
        out_specs=(rows, rows, rows, rows, rows, P(), P(), P()),
        check_vma=False,
    )
```

```python
import jax
import jax.numpy as jnp
import numpy as np
from jax import lax
from jax.experimental import pallas as pl
from jax.experimental.pallas import tpu as pltpu
from jax.sharding import Mesh
from jax.sharding import PartitionSpec as P

QH = 16
KVH = 8
HD = 64
STEP = 7

EPS_NORM = 1e-05
THETA = 10000.0
BETA_ONE = 0.5
BETA_TWO = 0.6
ADAM_EPS = 1e-08
DECAY = 0.1
GAIN_RATE = 0.3
NEG_BIG = -1e30
PLANE = ("x", "y", "c")
WSH = ("y", "c")
BF = jnp.bfloat16
F32 = jnp.float32


def swap(value, axis):
    return lax.ppermute(value, axis, [(0, 1), (1, 0)])


def shift(value, by):
    count = lax.axis_size("z")
    pairs = [(i, i + by) for i in range(count) if 0 <= i + by < count]
    return lax.ppermute(value, "z", pairs)


def took(us):
    return pl.CostEstimate(flops=int(us * 1e9), bytes_accessed=2**20, transcendentals=0)


def vmem(mib):
    return pltpu.CompilerParams(vmem_limit_bytes=mib * 2**20)


def whole(shape):
    return pl.BlockSpec(shape, lambda *_: (0,) * len(shape))


def half_specs(block, width, rows, at):
    low = pl.BlockSpec((block, width), lambda *g: (jnp.minimum(at(*g), rows // 2 // block - 1), 0))
    high = pl.BlockSpec((block, width), lambda *g: (jnp.maximum(at(*g) - rows // 2 // block, 0), 0))
    return [low, high]


def together(*values):
    return lax.optimization_barrier(values)


def after(value, *first):
    return lax.optimization_barrier((value, *first))[0]


def stack_kernel(*refs):
    at = 0
    for ref in refs[:-1]:
        refs[-1][at : at + ref.shape[0]] = ref[...]
        at += ref.shape[0]


def stack(pieces):
    shape = (sum(piece.shape[0] for piece in pieces), pieces[0].shape[1])
    return pl.pallas_call(
        stack_kernel,
        grid=(1,),
        in_specs=[whole(piece.shape) for piece in pieces],
        out_specs=whole(shape),
        out_shape=jax.ShapeDtypeStruct(shape, BF),
        cost_estimate=took(2),
        compiler_params=vmem(32),
    )(*pieces)


def plane_gather(rows, wait=lambda value: value, last=lambda value: value):
    half = rows.shape[0] // 2
    over_x = swap(rows, "x")
    over_y = swap(rows, "y")
    first, second = wait((over_x[:half], over_y[half:]))
    corner_top = swap(first, "y")
    corner_low = swap(second, "x")
    mine = stack([rows, over_x, over_y, corner_top, corner_low])
    return mine, swap(last(mine), "c")


def corner_kernel(kept_ref, got_ref, out_ref):
    out_ref[...] = (kept_ref[...].astype(F32) + got_ref[...].astype(F32)).astype(BF)


def corner_rows(kept, got):
    rows, width = kept.shape
    spec = pl.BlockSpec((rows // 4, width), lambda i: (3, 0))
    return pl.pallas_call(
        corner_kernel,
        grid=(1,),
        in_specs=[spec, spec],
        out_specs=whole((rows // 4, width)),
        out_shape=jax.ShapeDtypeStruct((rows // 4, width), BF),
        cost_estimate=took(1),
        compiler_params=vmem(32),
    )(kept, got)


def edge_kernel(kx_ref, gx_ref, ky_ref, gy_ref, fx_ref, fy_ref, x_ref, y_ref):
    half = fx_ref.shape[0]
    for kept, got, extra, out_ref, at in ((kx_ref, gx_ref, fx_ref, x_ref, 0), (ky_ref, gy_ref, fy_ref, y_ref, 1)):
        total = kept[...].astype(F32) + got[...].astype(F32)
        mine, rest = slice(at * half, (at + 1) * half), slice((1 - at) * half, (2 - at) * half)
        out_ref[mine] = (total[mine] + extra[...].astype(F32)).astype(BF)
        out_ref[rest] = total[rest].astype(BF)


def edge_rows(kept, got, for_x, for_y):
    rows, width = kept.shape
    step = rows // 4
    one, two = (pl.BlockSpec((step, width), lambda i, b=b: (b, 0)) for b in (1, 2))
    half = whole((step // 2, width))
    return pl.pallas_call(
        edge_kernel,
        grid=(1,),
        in_specs=[one, one, two, two, half, half],
        out_specs=[whole((step, width))] * 2,
        out_shape=[jax.ShapeDtypeStruct((step, width), BF)] * 2,
        cost_estimate=took(2),
        compiler_params=vmem(32),
    )(kept, got, kept, got, for_x, for_y)


def plane_reduce(kept, sent, waits=(None, None, None)):
    hold = [wait or (lambda value: value) for wait in waits]
    step = kept.shape[0] // 4
    half = step // 2
    got = swap(hold[0](sent), "c")
    corner = hold[1](corner_rows(kept, got))
    for_x = swap(corner[:half], "y")
    for_y = swap(corner[half:], "x")
    to_x, to_y = hold[2](edge_rows(kept, got, for_x, for_y))
    own = kept[:step].astype(F32) + got[:step].astype(F32)
    return own + swap(to_x, "x").astype(F32) + swap(to_y, "y").astype(F32)


def norm_scale(values):
    return lax.rsqrt(jnp.mean(values * values, axis=-1, keepdims=True) + EPS_NORM)


def norm_back(values, scale_row, gain_row, grad_out):
    weighted = grad_out * gain_row
    grad_in = scale_row * weighted - values * scale_row**3 * jnp.mean(
        values * weighted, axis=-1, keepdims=True
    )
    return grad_in


def kind_rates(width, hidden):
    base_rate = 0.5 * width ** (-0.5)
    return [
        base_rate,
        base_rate,
        base_rate,
        2.0 * (2 * hidden) ** (-0.5),
        base_rate,
        base_rate,
        3.0 * hidden ** (-0.5),
        base_rate,
    ]


def adamw(weight, first, second, grad, rate, decay):
    first_new = BETA_ONE * first + (1.0 - BETA_ONE) * grad
    second_new = BETA_TWO * second + (1.0 - BETA_TWO) * grad * grad
    first_hat = first_new / (1.0 - BETA_ONE**STEP)
    second_hat = second_new / (1.0 - BETA_TWO**STEP)
    weight_new = weight - rate * (first_hat / (jnp.sqrt(second_hat) + ADAM_EPS) + decay * weight)
    return (weight_new, first_new, second_new)


def dot_nn(left, right):
    return lax.dot_general(left, right, (((1,), (0,)), ((), ())), preferred_element_type=F32)


def dot_nt(left, right):
    return lax.dot_general(left, right, (((1,), (1,)), ((), ())), preferred_element_type=F32)


def dot_tn(left, right):
    return lax.dot_general(left, right, (((0,), (0,)), ((), ())), preferred_element_type=F32)


def turn(value, lane):
    low = (lane % HD) < (HD // 2)
    return jnp.where(
        low, -pltpu.roll(value, 2 * HD - HD // 2, 1), pltpu.roll(value, HD // 2, 1)
    )

def choose(early, low_ref, high_ref):
    return jnp.where(early, low_ref[...], high_ref[...])


def attn_send_kernel(at_ref, ok_ref, *refs):
    mats, out_ref = refs[:6], refs[6]

    def read(m):
        return jnp.where(ok_ref[m] == 1, mats[m][0], 0.0).astype(BF)

    part = out_ref.shape[3]
    for side in range(2):
        for kind, m in ((0, side), (2, 4 + side)):
            mat = read(m)
            for j in range(4):
                out_ref[4 * side + j, kind] = mat[:, j * part : (j + 1) * part]
    keys, values = read(2), read(3)
    for h in range(8):
        both = (keys[:, h * HD : (h + 1) * HD], values[:, h * HD : (h + 1) * HD])
        out_ref[h, 1] = jnp.concatenate(both, axis=1)


def attn_send(masters, at, ok):
    _, rows, hidden = masters.shape
    part = hidden // 4
    specs = [pl.BlockSpec((1, rows, hidden), lambda i, at, ok, m=m: (at[m], 0, 0)) for m in range(6)]
    return pl.pallas_call(
        attn_send_kernel,
        grid_spec=pltpu.PrefetchScalarGridSpec(
            num_scalar_prefetch=2,
            grid=(1,),
            in_specs=specs,
            out_specs=pl.BlockSpec((8, 3, rows, part), lambda i, at, ok: (0, 0, 0, 0)),
        ),
        out_shape=jax.ShapeDtypeStruct((8, 3, rows, part), BF),
        cost_estimate=took(3),
        compiler_params=vmem(62),
    )(at, ok, *([masters] * 6))


def bulk_send_kernel(info_ref, in_ref, *outs):
    part = outs[0].shape[2]
    for d, out_ref in enumerate(outs):
        start = pl.multiple_of((info_ref[1] ^ d) * part, part)
        out_ref[...] = in_ref[:, :, pl.ds(start, part)].astype(BF)


def bulk_send(info, masters):
    slots, rows, hidden = masters.shape
    step, part = 5 if slots % 5 == 0 else 1, hidden // 4
    return pl.pallas_call(
        bulk_send_kernel,
        grid=(slots // step,),
        in_specs=[
            pl.BlockSpec(memory_space=pltpu.SMEM),
            pl.BlockSpec((step, rows, hidden), lambda i: (i, 0, 0)),
        ],
        out_specs=[pl.BlockSpec((step, rows, part), lambda i: (i, 0, 0))] * 4,
        out_shape=[jax.ShapeDtypeStruct((slots, rows, part), BF)] * 4,
        cost_estimate=took(4),
        compiler_params=vmem(62),
    )(info, masters)


def over_wsh(arrays):
    across = [(i, i ^ 3) for i in range(4)]
    return [arrays[0], swap(arrays[1], "c"), swap(arrays[2], "y"), lax.ppermute(arrays[3], WSH, across)]


def pick_kernel(at_ref, *refs):
    slots, outs, held = refs[:4], refs[4:-1], refs[-1]
    count = slots[0].shape[0]
    part = held.shape[2]
    for d in range(4):
        held[d * count : (d + 1) * count] = slots[d][...]
    for i, out_ref in enumerate(outs):
        number = out_ref.shape[1] // part
        for k in range(number):
            out_ref[:, k * part : (k + 1) * part] = held[at_ref[i * number + k]]


def pick(places, slots, parts):
    count, rows, part = slots[0].shape
    wide = (rows, places.shape[0] // parts * part)
    return pl.pallas_call(
        pick_kernel,
        grid_spec=pltpu.PrefetchScalarGridSpec(
            num_scalar_prefetch=1,
            grid=(1,),
            in_specs=[pl.BlockSpec((count, rows, part), lambda i, a: (0, 0, 0))] * 4,
            out_specs=[pl.BlockSpec(wide, lambda i, a: (0, 0))] * parts,
            scratch_shapes=[pltpu.VMEM((4 * count, rows, part), BF)],
        ),
        out_shape=[jax.ShapeDtypeStruct(wide, BF)] * parts,
        cost_estimate=took(3),
        compiler_params=vmem(62),
    )(places, *slots)


def join_kernel(info_ref, *refs):
    count = len(refs) // 2
    keeps, gots, out_ref = refs[:count], refs[count:-1], refs[-1]
    rows, wide = keeps[0].shape
    first = info_ref[0] == 0
    for i in range(count):
        keep, got, lanes = keeps[i][...], gots[i][...], slice(i * wide, (i + 1) * wide)
        out_ref[:rows, lanes] = jnp.where(first, keep, got)
        out_ref[rows:, lanes] = jnp.where(first, got, keep)


def join(info, keeps, gots):
    rows, wide = keeps[0].shape
    shape = (2 * rows, wide * len(keeps))
    return pl.pallas_call(
        join_kernel,
        grid=(1,),
        in_specs=[pl.BlockSpec(memory_space=pltpu.SMEM)] + [whole((rows, wide))] * (2 * len(keeps)),
        out_specs=whole(shape),
        out_shape=jax.ShapeDtypeStruct(shape, BF),
        cost_estimate=took(1.5),
        compiler_params=vmem(32),
    )(info, *keeps, *gots)


def pack_kernel(place_ref, side_ref, info_ref, *refs):
    totals, gots, outs, held = refs[:2], refs[2:4], refs[4:-1], refs[-1]
    count, rows, part = outs[0].shape
    full = gots[0].shape[0]
    mine = pl.ds(pl.multiple_of(info_ref[0] * full, full), full)
    for c in range(2):
        held[c * full : (c + 1) * full] = totals[c][mine]
        held[(2 + c) * full : (3 + c) * full] = gots[c][...]
    held[4 * full :] = jnp.zeros((full, held.shape[1]), BF)
    for d in range(4):

        def one(j, carry):
            s = (info_ref[1] ^ d) * count + j
            lanes = pl.ds(pl.multiple_of(place_ref[s] * part, part), part)
            for h, out_ref in enumerate(outs[d::4]):
                start = pl.multiple_of(side_ref[s] * full + h * rows, rows)
                out_ref[j] = held[pl.ds(start, rows), lanes]
            return carry

        lax.fori_loop(0, count, one, 0)


def pack(place, side, info, totals, gots, part, halves):
    rows, wide = gots[0].shape
    shape = (place.shape[0] // 4, rows // halves, part)
    outs = pl.pallas_call(
        pack_kernel,
        grid_spec=pltpu.PrefetchScalarGridSpec(
            num_scalar_prefetch=3,
            grid=(1,),
            in_specs=[
                *[pl.BlockSpec((2 * rows, wide), lambda i, a, b, c: (0, 0))] * 2,
                *[pl.BlockSpec((rows, wide), lambda i, a, b, c: (0, 0))] * 2,
            ],
            out_specs=[pl.BlockSpec(shape, lambda i, a, b, c: (0, 0, 0))] * (4 * halves),
            scratch_shapes=[pltpu.VMEM((5 * rows, wide), BF)],
        ),
        out_shape=[jax.ShapeDtypeStruct(shape, BF)] * (4 * halves),
        cost_estimate=took(3),
        compiler_params=vmem(32),
    )(place, side, info, *totals, *gots)
    return [outs[4 * h : 4 * h + 4] for h in range(halves)]


def update_kernel(info_ref, rate_ref, *refs):
    grads, (w_ref, m_ref, v_ref, w_out, m_out, v_out) = refs[:-6], refs[-6:]
    part = grads[0].shape[2]
    rows = grads[0].shape[1]

    def one(s, carry):
        rate = rate_ref[pl.program_id(0) * w_ref.shape[0] + s]
        for i, grad_ref in enumerate(grads):
            lanes = pl.ds(pl.multiple_of((info_ref[1] ^ (i % 4)) * part, part), part)
            at = slice((i // 4) * rows, (i // 4 + 1) * rows)
            w_out[s, at, lanes], m_out[s, at, lanes], v_out[s, at, lanes] = adamw(
                w_ref[s, at, lanes],
                m_ref[s, at, lanes],
                v_ref[s, at, lanes],
                grad_ref[s].astype(F32),
                rate,
                DECAY,
            )
        return carry

    lax.fori_loop(0, w_ref.shape[0], one, 0)


def update(info, rates, grads, masters, first, second):
    slots, rows, hidden = masters.shape
    step = 4 if slots % 4 == 0 else 1
    smem = pl.BlockSpec(memory_space=pltpu.SMEM)
    spec = pl.BlockSpec((step, rows, hidden), lambda i: (i, 0, 0))
    grad_spec = pl.BlockSpec((step, *grads[0].shape[1:]), lambda i: (i, 0, 0))
    return pl.pallas_call(
        update_kernel,
        grid=(slots // step,),
        in_specs=[smem, smem] + [grad_spec] * len(grads) + [spec] * 3,
        out_specs=[spec] * 3,
        out_shape=[jax.ShapeDtypeStruct(masters.shape, F32)] * 3,
        cost_estimate=took(6),
        compiler_params=vmem(62),
    )(info, rates, *grads, masters, first, second)


def update_attn_kernel(slot_ref, held_ref, rate_ref, attn_ref, *refs):
    (w_ref, m_ref, v_ref), olds, news = refs[:3], refs[3:6], refs[6:]
    step = pl.program_id(0)
    held = held_ref[step]
    rate = rate_ref[step]
    part = w_ref.shape[2] // 4

    def write(j, grad):
        lanes = slice(j * part, (j + 1) * part)
        results = adamw(
            w_ref[0, :, lanes], m_ref[0, :, lanes], v_ref[0, :, lanes], grad.astype(F32), rate, DECAY
        )
        for new_ref, result in zip(news, results):
            new_ref[0, :, lanes] = result

    @pl.when(held < 0)
    def _():
        for old_ref, new_ref in zip(olds, news):
            new_ref[...] = old_ref[...]

    for m, side, kind in ((0, 0, 0), (1, 1, 0), (4, 0, 2), (5, 1, 2)):

        @pl.when(held == m)
        def _():
            for j in range(4):
                write(j, attn_ref[4 * side + j, :, kind * part : (kind + 1) * part])

    for m, start in ((2, part), (3, part + HD)):

        @pl.when(held == m)
        def _():
            for j in range(4):
                pieces = [attn_ref[2 * j + i, :, start : start + HD] for i in range(2)]
                write(j, jnp.concatenate(pieces, axis=1))


def update_attn(slots, held, rates, attn_back, masters, first, second, new):
    _, rows, hidden = masters.shape
    spec = pl.BlockSpec((1, rows, hidden), lambda i, at, held: (at[i], 0, 0))
    return pl.pallas_call(
        update_attn_kernel,
        grid_spec=pltpu.PrefetchScalarGridSpec(
            num_scalar_prefetch=2,
            grid=(slots.shape[0],),
            in_specs=[
                pl.BlockSpec(memory_space=pltpu.SMEM),
                pl.BlockSpec(attn_back.shape, lambda i, at, held: (0, 0, 0)),
                *[spec] * 6,
            ],
            out_specs=[spec] * 3,
        ),
        out_shape=[jax.ShapeDtypeStruct(masters.shape, F32)] * 3,
        input_output_aliases={7: 0, 8: 1, 9: 2},
        cost_estimate=took(5),
        compiler_params=vmem(62),
    )(slots, held, rates, attn_back, masters, first, second, *new)


def project_kernel(low_ref, high_ref, w_ref, cos_ref, sin_ref, q_ref, kv_ref):
    early = pl.program_id(0) < pl.num_programs(0) // 2
    both = dot_nn(choose(early, low_ref, high_ref), w_ref[...])
    cosine = cos_ref[0]
    sine = sin_ref[0]
    lane = lax.broadcasted_iota(jnp.int32, cosine.shape, 1)
    query = both[:, : 2 * HD]
    pair = both[:, 2 * HD :]
    q_ref[...] = (query * cosine + turn(query, lane) * sine).astype(BF)
    turned = pair * cosine + turn(pair, lane) * sine
    kv_ref[...] = jnp.where(lane < HD, turned, pair).astype(BF)


def project(x_low, x_high, weights, cosine, sine, block):
    rows = 2 * x_low.shape[0]
    width = weights.shape[0]
    table = pl.BlockSpec((1, block, 2 * HD), lambda i: (i % 2, 0, 0))
    return pl.pallas_call(
        project_kernel,
        grid=(rows // block,),
        in_specs=[
            *half_specs(block, width, rows, lambda i: i),
            pl.BlockSpec((width, 4 * HD), lambda i: (0, 0)),
            table,
            table,
        ],
        out_specs=[pl.BlockSpec((block, 2 * HD), lambda i: (i, 0))] * 2,
        out_shape=[jax.ShapeDtypeStruct((rows, 2 * HD), BF)] * 2,
        cost_estimate=took(6),
        compiler_params=vmem(32),
    )(x_low, x_high, weights, cosine, sine)


def head_rows(rows, head, lane, high):
    if (head == 1) != high:
        rows = pltpu.roll(rows, HD, 1)
    keep = (lane >= HD) if high else (lane < HD)
    return jnp.where(keep, rows, jnp.zeros_like(rows))


def masks(info_ref, qseg_ref, kseg, block, span):
    flip = info_ref[0]
    chunk = pl.program_id(1)
    key_at = lax.broadcasted_iota(jnp.int32, (span, 1), 0)
    query_at = lax.broadcasted_iota(jnp.int32, (1, block), 1)
    swapped = jnp.where(flip == 1, key_at ^ block, key_at)
    key_pos = jnp.where(key_at < 2 * block, swapped, -1)
    query_pos = query_at + block * jnp.where(flip == 1, 1 - chunk, chunk)
    return (key_pos <= query_pos) & (kseg == qseg_ref[0])


def load_pairs(refs, tails, kv_all, kv_turned, marks, kseg, reach):
    third = kv_all.shape[0] // 3
    for i, (ref, tail) in enumerate(zip(refs, tails)):
        kv_all[i * third : (i + 1) * third] = ref[...]
        marks[i] = tail[...].astype(F32).reshape(marks.shape[1:])
        columns = marks[i, pl.program_id(0)].T
        for j in range(third // 128):
            at = i * third + j * 128
            kseg[at : at + 128] = columns[:, j : j + 1]
    kv_turned[...] = kv_all[...].T
    seq = pl.program_id(0)
    least = jnp.min(marks[0, seq][: third // 128])
    far = jnp.max(marks[2, seq]) >= least
    near = jnp.max(marks[1, seq]) >= least
    reach[0] = jnp.where(far, 3, jnp.where(near, 2, 1)).astype(jnp.int32)


def attend_kernel(info_ref, q_ref, k0_ref, k1_ref, k2_ref, t0_ref, t1_ref, t2_ref, qseg_ref,
                  w_ref, mix_ref, stat_ref, low_ref, high_ref, kv_all, kv_turned, marks, kseg, reach):
    block = q_ref.shape[0]
    span = kv_all.shape[0]

    @pl.when(pl.program_id(1) == 0)
    def _():
        load_pairs((k0_ref, k1_ref, k2_ref), (t0_ref, t1_ref, t2_ref), kv_all, kv_turned, marks, kseg, reach)

    lane = lax.broadcasted_iota(jnp.int32, (block, 2 * HD), 1)
    query = q_ref[...] * jnp.asarray(HD**-0.5, BF)

    def attend_to(keys):
        allowed = masks(info_ref, qseg_ref, kseg[:keys], block, keys)
        mixed = []
        for head in range(2):
            scores = dot_nt(kv_all[:keys], head_rows(query, head, lane, False))
            scores = jnp.where(allowed, scores, NEG_BIG)
            top = jnp.max(scores, axis=0, keepdims=True)
            powers = jnp.exp(scores - top)
            total = jnp.sum(powers, axis=0, keepdims=True)
            stat_ref[0, 0, head : head + 1, :] = top + jnp.log(total)
            probs = (powers * (1.0 / total)).astype(BF)
            mixed.append(dot_nn(kv_turned[:, :keys], probs)[HD:])
        mix_ref[...] = jnp.concatenate(mixed, axis=0).T.astype(BF)

    for blocks in range(1, 4):

        @pl.when(reach[0] == blocks)
        def _():
            attend_to(blocks * span // 3)

    mix = mix_ref[...]
    out = dot_nt(mix, w_ref[...]).astype(BF)
    early = pl.program_id(0) < pl.num_programs(0) // 2

    @pl.when(early)
    def _():
        low_ref[...] = out

    @pl.when(jnp.logical_not(early))
    def _():
        high_ref[...] = out


def attend(info, query, kv, qseg, weights, block):
    rows = query.shape[0]
    seqs = rows // (2 * block)
    width = weights.shape[0]
    row_spec = pl.BlockSpec((block, 2 * HD), lambda s, i: (2 * s + i, 0))
    kv_spec = pl.BlockSpec((2 * block, 2 * HD), lambda s, i: (s, 0))
    tail_spec = pl.BlockSpec((8 * seqs, 2 * HD), lambda s, i: (rows // (8 * seqs), 0))
    return pl.pallas_call(
        attend_kernel,
        grid=(seqs, 2),
        in_specs=[
            pl.BlockSpec(memory_space=pltpu.SMEM),
            row_spec,
            kv_spec,
            kv_spec,
            kv_spec,
            tail_spec,
            tail_spec,
            tail_spec,
            pl.BlockSpec((1, 1, block), lambda s, i: (2 * s + i, 0, 0)),
            pl.BlockSpec((width, 2 * HD), lambda s, i: (0, 2)),
        ],
        out_specs=[
            row_spec,
            pl.BlockSpec((1, 1, 2, block), lambda s, i: (s, i, 0, 0)),
            *half_specs(block, width, rows, lambda s, i: 2 * s + i),
        ],
        out_shape=[
            jax.ShapeDtypeStruct((rows, 2 * HD), BF),
            jax.ShapeDtypeStruct((seqs, 2, 2, block), F32),
            *[jax.ShapeDtypeStruct((rows // 2, width), BF)] * 2,
        ],
        scratch_shapes=[
            pltpu.VMEM((6 * block, 2 * HD), BF),
            pltpu.VMEM((2 * HD, 6 * block), BF),
            pltpu.VMEM((3, seqs, 8, 128), F32),
            pltpu.VMEM((6 * block, 1), F32),
            pltpu.SMEM((1,), jnp.int32),
        ],
        cost_estimate=took(24),
        compiler_params=vmem(62),
    )(info, query, *kv, *kv, qseg, weights)


def attend_back_kernel(info_ref, q_ref, k0_ref, k1_ref, k2_ref, t0_ref, t1_ref, t2_ref, qseg_ref,
                       stat_ref, dy_low, dy_high, mix_ref, w_ref, cos_ref, sin_ref,
                       dq_ref, dk0_ref, dk1_ref, dk2_ref, dw_ref,
                       kv_all, kv_turned, marks, kseg, reach, sums, dw_sum, turned_sum):
    block = q_ref.shape[0]
    span = kv_all.shape[0]
    third = span // 3
    seq = pl.program_id(0)
    chunk = pl.program_id(1)

    @pl.when((chunk == 0) & (seq == 0))
    def _():
        dw_sum[...] = jnp.zeros_like(dw_sum)

    @pl.when(chunk == 0)
    def _():
        sums[...] = jnp.zeros_like(sums)
        load_pairs((k0_ref, k1_ref, k2_ref), (t0_ref, t1_ref, t2_ref), kv_all, kv_turned, marks, kseg, reach)

    lane = lax.broadcasted_iota(jnp.int32, (block, 2 * HD), 1)
    query = q_ref[...] * jnp.asarray(HD**-0.5, BF)
    grad_rows = choose(seq < pl.num_programs(0) // 2, dy_low, dy_high)
    dw_sum[...] += dot_tn(mix_ref[...], grad_rows)
    grad_mix = dot_nn(grad_rows, w_ref[...]).astype(BF)

    def attend_to(keys):
        allowed = masks(info_ref, qseg_ref, kseg[:keys], block, keys)
        grad_query = []
        for head in range(2):
            q_low = head_rows(query, head, lane, False)
            g_high = head_rows(grad_mix, head, lane, True)
            scores = dot_nt(kv_all[:keys], q_low)
            stat = stat_ref[0, 0, head : head + 1, :]
            probs = jnp.where(allowed, jnp.exp(scores - stat), 0.0)
            grad_probs = dot_nt(kv_all[:keys], g_high)
            delta = jnp.sum(probs * grad_probs, axis=0, keepdims=True)
            grad_scores = (probs * (grad_probs - delta)).astype(BF)
            sums[:keys] += dot_nn(grad_scores, q_low) + dot_nn(probs.astype(BF), g_high)
            grad_query.append(dot_nn(kv_turned[:, :keys], grad_scores)[:HD])
        turned_sum[...] = jnp.concatenate(grad_query, axis=0)

    for blocks in range(1, 4):

        @pl.when(reach[0] == blocks)
        def _():
            attend_to(blocks * span // 3)

    grad_q = turned_sum[...].T * HD**-0.5
    dq_ref[...] = (grad_q * cos_ref[0] - turn(grad_q * sin_ref[0], lane)).astype(BF)

    @pl.when(chunk == 1)
    def _():
        dk0_ref[...] = sums[:third]
        dk1_ref[...] = sums[third : 2 * third]
        dk2_ref[...] = sums[2 * third :].astype(BF)

    @pl.when((chunk == 1) & (seq == pl.num_programs(0) - 1))
    def _():
        dw_ref[...] = dw_sum[...].T.astype(BF)


def attend_back(info, query, kv, qseg, stat, grad_rows, mix, weights, cosine, sine, block):
    rows = query.shape[0]
    seqs = rows // (2 * block)
    width = weights.shape[0]
    row_spec = pl.BlockSpec((block, 2 * HD), lambda s, i: (2 * s + i, 0))
    kv_spec = pl.BlockSpec((2 * block, 2 * HD), lambda s, i: (s, 0))
    tail_spec = pl.BlockSpec((8 * seqs, 2 * HD), lambda s, i: (rows // (8 * seqs), 0))
    table = pl.BlockSpec((1, block, 2 * HD), lambda s, i: (i, 0, 0))
    return pl.pallas_call(
        attend_back_kernel,
        grid=(seqs, 2),
        in_specs=[
            pl.BlockSpec(memory_space=pltpu.SMEM),
            row_spec,
            kv_spec,
            kv_spec,
            kv_spec,
            tail_spec,
            tail_spec,
            tail_spec,
            pl.BlockSpec((1, 1, block), lambda s, i: (2 * s + i, 0, 0)),
            pl.BlockSpec((1, 1, 2, block), lambda s, i: (s, i, 0, 0)),
            *half_specs(block, width, rows, lambda s, i: 2 * s + i),
            row_spec,
            pl.BlockSpec((width, 2 * HD), lambda s, i: (0, 2)),
            table,
            table,
        ],
        out_specs=[row_spec, kv_spec, kv_spec, kv_spec, whole((width, 2 * HD))],
        out_shape=[
            jax.ShapeDtypeStruct((rows, 2 * HD), BF),
            jax.ShapeDtypeStruct((rows, 2 * HD), F32),
            jax.ShapeDtypeStruct((rows, 2 * HD), F32),
            jax.ShapeDtypeStruct((rows, 2 * HD), BF),
            jax.ShapeDtypeStruct((width, 2 * HD), BF),
        ],
        scratch_shapes=[
            pltpu.VMEM((6 * block, 2 * HD), BF),
            pltpu.VMEM((2 * HD, 6 * block), BF),
            pltpu.VMEM((3, seqs, 8, 128), F32),
            pltpu.VMEM((6 * block, 1), F32),
            pltpu.SMEM((1,), jnp.int32),
            pltpu.VMEM((6 * block, 2 * HD), F32),
            pltpu.VMEM((2 * HD, width), F32),
            pltpu.VMEM((2 * HD, block), F32),
        ],
        cost_estimate=took(12),
        compiler_params=vmem(62),
    )(info, query, *kv, *kv, qseg, stat, *grad_rows, mix, weights, cosine, sine)


def project_back_kernel(dq_ref, a_ref, b_ref, x_low, x_high, w_ref, cos_ref, sin_ref, dout_ref,
                        low_ref, high_ref, dw_ref, gain_ref, dw_sum):
    step = pl.program_id(0)

    @pl.when(step == 0)
    def _():
        dw_sum[...] = jnp.zeros_like(dw_sum)
        gain_ref[...] = jnp.zeros_like(gain_ref)

    grad = a_ref[...] + b_ref[...].astype(F32)
    lane = lax.broadcasted_iota(jnp.int32, grad.shape, 1)
    turned = grad * cos_ref[0] - turn(grad * sin_ref[0], lane)
    pair = jnp.where(lane < HD, turned, grad).astype(BF)
    both = jnp.concatenate([dq_ref[...], pair], axis=1)
    grad_in = dot_nt(both, w_ref[...])
    early = step < pl.num_programs(0) // 2

    @pl.when(early)
    def _():
        low_ref[...] = grad_in.astype(BF)

    @pl.when(jnp.logical_not(early))
    def _():
        high_ref[...] = grad_in.astype(BF)

    x_rows = choose(early, x_low, x_high)
    dw_sum[...] += dot_tn(both, x_rows)
    weighted = grad_in * x_rows.astype(F32)
    gain_ref[...] += jnp.sum(weighted.reshape(-1, 8, weighted.shape[1]), axis=0)

    @pl.when(step == pl.num_programs(0) - 1)
    def _():
        dw_ref[:, : 4 * HD] = dw_sum[...].T.astype(BF)
        dw_ref[:, 4 * HD :] = dout_ref[...]


def project_back(grad_q, here, arrived, x_rows, weights, cosine, sine, grad_out, block):
    rows = here.shape[0]
    width, cols = weights.shape[0], 4 * HD
    spec = pl.BlockSpec((block, 2 * HD), lambda i: (i, 0))
    table = pl.BlockSpec((1, block, 2 * HD), lambda i: (i % 2, 0, 0))
    return pl.pallas_call(
        project_back_kernel,
        grid=(rows // block,),
        in_specs=[
            *[spec] * 3,
            *half_specs(block, width, rows, lambda i: i),
            pl.BlockSpec((width, cols), lambda i: (0, 0)),
            table,
            table,
            whole(grad_out.shape),
        ],
        out_specs=[
            *half_specs(block, width, rows, lambda i: i),
            whole((width, 6 * HD)),
            whole((8, width)),
        ],
        out_shape=[
            *[jax.ShapeDtypeStruct((rows // 2, width), BF)] * 2,
            jax.ShapeDtypeStruct((width, 6 * HD), BF),
            jax.ShapeDtypeStruct((8, width), F32),
        ],
        scratch_shapes=[pltpu.VMEM((cols, width), F32)],
        cost_estimate=took(10),
        compiler_params=vmem(62),
    )(grad_q, here, arrived, *x_rows, weights, cosine, sine, grad_out)


def expert_kernel(part, start, more, e_low, e_high, g_low, g_high, gate_ref, w_ref, *refs):
    before, (low_ref, high_ref, hidden_ref, grads_ref), (e_ref, g_ref, act_ref, sums) = (
        refs[:more],
        refs[more : more + 4],
        refs[more + 4 :],
    )
    rows = e_ref.shape[0]
    step_id = pl.program_id(0)
    last = pl.num_programs(0) - 1
    early = step_id < pl.num_programs(0) // 2
    e_ref[...] = choose(early, e_low, e_high)
    g_ref[...] = choose(early, g_low, g_high)
    cols = w_ref.shape[1] // 3
    step = 2 * part
    lane = lax.broadcasted_iota(jnp.int32, (rows, step), 1)
    for j in range(cols // step):
        at = j * step
        first = start + 2 * j
        gate = jnp.where(lane < part, gate_ref[:, first : first + 1], gate_ref[:, first + 1 : first + 2])
        pre = dot_nn(e_ref[...], w_ref[:, at : at + step])
        up = dot_nn(e_ref[...], w_ref[:, cols + at : cols + at + step])
        grad = dot_nn(g_ref[...], w_ref[:, 2 * cols + at : 2 * cols + at + step]) * gate
        logistic = 1.0 / (1.0 + jnp.exp(-pre))
        active = pre * logistic
        act_ref[:, at : at + step] = (
            grad * up * logistic * (1.0 + pre * (1.0 - logistic))
        ).astype(BF)
        act_ref[:, cols + at : cols + at + step] = (grad * active).astype(BF)
        act_ref[:, 2 * cols + at : 2 * cols + at + step] = (active * up * gate).astype(BF)
    hidden_ref[...] = act_ref[:, 2 * cols :]
    dx = dot_nt(act_ref[:, : 2 * cols], w_ref[:, : 2 * cols])
    if more:
        dx = dx + choose(early, *before).astype(F32)

    @pl.when(early)
    def _():
        low_ref[...] = dx.astype(BF)

    @pl.when(jnp.logical_not(early))
    def _():
        high_ref[...] = dx.astype(BF)

    e_turned = e_ref[...].T
    g_turned = g_ref[...].T
    chunk = 2 * step

    def part_sum(at):
        left = e_turned if at < 2 * cols else g_turned
        return dot_nn(left, act_ref[:, at : at + chunk])

    @pl.when(step_id == 0)
    def _():
        for at in range(0, 3 * cols, chunk):
            sums[:, at : at + chunk] = part_sum(at)

    @pl.when((step_id > 0) & (step_id < last))
    def _():
        for at in range(0, 3 * cols, chunk):
            sums[:, at : at + chunk] += part_sum(at)

    @pl.when(step_id == last)
    def _():
        for at in range(0, 3 * cols, chunk):
            grads_ref[:, at : at + chunk] = (sums[:, at : at + chunk] + part_sum(at)).astype(BF)


def expert_rows(e_rows, g_rows, gates, weights, part, start, before, block):
    rows, width = 2 * e_rows[0].shape[0], e_rows[0].shape[1]
    wide = weights.shape[1] // 2
    once = pl.Buffered(1)
    column = 1 if before else 0
    return pl.pallas_call(
        lambda *refs: expert_kernel(part, start, len(before), *refs),
        grid=(rows // block,),
        in_specs=[
            *half_specs(block, width, rows, lambda i: i) * 2,
            pl.BlockSpec((block, gates.shape[1]), lambda i: (i, 0)),
            pl.BlockSpec((width, wide), lambda i: (0, column), pipeline_mode=once),
            *half_specs(block, width, rows, lambda i: i)[: len(before)],
        ],
        out_specs=[
            *half_specs(block, width, rows, lambda i: i),
            pl.BlockSpec((block, wide // 3), lambda i: (i, 0)),
            pl.BlockSpec((width, wide), lambda i: (0, 0), pipeline_mode=once),
        ],
        out_shape=[
            *[jax.ShapeDtypeStruct((rows // 2, width), BF)] * 2,
            jax.ShapeDtypeStruct((rows, wide // 3), BF),
            jax.ShapeDtypeStruct((width, wide), BF),
        ],
        scratch_shapes=[
            *[pltpu.VMEM((block, width), BF)] * 2,
            pltpu.VMEM((block, wide), BF),
            pltpu.VMEM((width, wide), F32),
        ],
        cost_estimate=took(0.01),
        compiler_params=vmem(62),
    )(*e_rows, *g_rows, gates, weights, *before)


def expert_out_kernel(h0_ref, h1_ref, w0_ref, w1_ref, low_ref, high_ref):
    out = (dot_nt(h0_ref[...], w0_ref[...]) + dot_nt(h1_ref[...], w1_ref[...])).astype(BF)
    early = pl.program_id(0) < pl.num_programs(0) // 2

    @pl.when(early)
    def _():
        low_ref[...] = out

    @pl.when(jnp.logical_not(early))
    def _():
        high_ref[...] = out


def expert_out(hidden, weights, block):
    rows, cols = hidden[0].shape
    width = weights.shape[0]
    return pl.pallas_call(
        expert_out_kernel,
        grid=(rows // block,),
        in_specs=[
            *[pl.BlockSpec((block, cols), lambda i: (i, 0))] * 2,
            pl.BlockSpec((width, cols), lambda i: (0, 2)),
            pl.BlockSpec((width, cols), lambda i: (0, 5)),
        ],
        out_specs=half_specs(block, width, rows, lambda i: i),
        out_shape=[jax.ShapeDtypeStruct((rows // 2, width), BF)] * 2,
        cost_estimate=took(2),
        compiler_params=vmem(62),
    )(*hidden, weights, weights)


def shards(
    tokens,
    segments,
    routes,
    gate_weights,
    cotangent,
    owners,
    masters,
    first_moments,
    second_moments,
    norm_gains,
    gain_first,
    gain_second,
):
    z_index = lax.axis_index("z")
    x_index = lax.axis_index("x")
    w_index = lax.axis_index("y") * 2 + lax.axis_index("c")
    slot_count, row_count, hidden = masters.shape
    slot_total = slot_count * 4
    seg_len = tokens.shape[1]
    width = tokens.shape[2]
    ctx_count = width // row_count
    matrix_count = owners.shape[0]
    experts = (matrix_count - 6) // 3
    group = experts // 2
    part = hidden // 4
    halves = 2 if row_count % 32 == 0 else 1
    team = group // 2
    x_even = x_index == 0
    info = jnp.stack([x_index, w_index]).astype(jnp.int32)

    slot_ids = jnp.arange(slot_total, dtype=jnp.int32)
    hits = owners[None, :] == slot_ids[:, None]
    held = jnp.sum(hits * (jnp.arange(matrix_count, dtype=jnp.int32) + 1)[None, :], axis=1) - 1

    local_at = owners[:6] - slot_count * w_index
    local_ok = (local_at >= 0) & (local_at < slot_count)
    attn_sent = attn_send(masters, jnp.clip(local_at, 0, slot_count - 1), local_ok.astype(jnp.int32))
    bulk = bulk_send(info, masters)
    attn_got = lax.all_to_all(attn_sent, PLANE, split_axis=0, concat_axis=0, tiled=True)
    attn_got, *bulk = together(attn_got, *bulk)
    attn_mine = jnp.sum(attn_got.reshape(2, 4, 3, row_count, part).astype(F32), axis=1).astype(BF)
    attn_mine = jnp.transpose(attn_mine, (0, 2, 1, 3)).reshape(2 * row_count, 3 * part)

    order = np.array(
        [
            [6 + 3 * (group * g + team * c + e) + k for c in range(2) for k in range(3) for e in range(team)]
            for g in range(2)
        ]
    )
    picks = jnp.take(owners, jnp.asarray(order))
    picks = jnp.stack([jnp.where(x_even, picks[0], picks[1]), jnp.where(x_even, picks[1], picks[0])])
    places = ((picks // slot_count) ^ w_index) * slot_count + picks % slot_count

    gains = norm_gains
    tokens_f = tokens[0].astype(F32)
    cot_low = cotangent[0]
    scale_one = norm_scale(tokens_f)
    attn_in = (tokens_f * scale_one * gains[0]).astype(BF)
    expert_ids = jnp.arange(experts, dtype=jnp.int32)
    gates = jnp.sum(
        jnp.where(routes[0][:, :, None] == expert_ids[None, None, :], gate_weights[0][:, :, None], 0.0),
        axis=1,
    )
    gates_high = gates.astype(BF)
    gates_low = (gates - gates_high.astype(F32)).astype(BF)
    marks = (segments[0] + 1).astype(BF)[:, None]
    spare = jnp.zeros((seg_len, 128 - 2 * experts - 1), BF)
    packed = jnp.concatenate([attn_in, gates_high, gates_low, marks, spare], axis=1)

    across = [(i, i ^ 3) for i in range(4)]
    half = seg_len // 2
    packed = after(packed, attn_got)
    over_x, over_y, from_y, attn_w = together(
        swap(packed, "x"),
        swap(packed, "y"),
        swap(bulk[2], "y"),
        lax.all_gather(attn_mine, "z", axis=0, tiled=True),
    )
    corner, from_c, from_corner = together(
        swap(over_y, "x"),
        swap(bulk[1], "c"),
        lax.ppermute(after(bulk[3], from_y), WSH, across),
    )
    mine = stack([packed, over_x, over_y, corner])
    other, *picked = together(
        swap(mine, "c"), *pick(places.reshape(-1), [bulk[0], from_c, from_y, from_corner], 2)
    )
    packed_all = (mine, other)
    extras = jnp.concatenate([rows[:, width:] for rows in packed_all], axis=0)
    gates_all = extras[:, :experts].astype(F32) + extras[:, experts : 2 * experts].astype(F32)
    my_gates = jnp.where(x_even, gates_all[:, :group], gates_all[:, group:])
    seqs = 4
    rows_all = seqs * 2 * seg_len
    marks_all = extras[:, 2 * experts].reshape(seqs, -1, 128)
    marks_tail = jnp.pad(marks_all, ((0, 0), (0, 8 - marks_all.shape[1]), (0, 0))).reshape(-1, 128)

    inverse = THETA ** (-(jnp.arange(HD // 2, dtype=F32) * 2.0 / HD))
    at = jnp.arange(seg_len, dtype=jnp.int32)
    first_pos = z_index * 2 * seg_len + x_index * seg_len + at
    second_pos = z_index * 2 * seg_len + (1 - x_index) * seg_len + at
    positions = jnp.stack([first_pos, second_pos])
    angles = positions.astype(F32)[:, :, None] * inverse[None, None, :]
    cosine = jnp.tile(jnp.cos(angles), (1, 1, 4))
    sine = jnp.tile(jnp.sin(angles), (1, 1, 4))

    query, kv_low = project(*packed_all, attn_w, cosine, sine, seg_len)
    kv_zero = jnp.concatenate([kv_low, marks_tail], axis=0)
    kv_one = shift(kv_zero, 1)
    joined = join(info, picked[:1], [swap(picked[1], "x")])
    expert_w = lax.all_gather(joined, "z", axis=0, tiled=True)
    kv_two = shift(after(kv_one, joined), 1)
    g_all = plane_gather(after(cot_low, joined))
    kv = (kv_zero, kv_one, kv_two)
    qseg = marks_all.astype(F32).reshape(2 * seqs, 1, seg_len)
    attn_mix, stat, out_low, out_high = attend(
        info, query, kv, qseg, attn_w, seg_len
    )
    resid_one = tokens_f + plane_reduce(out_low, out_high)
    scale_two = norm_scale(resid_one)
    expert_in = (resid_one * scale_two * gains[1]).astype(BF)
    e_all = plane_gather(expert_in)

    held, local_at, local_ok = together(*after((held, local_at, local_ok), expert_in))
    expert_of = (held - 6) // 3
    kind_of = (held - 6) % 3
    place = jnp.where(held >= 6, kind_of * team + expert_of % team, 0)
    side = jnp.where(held >= 6, 2 * ((expert_of // group) ^ x_index) + expert_of % group // team, 4)

    held_mine = lax.dynamic_slice_in_dim(held, w_index * slot_count, slot_count)
    table = jnp.asarray(np.array([7, 0, 0, 1, 2, 3, 3] + [4, 5, 6] * experts, np.int32))
    rates = jnp.take(jnp.asarray(kind_rates(width, hidden), F32), jnp.take(table, held_mine + 1))

    rank = jnp.cumsum(local_ok.astype(jnp.int32)) - 1
    count = rank[5] + 1
    wanted = jnp.minimum(jnp.arange(6, dtype=jnp.int32), count - 1)
    chosen = local_ok[None, :] & (rank[None, :] == wanted[:, None])
    attn_slots = jnp.sum(jnp.where(chosen, local_at[None, :], 0), axis=1)
    attn_held = jnp.sum(jnp.where(chosen, jnp.arange(6, dtype=jnp.int32)[None, :] + 1, 0), axis=1) - 1
    attn_rates = jnp.take(rates, attn_slots)
    e_all, place, side, rates, attn_slots, attn_held, attn_rates = together(
        e_all, place, side, rates, attn_slots, attn_held, attn_rates
    )

    before = ()
    hidden_all = []
    sums = []
    for c in range(2):
        *before, units, grads = expert_rows(
            e_all, g_all, my_gates, expert_w, part, team * c, before, 2 * seg_len
        )
        hidden_all.append(units)
        sums.append(lax.psum_scatter(after(grads, *sums), "z", scatter_dimension=0, tiled=True))
    grad_expert_in = plane_reduce(*before)

    cot_rows = cot_low.astype(F32)
    norm_grad_two = norm_back(resid_one, scale_two, gains[1], grad_expert_in)
    gain_grad_two = jnp.sum(grad_expert_in * resid_one * scale_two, axis=0)
    grad_resid = cot_rows + norm_grad_two
    def over(total):
        give = lax.dynamic_slice_in_dim(total, (1 - x_index) * row_count, row_count, axis=0)
        return swap(give, "x")

    dy = after(grad_resid.astype(BF), sums[0])
    over_x, over_y, moe = together(
        swap(dy, "x"), swap(dy, "y"), expert_out([after(units, dy) for units in hidden_all], expert_w, 2 * seg_len)
    )
    corner_top, corner_low, moe_got = together(
        swap(over_x[:half], "y"), swap(over_y[half:], "x"), swap(moe[1], "c")
    )
    dy_mine = stack([dy, over_x, over_y, corner_top, corner_low])
    dy_other, moe_corner = together(swap(dy_mine, "c"), corner_rows(moe[0], moe_got))
    dy_all = (dy_mine, dy_other)
    back = attend_back(info, query, kv, qseg, stat, dy_all, attn_mix, attn_w, cosine, sine, seg_len)
    (grad_q_low, dkv_zero, dkv_one, dkv_two, grad_w_out), got_one, moe_x, moe_y = together(
        back, over(sums[0]), swap(moe_corner[:half], "y"), swap(moe_corner[half:], "x")
    )
    to_x, to_y = edge_rows(moe[0], moe_got, moe_x, moe_y)

    passed_one, got_two, out_y = together(
        shift(dkv_two, -1), over(after(sums[1], grad_q_low)), swap(to_y, "y")
    )
    passing = (dkv_one + passed_one.astype(F32)).astype(BF)
    first_half, *second_half = pack(place, side, info, sums, [got_one, got_two], part, halves)
    passed, slot_grads, out_x = together(shift(passing, -1), over_wsh(first_half), swap(to_x, "x"))
    *grads, attn_grads, gain_part = project_back(
        grad_q_low, dkv_zero, passed, packed_all, attn_w, cosine, sine, grad_w_out, seg_len
    )
    attn_sum = lax.psum_scatter(attn_grads, "z", scatter_dimension=0, tiled=True)
    (grad_low, grad_high), *more = together(
        grads,
        *[over_wsh([after(array, passed) for array in arrays]) for arrays in second_half],
    )
    slot_grads = sum(more, slot_grads)

    hops = [("x", 1), ("z", 0), *[("z", k) for k in range(1, lax.axis_size("z").bit_length() - 1)], ("y", 1), ("c", 1)]

    def hop(value, at):
        axis, k = hops[at]
        if axis != "z":
            return value + swap(value, axis)
        return value + lax.ppermute(value, "z", [(i, i ^ (1 << k)) for i in range(lax.axis_size("z"))])

    gain_grad = jnp.stack([jnp.sum(gain_part, axis=0) / gains[0], gain_grad_two])
    grad_got = swap(grad_high, "c")
    grad_corner = corner_rows(grad_low, grad_got)
    grad_x, grad_y, gain_grad = together(
        swap(grad_corner[:half], "y"),
        swap(grad_corner[half:], "x"),
        hop(after(gain_grad, grad_corner), 0),
    )
    to_x, to_y = edge_rows(grad_low, grad_got, grad_x, grad_y)
    attn_sum, last_x, last_y, gain_grad, new = together(
        attn_sum,
        swap(to_x, "x"),
        swap(to_y, "y"),
        hop(gain_grad, 1),
        update(after(info, to_x), rates, slot_grads, masters, first_moments, second_moments),
    )

    attn_rows = jnp.broadcast_to(
        attn_sum.reshape(2, 1, row_count, 3 * part), (2, 4, row_count, 3 * part)
    ).reshape(8, row_count, 3 * part)
    attn_back, gain_grad = together(
        lax.all_to_all(attn_rows, PLANE, split_axis=0, concat_axis=0, tiled=True),
        hop(gain_grad, 2),
    )
    for at in range(3, len(hops)):
        gain_grad = hop(gain_grad, at)

    def own(kept, got, *rest):
        total = kept[:seg_len].astype(F32) + got[:seg_len].astype(F32)
        return total + sum(value.astype(F32) for value in rest)

    output = (resid_one + own(moe[0], moe_got, out_x, out_y)).astype(BF)
    grad_in_one = own(grad_low, grad_got, last_x, last_y)
    input_grad = grad_resid + norm_back(tokens_f, scale_one, gains[0], grad_in_one)
    new_masters, new_first, new_second = update_attn(
        attn_slots, attn_held, attn_rates, attn_back, masters, first_moments, second_moments, new
    )
    new_gains, new_gain_first, new_gain_second = adamw(
        norm_gains, gain_first, gain_second, gain_grad, GAIN_RATE, 0.0
    )
    return (
        output[None],
        input_grad[None],
        new_masters,
        new_first,
        new_second,
        new_gains,
        new_gain_first,
        new_gain_second,
    )


def solution(mesh):
    ctx, wsh = mesh.devices.shape
    fine = Mesh(mesh.devices.reshape(ctx // 2, 2, wsh // 2, 2), ("z", "x", "y", "c"))
    rows = P(WSH, ("z", "x"), None)
    marks = P(WSH, ("z", "x"))
    return jax.shard_map(
        shards,
        mesh=fine,
        in_specs=(rows, marks, rows, rows, rows, P(), rows, rows, rows, P(), P(), P()),
        out_specs=(rows, rows, rows, rows, rows, P(), P(), P()),
        check_vma=False,
    )
```

```python
import jax
import jax.numpy as jnp
import numpy as np
from jax import lax
from jax.experimental import pallas as pl
from jax.experimental.pallas import tpu as pltpu
from jax.sharding import Mesh
from jax.sharding import PartitionSpec as P

QH = 16
KVH = 8
HD = 64
STEP = 7

EPS_NORM = 1e-05
THETA = 10000.0
BETA_ONE = 0.5
BETA_TWO = 0.6
ADAM_EPS = 1e-08
DECAY = 0.1
GAIN_RATE = 0.3
NEG_BIG = -1e30
PLANE = ("x", "y", "c")
WSH = ("y", "c")
BF = jnp.bfloat16
F32 = jnp.float32


def swap(value, axis):
    return lax.ppermute(value, axis, [(0, 1), (1, 0)])


def shift(value, by):
    count = lax.axis_size("z")
    pairs = [(i, i + by) for i in range(count) if 0 <= i + by < count]
    return lax.ppermute(value, "z", pairs)


def took(us):
    return pl.CostEstimate(flops=int(us * 1e9), bytes_accessed=2**20, transcendentals=0)


def vmem(mib):
    return pltpu.CompilerParams(vmem_limit_bytes=mib * 2**20)


def whole(shape):
    return pl.BlockSpec(shape, lambda *_: (0,) * len(shape))


def half_specs(block, width, rows, at):
    low = pl.BlockSpec((block, width), lambda *g: (jnp.minimum(at(*g), rows // 2 // block - 1), 0))
    high = pl.BlockSpec((block, width), lambda *g: (jnp.maximum(at(*g) - rows // 2 // block, 0), 0))
    return [low, high]


def together(*values):
    return lax.optimization_barrier(values)


def after(value, *first):
    return lax.optimization_barrier((value, *first))[0]


def stack_kernel(*refs):
    at = 0
    for ref in refs[:-1]:
        refs[-1][at : at + ref.shape[0]] = ref[...]
        at += ref.shape[0]


def stack(pieces):
    shape = (sum(piece.shape[0] for piece in pieces), pieces[0].shape[1])
    return pl.pallas_call(
        stack_kernel,
        grid=(1,),
        in_specs=[whole(piece.shape) for piece in pieces],
        out_specs=whole(shape),
        out_shape=jax.ShapeDtypeStruct(shape, BF),
        cost_estimate=took(2),
        compiler_params=vmem(32),
    )(*pieces)


def plane_gather(rows, wait=lambda value: value, last=lambda value: value):
    half = rows.shape[0] // 2
    over_x = swap(rows, "x")
    over_y = swap(rows, "y")
    first, second = wait((over_x[:half], over_y[half:]))
    corner_top = swap(first, "y")
    corner_low = swap(second, "x")
    mine = stack([rows, over_x, over_y, corner_top, corner_low])
    return mine, swap(last(mine), "c")


def corner_kernel(kept_ref, got_ref, out_ref):
    out_ref[...] = (kept_ref[...].astype(F32) + got_ref[...].astype(F32)).astype(BF)


def corner_rows(kept, got):
    rows, width = kept.shape
    spec = pl.BlockSpec((rows // 4, width), lambda i: (3, 0))
    return pl.pallas_call(
        corner_kernel,
        grid=(1,),
        in_specs=[spec, spec],
        out_specs=whole((rows // 4, width)),
        out_shape=jax.ShapeDtypeStruct((rows // 4, width), BF),
        cost_estimate=took(1),
        compiler_params=vmem(32),
    )(kept, got)


def edge_kernel(kx_ref, gx_ref, ky_ref, gy_ref, fx_ref, fy_ref, x_ref, y_ref):
    half = fx_ref.shape[0]
    for kept, got, extra, out_ref, at in ((kx_ref, gx_ref, fx_ref, x_ref, 0), (ky_ref, gy_ref, fy_ref, y_ref, 1)):
        total = kept[...].astype(F32) + got[...].astype(F32)
        mine, rest = slice(at * half, (at + 1) * half), slice((1 - at) * half, (2 - at) * half)
        out_ref[mine] = (total[mine] + extra[...].astype(F32)).astype(BF)
        out_ref[rest] = total[rest].astype(BF)


def edge_rows(kept, got, for_x, for_y):
    rows, width = kept.shape
    step = rows // 4
    one, two = (pl.BlockSpec((step, width), lambda i, b=b: (b, 0)) for b in (1, 2))
    half = whole((step // 2, width))
    return pl.pallas_call(
        edge_kernel,
        grid=(1,),
        in_specs=[one, one, two, two, half, half],
        out_specs=[whole((step, width))] * 2,
        out_shape=[jax.ShapeDtypeStruct((step, width), BF)] * 2,
        cost_estimate=took(2),
        compiler_params=vmem(32),
    )(kept, got, kept, got, for_x, for_y)


def plane_reduce(kept, sent, waits=(None, None, None)):
    hold = [wait or (lambda value: value) for wait in waits]
    step = kept.shape[0] // 4
    half = step // 2
    got = swap(hold[0](sent), "c")
    corner = hold[1](corner_rows(kept, got))
    for_x = swap(corner[:half], "y")
    for_y = swap(corner[half:], "x")
    to_x, to_y = hold[2](edge_rows(kept, got, for_x, for_y))
    own = kept[:step].astype(F32) + got[:step].astype(F32)
    return own + swap(to_x, "x").astype(F32) + swap(to_y, "y").astype(F32)


def norm_scale(values):
    return lax.rsqrt(jnp.mean(values * values, axis=-1, keepdims=True) + EPS_NORM)


def norm_back(values, scale_row, gain_row, grad_out):
    weighted = grad_out * gain_row
    grad_in = scale_row * weighted - values * scale_row**3 * jnp.mean(
        values * weighted, axis=-1, keepdims=True
    )
    return grad_in


def kind_rates(width, hidden):
    base_rate = 0.5 * width ** (-0.5)
    return [
        base_rate,
        base_rate,
        base_rate,
        2.0 * (2 * hidden) ** (-0.5),
        base_rate,
        base_rate,
        3.0 * hidden ** (-0.5),
        base_rate,
    ]


def adamw(weight, first, second, grad, rate, decay):
    first_new = BETA_ONE * first + (1.0 - BETA_ONE) * grad
    second_new = BETA_TWO * second + (1.0 - BETA_TWO) * grad * grad
    first_hat = first_new / (1.0 - BETA_ONE**STEP)
    second_hat = second_new / (1.0 - BETA_TWO**STEP)
    weight_new = weight - rate * (first_hat / (jnp.sqrt(second_hat) + ADAM_EPS) + decay * weight)
    return (weight_new, first_new, second_new)


def dot_nn(left, right):
    return lax.dot_general(left, right, (((1,), (0,)), ((), ())), preferred_element_type=F32)


def dot_nt(left, right):
    return lax.dot_general(left, right, (((1,), (1,)), ((), ())), preferred_element_type=F32)


def dot_tn(left, right):
    return lax.dot_general(left, right, (((0,), (0,)), ((), ())), preferred_element_type=F32)


def turn(value, lane):
    low = (lane % HD) < (HD // 2)
    return jnp.where(
        low, -pltpu.roll(value, 2 * HD - HD // 2, 1), pltpu.roll(value, HD // 2, 1)
    )

def choose(early, low_ref, high_ref):
    return jnp.where(early, low_ref[...], high_ref[...])


def attn_send_kernel(at_ref, ok_ref, *refs):
    mats, out_ref = refs[:6], refs[6]

    def read(m):
        return jnp.where(ok_ref[m] == 1, mats[m][0], 0.0).astype(BF)

    part = out_ref.shape[3]
    for side in range(2):
        for kind, m in ((0, side), (2, 4 + side)):
            mat = read(m)
            for j in range(4):
                out_ref[4 * side + j, kind] = mat[:, j * part : (j + 1) * part]
    keys, values = read(2), read(3)
    for h in range(8):
        both = (keys[:, h * HD : (h + 1) * HD], values[:, h * HD : (h + 1) * HD])
        out_ref[h, 1] = jnp.concatenate(both, axis=1)


def attn_send(masters, at, ok):
    _, rows, hidden = masters.shape
    part = hidden // 4
    specs = [pl.BlockSpec((1, rows, hidden), lambda i, at, ok, m=m: (at[m], 0, 0)) for m in range(6)]
    return pl.pallas_call(
        attn_send_kernel,
        grid_spec=pltpu.PrefetchScalarGridSpec(
            num_scalar_prefetch=2,
            grid=(1,),
            in_specs=specs,
            out_specs=pl.BlockSpec((8, 3, rows, part), lambda i, at, ok: (0, 0, 0, 0)),
        ),
        out_shape=jax.ShapeDtypeStruct((8, 3, rows, part), BF),
        cost_estimate=took(3),
        compiler_params=vmem(62),
    )(at, ok, *([masters] * 6))


def bulk_send_kernel(info_ref, in_ref, *outs):
    part = outs[0].shape[2]
    for d, out_ref in enumerate(outs):
        start = pl.multiple_of((info_ref[1] ^ d) * part, part)
        out_ref[...] = in_ref[:, :, pl.ds(start, part)].astype(BF)


def bulk_send(info, masters):
    slots, rows, hidden = masters.shape
    step, part = 5 if slots % 5 == 0 else 1, hidden // 4
    return pl.pallas_call(
        bulk_send_kernel,
        grid=(slots // step,),
        in_specs=[
            pl.BlockSpec(memory_space=pltpu.SMEM),
            pl.BlockSpec((step, rows, hidden), lambda i: (i, 0, 0)),
        ],
        out_specs=[pl.BlockSpec((step, rows, part), lambda i: (i, 0, 0))] * 4,
        out_shape=[jax.ShapeDtypeStruct((slots, rows, part), BF)] * 4,
        cost_estimate=took(4),
        compiler_params=vmem(62),
    )(info, masters)


def over_wsh(arrays):
    across = [(i, i ^ 3) for i in range(4)]
    return [arrays[0], swap(arrays[1], "c"), swap(arrays[2], "y"), lax.ppermute(arrays[3], WSH, across)]


def pick_kernel(at_ref, *refs):
    slots, outs, held = refs[:4], refs[4:-1], refs[-1]
    count = slots[0].shape[0]
    part = held.shape[2]
    for d in range(4):
        held[d * count : (d + 1) * count] = slots[d][...]
    for i, out_ref in enumerate(outs):
        number = out_ref.shape[1] // part
        for k in range(number):
            out_ref[:, k * part : (k + 1) * part] = held[at_ref[i * number + k]]


def pick(places, slots, parts):
    count, rows, part = slots[0].shape
    wide = (rows, places.shape[0] // parts * part)
    return pl.pallas_call(
        pick_kernel,
        grid_spec=pltpu.PrefetchScalarGridSpec(
            num_scalar_prefetch=1,
            grid=(1,),
            in_specs=[pl.BlockSpec((count, rows, part), lambda i, a: (0, 0, 0))] * 4,
            out_specs=[pl.BlockSpec(wide, lambda i, a: (0, 0))] * parts,
            scratch_shapes=[pltpu.VMEM((4 * count, rows, part), BF)],
        ),
        out_shape=[jax.ShapeDtypeStruct(wide, BF)] * parts,
        cost_estimate=took(3),
        compiler_params=vmem(62),
    )(places, *slots)


def join_kernel(info_ref, *refs):
    count = len(refs) // 2
    keeps, gots, out_ref = refs[:count], refs[count:-1], refs[-1]
    rows, wide = keeps[0].shape
    first = info_ref[0] == 0
    for i in range(count):
        keep, got, lanes = keeps[i][...], gots[i][...], slice(i * wide, (i + 1) * wide)
        out_ref[:rows, lanes] = jnp.where(first, keep, got)
        out_ref[rows:, lanes] = jnp.where(first, got, keep)


def join(info, keeps, gots):
    rows, wide = keeps[0].shape
    shape = (2 * rows, wide * len(keeps))
    return pl.pallas_call(
        join_kernel,
        grid=(1,),
        in_specs=[pl.BlockSpec(memory_space=pltpu.SMEM)] + [whole((rows, wide))] * (2 * len(keeps)),
        out_specs=whole(shape),
        out_shape=jax.ShapeDtypeStruct(shape, BF),
        cost_estimate=took(1.5),
        compiler_params=vmem(32),
    )(info, *keeps, *gots)


def pack_kernel(place_ref, side_ref, info_ref, *refs):
    totals, gots, outs, held = refs[:2], refs[2:4], refs[4:-1], refs[-1]
    count, rows, part = outs[0].shape
    full = gots[0].shape[0]
    mine = pl.ds(pl.multiple_of(info_ref[0] * full, full), full)
    for c in range(2):
        held[c * full : (c + 1) * full] = totals[c][mine]
        held[(2 + c) * full : (3 + c) * full] = gots[c][...]
    held[4 * full :] = jnp.zeros((full, held.shape[1]), BF)
    for d in range(4):

        def one(j, carry):
            s = (info_ref[1] ^ d) * count + j
            lanes = pl.ds(pl.multiple_of(place_ref[s] * part, part), part)
            for h, out_ref in enumerate(outs[d::4]):
                start = pl.multiple_of(side_ref[s] * full + h * rows, rows)
                out_ref[j] = held[pl.ds(start, rows), lanes]
            return carry

        lax.fori_loop(0, count, one, 0)


def pack(place, side, info, totals, gots, part, halves):
    rows, wide = gots[0].shape
    shape = (place.shape[0] // 4, rows // halves, part)
    outs = pl.pallas_call(
        pack_kernel,
        grid_spec=pltpu.PrefetchScalarGridSpec(
            num_scalar_prefetch=3,
            grid=(1,),
            in_specs=[
                *[pl.BlockSpec((2 * rows, wide), lambda i, a, b, c: (0, 0))] * 2,
                *[pl.BlockSpec((rows, wide), lambda i, a, b, c: (0, 0))] * 2,
            ],
            out_specs=[pl.BlockSpec(shape, lambda i, a, b, c: (0, 0, 0))] * (4 * halves),
            scratch_shapes=[pltpu.VMEM((5 * rows, wide), BF)],
        ),
        out_shape=[jax.ShapeDtypeStruct(shape, BF)] * (4 * halves),
        cost_estimate=took(3),
        compiler_params=vmem(32),
    )(place, side, info, *totals, *gots)
    return [outs[4 * h : 4 * h + 4] for h in range(halves)]


def update_kernel(info_ref, rate_ref, *refs):
    grads, (w_ref, m_ref, v_ref, w_out, m_out, v_out) = refs[:-6], refs[-6:]
    part = grads[0].shape[2]
    rows = grads[0].shape[1]

    def one(s, carry):
        rate = rate_ref[pl.program_id(0) * w_ref.shape[0] + s]
        for i, grad_ref in enumerate(grads):
            lanes = pl.ds(pl.multiple_of((info_ref[1] ^ (i % 4)) * part, part), part)
            at = slice((i // 4) * rows, (i // 4 + 1) * rows)
            w_out[s, at, lanes], m_out[s, at, lanes], v_out[s, at, lanes] = adamw(
                w_ref[s, at, lanes],
                m_ref[s, at, lanes],
                v_ref[s, at, lanes],
                grad_ref[s].astype(F32),
                rate,
                DECAY,
            )
        return carry

    lax.fori_loop(0, w_ref.shape[0], one, 0)


def update(info, rates, grads, masters, first, second):
    slots, rows, hidden = masters.shape
    step = 4 if slots % 4 == 0 else 1
    smem = pl.BlockSpec(memory_space=pltpu.SMEM)
    spec = pl.BlockSpec((step, rows, hidden), lambda i: (i, 0, 0))
    grad_spec = pl.BlockSpec((step, *grads[0].shape[1:]), lambda i: (i, 0, 0))
    return pl.pallas_call(
        update_kernel,
        grid=(slots // step,),
        in_specs=[smem, smem] + [grad_spec] * len(grads) + [spec] * 3,
        out_specs=[spec] * 3,
        out_shape=[jax.ShapeDtypeStruct(masters.shape, F32)] * 3,
        cost_estimate=took(6),
        compiler_params=vmem(62),
    )(info, rates, *grads, masters, first, second)


def update_attn_kernel(slot_ref, held_ref, rate_ref, attn_ref, *refs):
    (w_ref, m_ref, v_ref), olds, news = refs[:3], refs[3:6], refs[6:]
    step = pl.program_id(0)
    held = held_ref[step]
    rate = rate_ref[step]
    part = w_ref.shape[2] // 4

    def write(j, grad):
        lanes = slice(j * part, (j + 1) * part)
        results = adamw(
            w_ref[0, :, lanes], m_ref[0, :, lanes], v_ref[0, :, lanes], grad.astype(F32), rate, DECAY
        )
        for new_ref, result in zip(news, results):
            new_ref[0, :, lanes] = result

    @pl.when(held < 0)
    def _():
        for old_ref, new_ref in zip(olds, news):
            new_ref[...] = old_ref[...]

    for m, side, kind in ((0, 0, 0), (1, 1, 0), (4, 0, 2), (5, 1, 2)):

        @pl.when(held == m)
        def _():
            for j in range(4):
                write(j, attn_ref[4 * side + j, :, kind * part : (kind + 1) * part])

    for m, start in ((2, part), (3, part + HD)):

        @pl.when(held == m)
        def _():
            for j in range(4):
                pieces = [attn_ref[2 * j + i, :, start : start + HD] for i in range(2)]
                write(j, jnp.concatenate(pieces, axis=1))


def update_attn(slots, held, rates, attn_back, masters, first, second, new):
    _, rows, hidden = masters.shape
    spec = pl.BlockSpec((1, rows, hidden), lambda i, at, held: (at[i], 0, 0))
    return pl.pallas_call(
        update_attn_kernel,
        grid_spec=pltpu.PrefetchScalarGridSpec(
            num_scalar_prefetch=2,
            grid=(slots.shape[0],),
            in_specs=[
                pl.BlockSpec(memory_space=pltpu.SMEM),
                pl.BlockSpec(attn_back.shape, lambda i, at, held: (0, 0, 0)),
                *[spec] * 6,
            ],
            out_specs=[spec] * 3,
        ),
        out_shape=[jax.ShapeDtypeStruct(masters.shape, F32)] * 3,
        input_output_aliases={7: 0, 8: 1, 9: 2},
        cost_estimate=took(5),
        compiler_params=vmem(62),
    )(slots, held, rates, attn_back, masters, first, second, *new)


def project_kernel(low_ref, high_ref, w_ref, cos_ref, sin_ref, q_ref, kv_ref):
    early = pl.program_id(0) < pl.num_programs(0) // 2
    both = dot_nn(choose(early, low_ref, high_ref), w_ref[...])
    cosine = cos_ref[0]
    sine = sin_ref[0]
    lane = lax.broadcasted_iota(jnp.int32, cosine.shape, 1)
    query = both[:, : 2 * HD]
    pair = both[:, 2 * HD :]
    q_ref[...] = (query * cosine + turn(query, lane) * sine).astype(BF)
    turned = pair * cosine + turn(pair, lane) * sine
    kv_ref[...] = jnp.where(lane < HD, turned, pair).astype(BF)


def project(x_low, x_high, weights, cosine, sine, block):
    rows = 2 * x_low.shape[0]
    width = weights.shape[0]
    table = pl.BlockSpec((1, block, 2 * HD), lambda i: (i % 2, 0, 0))
    return pl.pallas_call(
        project_kernel,
        grid=(rows // block,),
        in_specs=[
            *half_specs(block, width, rows, lambda i: i),
            pl.BlockSpec((width, 4 * HD), lambda i: (0, 0)),
            table,
            table,
        ],
        out_specs=[pl.BlockSpec((block, 2 * HD), lambda i: (i, 0))] * 2,
        out_shape=[jax.ShapeDtypeStruct((rows, 2 * HD), BF)] * 2,
        cost_estimate=took(6),
        compiler_params=vmem(32),
    )(x_low, x_high, weights, cosine, sine)


def head_rows(rows, head, lane, high):
    if (head == 1) != high:
        rows = pltpu.roll(rows, HD, 1)
    keep = (lane >= HD) if high else (lane < HD)
    return jnp.where(keep, rows, jnp.zeros_like(rows))


def masks(info_ref, qseg_ref, kseg, block, span):
    flip = info_ref[0]
    chunk = pl.program_id(1)
    key_at = lax.broadcasted_iota(jnp.int32, (span, 1), 0)
    query_at = lax.broadcasted_iota(jnp.int32, (1, block), 1)
    swapped = jnp.where(flip == 1, key_at ^ block, key_at)
    key_pos = jnp.where(key_at < 2 * block, swapped, -1)
    query_pos = query_at + block * jnp.where(flip == 1, 1 - chunk, chunk)
    return (key_pos <= query_pos) & (kseg == qseg_ref[0])


def load_pairs(refs, tails, kv_all, kv_turned, marks, kseg, reach):
    third = kv_all.shape[0] // 3
    for i, (ref, tail) in enumerate(zip(refs, tails)):
        kv_all[i * third : (i + 1) * third] = ref[...]
        marks[i] = tail[...].astype(F32).reshape(marks.shape[1:])
        columns = marks[i, pl.program_id(0)].T
        for j in range(third // 128):
            at = i * third + j * 128
            kseg[at : at + 128] = columns[:, j : j + 1]
    kv_turned[...] = kv_all[...].T
    seq = pl.program_id(0)
    least = jnp.min(marks[0, seq][: third // 128])
    far = jnp.max(marks[2, seq]) >= least
    near = jnp.max(marks[1, seq]) >= least
    reach[0] = jnp.where(far, 3, jnp.where(near, 2, 1)).astype(jnp.int32)


def attend_kernel(info_ref, q_ref, k0_ref, k1_ref, k2_ref, t0_ref, t1_ref, t2_ref, qseg_ref,
                  w_ref, mix_ref, stat_ref, low_ref, high_ref, kv_all, kv_turned, marks, kseg, reach):
    block = q_ref.shape[0]
    span = kv_all.shape[0]

    @pl.when(pl.program_id(1) == 0)
    def _():
        load_pairs((k0_ref, k1_ref, k2_ref), (t0_ref, t1_ref, t2_ref), kv_all, kv_turned, marks, kseg, reach)

    lane = lax.broadcasted_iota(jnp.int32, (block, 2 * HD), 1)
    query = q_ref[...] * jnp.asarray(HD**-0.5, BF)

    def attend_to(keys):
        allowed = masks(info_ref, qseg_ref, kseg[:keys], block, keys)
        mixed = []
        for head in range(2):
            scores = dot_nt(kv_all[:keys], head_rows(query, head, lane, False))
            scores = jnp.where(allowed, scores, NEG_BIG)
            top = jnp.max(scores, axis=0, keepdims=True)
            powers = jnp.exp(scores - top)
            total = jnp.sum(powers, axis=0, keepdims=True)
            stat_ref[0, 0, head : head + 1, :] = top + jnp.log(total)
            probs = (powers * (1.0 / total)).astype(BF)
            mixed.append(dot_nn(kv_turned[:, :keys], probs)[HD:])
        mix_ref[...] = jnp.concatenate(mixed, axis=0).T.astype(BF)

    for blocks in range(1, 4):

        @pl.when(reach[0] == blocks)
        def _():
            attend_to(blocks * span // 3)

    mix = mix_ref[...]
    out = dot_nt(mix, w_ref[...]).astype(BF)
    early = pl.program_id(0) < pl.num_programs(0) // 2

    @pl.when(early)
    def _():
        low_ref[...] = out

    @pl.when(jnp.logical_not(early))
    def _():
        high_ref[...] = out


def attend(info, query, kv, qseg, weights, block):
    rows = query.shape[0]
    seqs = rows // (2 * block)
    width = weights.shape[0]
    row_spec = pl.BlockSpec((block, 2 * HD), lambda s, i: (2 * s + i, 0))
    kv_spec = pl.BlockSpec((2 * block, 2 * HD), lambda s, i: (s, 0))
    tail_spec = pl.BlockSpec((8 * seqs, 2 * HD), lambda s, i: (rows // (8 * seqs), 0))
    return pl.pallas_call(
        attend_kernel,
        grid=(seqs, 2),
        in_specs=[
            pl.BlockSpec(memory_space=pltpu.SMEM),
            row_spec,
            kv_spec,
            kv_spec,
            kv_spec,
            tail_spec,
            tail_spec,
            tail_spec,
            pl.BlockSpec((1, 1, block), lambda s, i: (2 * s + i, 0, 0)),
            pl.BlockSpec((width, 2 * HD), lambda s, i: (0, 2)),
        ],
        out_specs=[
            row_spec,
            pl.BlockSpec((1, 1, 2, block), lambda s, i: (s, i, 0, 0)),
            *half_specs(block, width, rows, lambda s, i: 2 * s + i),
        ],
        out_shape=[
            jax.ShapeDtypeStruct((rows, 2 * HD), BF),
            jax.ShapeDtypeStruct((seqs, 2, 2, block), F32),
            *[jax.ShapeDtypeStruct((rows // 2, width), BF)] * 2,
        ],
        scratch_shapes=[
            pltpu.VMEM((6 * block, 2 * HD), BF),
            pltpu.VMEM((2 * HD, 6 * block), BF),
            pltpu.VMEM((3, seqs, 8, 128), F32),
            pltpu.VMEM((6 * block, 1), F32),
            pltpu.SMEM((1,), jnp.int32),
        ],
        cost_estimate=took(24),
        compiler_params=vmem(32),
    )(info, query, *kv, *kv, qseg, weights)


def attend_back_kernel(info_ref, q_ref, k0_ref, k1_ref, k2_ref, t0_ref, t1_ref, t2_ref, qseg_ref,
                       stat_ref, dy_low, dy_high, mix_ref, w_ref, cos_ref, sin_ref,
                       dq_ref, dk0_ref, dk1_ref, dk2_ref, dw_ref,
                       kv_all, kv_turned, marks, kseg, reach, sums, dw_sum, turned_sum):
    block = q_ref.shape[0]
    span = kv_all.shape[0]
    third = span // 3
    seq = pl.program_id(0)
    chunk = pl.program_id(1)

    @pl.when((chunk == 0) & (seq == 0))
    def _():
        dw_sum[...] = jnp.zeros_like(dw_sum)

    @pl.when(chunk == 0)
    def _():
        sums[...] = jnp.zeros_like(sums)
        load_pairs((k0_ref, k1_ref, k2_ref), (t0_ref, t1_ref, t2_ref), kv_all, kv_turned, marks, kseg, reach)

    lane = lax.broadcasted_iota(jnp.int32, (block, 2 * HD), 1)
    query = q_ref[...] * jnp.asarray(HD**-0.5, BF)
    grad_rows = choose(seq < pl.num_programs(0) // 2, dy_low, dy_high)
    dw_sum[...] += dot_tn(mix_ref[...], grad_rows)
    grad_mix = dot_nn(grad_rows, w_ref[...]).astype(BF)

    def attend_to(keys):
        allowed = masks(info_ref, qseg_ref, kseg[:keys], block, keys)
        grad_query = []
        for head in range(2):
            q_low = head_rows(query, head, lane, False)
            g_high = head_rows(grad_mix, head, lane, True)
            scores = dot_nt(kv_all[:keys], q_low)
            stat = stat_ref[0, 0, head : head + 1, :]
            probs = jnp.where(allowed, jnp.exp(scores - stat), 0.0)
            grad_probs = dot_nt(kv_all[:keys], g_high)
            delta = jnp.sum(probs * grad_probs, axis=0, keepdims=True)
            grad_scores = (probs * (grad_probs - delta)).astype(BF)
            sums[:keys] += dot_nn(grad_scores, q_low) + dot_nn(probs.astype(BF), g_high)
            grad_query.append(dot_nn(kv_turned[:, :keys], grad_scores)[:HD])
        turned_sum[...] = jnp.concatenate(grad_query, axis=0)

    for blocks in range(1, 4):

        @pl.when(reach[0] == blocks)
        def _():
            attend_to(blocks * span // 3)

    grad_q = turned_sum[...].T * HD**-0.5
    dq_ref[...] = (grad_q * cos_ref[0] - turn(grad_q * sin_ref[0], lane)).astype(BF)

    @pl.when(chunk == 1)
    def _():
        dk0_ref[...] = sums[:third]
        dk1_ref[...] = sums[third : 2 * third]
        dk2_ref[...] = sums[2 * third :].astype(BF)

    @pl.when((chunk == 1) & (seq == pl.num_programs(0) - 1))
    def _():
        dw_ref[...] = dw_sum[...].T.astype(BF)


def attend_back(info, query, kv, qseg, stat, grad_rows, mix, weights, cosine, sine, block):
    rows = query.shape[0]
    seqs = rows // (2 * block)
    width = weights.shape[0]
    row_spec = pl.BlockSpec((block, 2 * HD), lambda s, i: (2 * s + i, 0))
    kv_spec = pl.BlockSpec((2 * block, 2 * HD), lambda s, i: (s, 0))
    tail_spec = pl.BlockSpec((8 * seqs, 2 * HD), lambda s, i: (rows // (8 * seqs), 0))
    table = pl.BlockSpec((1, block, 2 * HD), lambda s, i: (i, 0, 0))
    return pl.pallas_call(
        attend_back_kernel,
        grid=(seqs, 2),
        in_specs=[
            pl.BlockSpec(memory_space=pltpu.SMEM),
            row_spec,
            kv_spec,
            kv_spec,
            kv_spec,
            tail_spec,
            tail_spec,
            tail_spec,
            pl.BlockSpec((1, 1, block), lambda s, i: (2 * s + i, 0, 0)),
            pl.BlockSpec((1, 1, 2, block), lambda s, i: (s, i, 0, 0)),
            *half_specs(block, width, rows, lambda s, i: 2 * s + i),
            row_spec,
            pl.BlockSpec((width, 2 * HD), lambda s, i: (0, 2)),
            table,
            table,
        ],
        out_specs=[row_spec, kv_spec, kv_spec, kv_spec, whole((width, 2 * HD))],
        out_shape=[
            jax.ShapeDtypeStruct((rows, 2 * HD), BF),
            jax.ShapeDtypeStruct((rows, 2 * HD), F32),
            jax.ShapeDtypeStruct((rows, 2 * HD), F32),
            jax.ShapeDtypeStruct((rows, 2 * HD), BF),
            jax.ShapeDtypeStruct((width, 2 * HD), BF),
        ],
        scratch_shapes=[
            pltpu.VMEM((6 * block, 2 * HD), BF),
            pltpu.VMEM((2 * HD, 6 * block), BF),
            pltpu.VMEM((3, seqs, 8, 128), F32),
            pltpu.VMEM((6 * block, 1), F32),
            pltpu.SMEM((1,), jnp.int32),
            pltpu.VMEM((6 * block, 2 * HD), F32),
            pltpu.VMEM((2 * HD, width), F32),
            pltpu.VMEM((2 * HD, block), F32),
        ],
        cost_estimate=took(12),
        compiler_params=vmem(36),
    )(info, query, *kv, *kv, qseg, stat, *grad_rows, mix, weights, cosine, sine)


def project_back_kernel(dq_ref, a_ref, b_ref, x_low, x_high, w_ref, cos_ref, sin_ref, dout_ref,
                        low_ref, high_ref, dw_ref, gain_ref, dw_sum):
    step = pl.program_id(0)

    @pl.when(step == 0)
    def _():
        dw_sum[...] = jnp.zeros_like(dw_sum)
        gain_ref[...] = jnp.zeros_like(gain_ref)

    grad = a_ref[...] + b_ref[...].astype(F32)
    lane = lax.broadcasted_iota(jnp.int32, grad.shape, 1)
    turned = grad * cos_ref[0] - turn(grad * sin_ref[0], lane)
    pair = jnp.where(lane < HD, turned, grad).astype(BF)
    both = jnp.concatenate([dq_ref[...], pair], axis=1)
    grad_in = dot_nt(both, w_ref[...])
    early = step < pl.num_programs(0) // 2

    @pl.when(early)
    def _():
        low_ref[...] = grad_in.astype(BF)

    @pl.when(jnp.logical_not(early))
    def _():
        high_ref[...] = grad_in.astype(BF)

    x_rows = choose(early, x_low, x_high)
    dw_sum[...] += dot_tn(both, x_rows)
    weighted = grad_in * x_rows.astype(F32)
    gain_ref[...] += jnp.sum(weighted.reshape(-1, 8, weighted.shape[1]), axis=0)

    @pl.when(step == pl.num_programs(0) - 1)
    def _():
        dw_ref[:, : 4 * HD] = dw_sum[...].T.astype(BF)
        dw_ref[:, 4 * HD :] = dout_ref[...]


def project_back(grad_q, here, arrived, x_rows, weights, cosine, sine, grad_out, block):
    rows = here.shape[0]
    width, cols = weights.shape[0], 4 * HD
    spec = pl.BlockSpec((block, 2 * HD), lambda i: (i, 0))
    table = pl.BlockSpec((1, block, 2 * HD), lambda i: (i % 2, 0, 0))
    return pl.pallas_call(
        project_back_kernel,
        grid=(rows // block,),
        in_specs=[
            *[spec] * 3,
            *half_specs(block, width, rows, lambda i: i),
            pl.BlockSpec((width, cols), lambda i: (0, 0)),
            table,
            table,
            whole(grad_out.shape),
        ],
        out_specs=[
            *half_specs(block, width, rows, lambda i: i),
            whole((width, 6 * HD)),
            whole((8, width)),
        ],
        out_shape=[
            *[jax.ShapeDtypeStruct((rows // 2, width), BF)] * 2,
            jax.ShapeDtypeStruct((width, 6 * HD), BF),
            jax.ShapeDtypeStruct((8, width), F32),
        ],
        scratch_shapes=[pltpu.VMEM((cols, width), F32)],
        cost_estimate=took(10),
        compiler_params=vmem(20),
    )(grad_q, here, arrived, *x_rows, weights, cosine, sine, grad_out)


def expert_kernel(part, start, more, e_low, e_high, g_low, g_high, gate_ref, w_ref, *refs):
    before, (low_ref, high_ref, hidden_ref, grads_ref), (e_ref, g_ref, act_ref, sums) = (
        refs[:more],
        refs[more : more + 4],
        refs[more + 4 :],
    )
    rows = e_ref.shape[0]
    step_id = pl.program_id(0)
    last = pl.num_programs(0) - 1
    early = step_id < pl.num_programs(0) // 2
    e_ref[...] = choose(early, e_low, e_high)
    g_ref[...] = choose(early, g_low, g_high)
    cols = w_ref.shape[1] // 3
    step = 2 * part
    lane = lax.broadcasted_iota(jnp.int32, (rows, step), 1)
    for j in range(cols // step):
        at = j * step
        first = start + 2 * j
        gate = jnp.where(lane < part, gate_ref[:, first : first + 1], gate_ref[:, first + 1 : first + 2])
        pre = dot_nn(e_ref[...], w_ref[:, at : at + step])
        up = dot_nn(e_ref[...], w_ref[:, cols + at : cols + at + step])
        grad = dot_nn(g_ref[...], w_ref[:, 2 * cols + at : 2 * cols + at + step]) * gate
        logistic = 1.0 / (1.0 + jnp.exp(-pre))
        active = pre * logistic
        act_ref[:, at : at + step] = (
            grad * up * logistic * (1.0 + pre * (1.0 - logistic))
        ).astype(BF)
        act_ref[:, cols + at : cols + at + step] = (grad * active).astype(BF)
        act_ref[:, 2 * cols + at : 2 * cols + at + step] = (active * up * gate).astype(BF)
    hidden_ref[...] = act_ref[:, 2 * cols :]
    dx = dot_nt(act_ref[:, : 2 * cols], w_ref[:, : 2 * cols])
    if more:
        dx = dx + choose(early, *before).astype(F32)

    @pl.when(early)
    def _():
        low_ref[...] = dx.astype(BF)

    @pl.when(jnp.logical_not(early))
    def _():
        high_ref[...] = dx.astype(BF)

    e_turned = e_ref[...].T
    g_turned = g_ref[...].T
    chunk = 2 * step

    def part_sum(at):
        left = e_turned if at < 2 * cols else g_turned
        return dot_nn(left, act_ref[:, at : at + chunk])

    @pl.when(step_id == 0)
    def _():
        for at in range(0, 3 * cols, chunk):
            sums[:, at : at + chunk] = part_sum(at)

    @pl.when((step_id > 0) & (step_id < last))
    def _():
        for at in range(0, 3 * cols, chunk):
            sums[:, at : at + chunk] += part_sum(at)

    @pl.when(step_id == last)
    def _():
        for at in range(0, 3 * cols, chunk):
            grads_ref[:, at : at + chunk] = (sums[:, at : at + chunk] + part_sum(at)).astype(BF)


def expert_rows(e_rows, g_rows, gates, weights, part, start, before, block):
    rows, width = 2 * e_rows[0].shape[0], e_rows[0].shape[1]
    wide = weights.shape[1] // 2
    once = pl.Buffered(1)
    column = 1 if before else 0
    return pl.pallas_call(
        lambda *refs: expert_kernel(part, start, len(before), *refs),
        grid=(rows // block,),
        in_specs=[
            *half_specs(block, width, rows, lambda i: i) * 2,
            pl.BlockSpec((block, gates.shape[1]), lambda i: (i, 0)),
            pl.BlockSpec((width, wide), lambda i: (0, column), pipeline_mode=once),
            *half_specs(block, width, rows, lambda i: i)[: len(before)],
        ],
        out_specs=[
            *half_specs(block, width, rows, lambda i: i),
            pl.BlockSpec((block, wide // 3), lambda i: (i, 0)),
            pl.BlockSpec((width, wide), lambda i: (0, 0), pipeline_mode=once),
        ],
        out_shape=[
            *[jax.ShapeDtypeStruct((rows // 2, width), BF)] * 2,
            jax.ShapeDtypeStruct((rows, wide // 3), BF),
            jax.ShapeDtypeStruct((width, wide), BF),
        ],
        scratch_shapes=[
            *[pltpu.VMEM((block, width), BF)] * 2,
            pltpu.VMEM((block, wide), BF),
            pltpu.VMEM((width, wide), F32),
        ],
        cost_estimate=took(0.01),
        compiler_params=vmem(62),
    )(*e_rows, *g_rows, gates, weights, *before)


def expert_out_kernel(h0_ref, h1_ref, w0_ref, w1_ref, low_ref, high_ref):
    out = (dot_nt(h0_ref[...], w0_ref[...]) + dot_nt(h1_ref[...], w1_ref[...])).astype(BF)
    early = pl.program_id(0) < pl.num_programs(0) // 2

    @pl.when(early)
    def _():
        low_ref[...] = out

    @pl.when(jnp.logical_not(early))
    def _():
        high_ref[...] = out


def expert_out(hidden, weights, block):
    rows, cols = hidden[0].shape
    width = weights.shape[0]
    return pl.pallas_call(
        expert_out_kernel,
        grid=(rows // block,),
        in_specs=[
            *[pl.BlockSpec((block, cols), lambda i: (i, 0))] * 2,
            pl.BlockSpec((width, cols), lambda i: (0, 2)),
            pl.BlockSpec((width, cols), lambda i: (0, 5)),
        ],
        out_specs=half_specs(block, width, rows, lambda i: i),
        out_shape=[jax.ShapeDtypeStruct((rows // 2, width), BF)] * 2,
        cost_estimate=took(2),
        compiler_params=vmem(24),
    )(*hidden, weights, weights)


def shards(
    tokens,
    segments,
    routes,
    gate_weights,
    cotangent,
    owners,
    masters,
    first_moments,
    second_moments,
    norm_gains,
    gain_first,
    gain_second,
):
    z_index = lax.axis_index("z")
    x_index = lax.axis_index("x")
    w_index = lax.axis_index("y") * 2 + lax.axis_index("c")
    slot_count, row_count, hidden = masters.shape
    slot_total = slot_count * 4
    seg_len = tokens.shape[1]
    width = tokens.shape[2]
    ctx_count = width // row_count
    matrix_count = owners.shape[0]
    experts = (matrix_count - 6) // 3
    group = experts // 2
    part = hidden // 4
    halves = 2 if row_count % 32 == 0 else 1
    team = group // 2
    x_even = x_index == 0
    info = jnp.stack([x_index, w_index]).astype(jnp.int32)

    slot_ids = jnp.arange(slot_total, dtype=jnp.int32)
    hits = owners[None, :] == slot_ids[:, None]
    held = jnp.sum(hits * (jnp.arange(matrix_count, dtype=jnp.int32) + 1)[None, :], axis=1) - 1

    local_at = owners[:6] - slot_count * w_index
    local_ok = (local_at >= 0) & (local_at < slot_count)
    attn_sent = attn_send(masters, jnp.clip(local_at, 0, slot_count - 1), local_ok.astype(jnp.int32))
    bulk = bulk_send(info, masters)
    attn_got = lax.all_to_all(attn_sent, PLANE, split_axis=0, concat_axis=0, tiled=True)
    attn_got, *bulk = together(attn_got, *bulk)
    attn_mine = jnp.sum(attn_got.reshape(2, 4, 3, row_count, part).astype(F32), axis=1).astype(BF)
    attn_mine = jnp.transpose(attn_mine, (0, 2, 1, 3)).reshape(2 * row_count, 3 * part)

    order = np.array(
        [
            [6 + 3 * (group * g + team * c + e) + k for c in range(2) for k in range(3) for e in range(team)]
            for g in range(2)
        ]
    )
    picks = jnp.take(owners, jnp.asarray(order))
    picks = jnp.stack([jnp.where(x_even, picks[0], picks[1]), jnp.where(x_even, picks[1], picks[0])])
    places = ((picks // slot_count) ^ w_index) * slot_count + picks % slot_count

    gains = norm_gains
    tokens_f = tokens[0].astype(F32)
    cot_low = cotangent[0]
    scale_one = norm_scale(tokens_f)
    attn_in = (tokens_f * scale_one * gains[0]).astype(BF)
    expert_ids = jnp.arange(experts, dtype=jnp.int32)
    gates = jnp.sum(
        jnp.where(routes[0][:, :, None] == expert_ids[None, None, :], gate_weights[0][:, :, None], 0.0),
        axis=1,
    )
    gates_high = gates.astype(BF)
    gates_low = (gates - gates_high.astype(F32)).astype(BF)
    marks = (segments[0] + 1).astype(BF)[:, None]
    spare = jnp.zeros((seg_len, 128 - 2 * experts - 1), BF)
    packed = jnp.concatenate([attn_in, gates_high, gates_low, marks, spare], axis=1)

    across = [(i, i ^ 3) for i in range(4)]
    half = seg_len // 2
    packed = after(packed, attn_got)
    over_x, over_y, from_y, attn_w = together(
        swap(packed, "x"),
        swap(packed, "y"),
        swap(bulk[2], "y"),
        lax.all_gather(attn_mine, "z", axis=0, tiled=True),
    )
    corner, from_c, from_corner = together(
        swap(over_y, "x"),
        swap(bulk[1], "c"),
        lax.ppermute(after(bulk[3], from_y), WSH, across),
    )
    mine = stack([packed, over_x, over_y, corner])
    other, *picked = together(
        swap(mine, "c"), *pick(places.reshape(-1), [bulk[0], from_c, from_y, from_corner], 2)
    )
    packed_all = (mine, other)
    extras = jnp.concatenate([rows[:, width:] for rows in packed_all], axis=0)
    gates_all = extras[:, :experts].astype(F32) + extras[:, experts : 2 * experts].astype(F32)
    my_gates = jnp.where(x_even, gates_all[:, :group], gates_all[:, group:])
    seqs = 4
    rows_all = seqs * 2 * seg_len
    marks_all = extras[:, 2 * experts].reshape(seqs, -1, 128)
    marks_tail = jnp.pad(marks_all, ((0, 0), (0, 8 - marks_all.shape[1]), (0, 0))).reshape(-1, 128)

    inverse = THETA ** (-(jnp.arange(HD // 2, dtype=F32) * 2.0 / HD))
    at = jnp.arange(seg_len, dtype=jnp.int32)
    first_pos = z_index * 2 * seg_len + x_index * seg_len + at
    second_pos = z_index * 2 * seg_len + (1 - x_index) * seg_len + at
    positions = jnp.stack([first_pos, second_pos])
    angles = positions.astype(F32)[:, :, None] * inverse[None, None, :]
    cosine = jnp.tile(jnp.cos(angles), (1, 1, 4))
    sine = jnp.tile(jnp.sin(angles), (1, 1, 4))

    query, kv_low = project(*packed_all, attn_w, cosine, sine, seg_len)
    kv_zero = jnp.concatenate([kv_low, marks_tail], axis=0)
    kv_one = shift(kv_zero, 1)
    joined = join(info, picked[:1], [swap(picked[1], "x")])
    expert_w = lax.all_gather(joined, "z", axis=0, tiled=True)
    kv_two = shift(after(kv_one, joined), 1)
    g_all = plane_gather(after(cot_low, joined))
    kv = (kv_zero, kv_one, kv_two)
    qseg = marks_all.astype(F32).reshape(2 * seqs, 1, seg_len)
    attn_mix, stat, out_low, out_high = attend(
        info, query, kv, qseg, attn_w, seg_len
    )
    resid_one = tokens_f + plane_reduce(out_low, out_high)
    scale_two = norm_scale(resid_one)
    expert_in = (resid_one * scale_two * gains[1]).astype(BF)
    e_all = plane_gather(expert_in)

    held, local_at, local_ok = together(*after((held, local_at, local_ok), expert_in))
    expert_of = (held - 6) // 3
    kind_of = (held - 6) % 3
    place = jnp.where(held >= 6, kind_of * team + expert_of % team, 0)
    side = jnp.where(held >= 6, 2 * ((expert_of // group) ^ x_index) + expert_of % group // team, 4)

    held_mine = lax.dynamic_slice_in_dim(held, w_index * slot_count, slot_count)
    table = jnp.asarray(np.array([7, 0, 0, 1, 2, 3, 3] + [4, 5, 6] * experts, np.int32))
    rates = jnp.take(jnp.asarray(kind_rates(width, hidden), F32), jnp.take(table, held_mine + 1))

    rank = jnp.cumsum(local_ok.astype(jnp.int32)) - 1
    count = rank[5] + 1
    wanted = jnp.minimum(jnp.arange(6, dtype=jnp.int32), count - 1)
    chosen = local_ok[None, :] & (rank[None, :] == wanted[:, None])
    attn_slots = jnp.sum(jnp.where(chosen, local_at[None, :], 0), axis=1)
    attn_held = jnp.sum(jnp.where(chosen, jnp.arange(6, dtype=jnp.int32)[None, :] + 1, 0), axis=1) - 1
    attn_rates = jnp.take(rates, attn_slots)
    e_all, place, side, rates, attn_slots, attn_held, attn_rates = together(
        e_all, place, side, rates, attn_slots, attn_held, attn_rates
    )

    before = ()
    hidden_all = []
    sums = []
    for c in range(2):
        *before, units, grads = expert_rows(
            e_all, g_all, my_gates, expert_w, part, team * c, before, 2 * seg_len
        )
        hidden_all.append(units)
        sums.append(lax.psum_scatter(after(grads, *sums), "z", scatter_dimension=0, tiled=True))
    grad_expert_in = plane_reduce(*before)

    cot_rows = cot_low.astype(F32)
    norm_grad_two = norm_back(resid_one, scale_two, gains[1], grad_expert_in)
    gain_grad_two = jnp.sum(grad_expert_in * resid_one * scale_two, axis=0)
    grad_resid = cot_rows + norm_grad_two
    def over(total):
        give = lax.dynamic_slice_in_dim(total, (1 - x_index) * row_count, row_count, axis=0)
        return swap(give, "x")

    dy = after(grad_resid.astype(BF), sums[0])
    over_x, over_y, moe = together(
        swap(dy, "x"), swap(dy, "y"), expert_out([after(units, dy) for units in hidden_all], expert_w, 2 * seg_len)
    )
    corner_top, corner_low, moe_got = together(
        swap(over_x[:half], "y"), swap(over_y[half:], "x"), swap(moe[1], "c")
    )
    dy_mine = stack([dy, over_x, over_y, corner_top, corner_low])
    dy_other, moe_corner = together(swap(dy_mine, "c"), corner_rows(moe[0], moe_got))
    dy_all = (dy_mine, dy_other)
    back = attend_back(info, query, kv, qseg, stat, dy_all, attn_mix, attn_w, cosine, sine, seg_len)
    (grad_q_low, dkv_zero, dkv_one, dkv_two, grad_w_out), got_one, moe_x, moe_y = together(
        back, over(sums[0]), swap(moe_corner[:half], "y"), swap(moe_corner[half:], "x")
    )
    to_x, to_y = edge_rows(moe[0], moe_got, moe_x, moe_y)

    passed_one, got_two, out_y = together(
        shift(dkv_two, -1), over(after(sums[1], grad_q_low)), swap(to_y, "y")
    )
    passing = (dkv_one + passed_one.astype(F32)).astype(BF)
    first_half, *second_half = pack(place, side, info, sums, [got_one, got_two], part, halves)
    passed, slot_grads, out_x = together(shift(passing, -1), over_wsh(first_half), swap(to_x, "x"))
    *grads, attn_grads, gain_part = project_back(
        grad_q_low, dkv_zero, passed, packed_all, attn_w, cosine, sine, grad_w_out, seg_len
    )
    attn_sum = lax.psum_scatter(attn_grads, "z", scatter_dimension=0, tiled=True)
    (grad_low, grad_high), *more = together(
        grads,
        *[over_wsh([after(array, passed) for array in arrays]) for arrays in second_half],
    )
    slot_grads = sum(more, slot_grads)

    hops = [("x", 1), ("z", 0), *[("z", k) for k in range(1, lax.axis_size("z").bit_length() - 1)], ("y", 1), ("c", 1)]

    def hop(value, at):
        axis, k = hops[at]
        if axis != "z":
            return value + swap(value, axis)
        return value + lax.ppermute(value, "z", [(i, i ^ (1 << k)) for i in range(lax.axis_size("z"))])

    gain_grad = jnp.stack([jnp.sum(gain_part, axis=0) / gains[0], gain_grad_two])
    grad_got = swap(grad_high, "c")
    grad_corner = corner_rows(grad_low, grad_got)
    grad_x, grad_y, gain_grad = together(
        swap(grad_corner[:half], "y"),
        swap(grad_corner[half:], "x"),
        hop(after(gain_grad, grad_corner), 0),
    )
    to_x, to_y = edge_rows(grad_low, grad_got, grad_x, grad_y)
    attn_sum, last_x, last_y, gain_grad, new = together(
        attn_sum,
        swap(to_x, "x"),
        swap(to_y, "y"),
        hop(gain_grad, 1),
        update(after(info, to_x), rates, slot_grads, masters, first_moments, second_moments),
    )

    attn_rows = jnp.broadcast_to(
        attn_sum.reshape(2, 1, row_count, 3 * part), (2, 4, row_count, 3 * part)
    ).reshape(8, row_count, 3 * part)
    attn_back, gain_grad = together(
        lax.all_to_all(attn_rows, PLANE, split_axis=0, concat_axis=0, tiled=True),
        hop(gain_grad, 2),
    )
    for at in range(3, len(hops)):
        gain_grad = hop(gain_grad, at)

    def own(kept, got, *rest):
        total = kept[:seg_len].astype(F32) + got[:seg_len].astype(F32)
        return total + sum(value.astype(F32) for value in rest)

    output = (resid_one + own(moe[0], moe_got, out_x, out_y)).astype(BF)
    grad_in_one = own(grad_low, grad_got, last_x, last_y)
    input_grad = grad_resid + norm_back(tokens_f, scale_one, gains[0], grad_in_one)
    new_masters, new_first, new_second = update_attn(
        attn_slots, attn_held, attn_rates, attn_back, masters, first_moments, second_moments, new
    )
    new_gains, new_gain_first, new_gain_second = adamw(
        norm_gains, gain_first, gain_second, gain_grad, GAIN_RATE, 0.0
    )
    return (
        output[None],
        input_grad[None],
        new_masters,
        new_first,
        new_second,
        new_gains,
        new_gain_first,
        new_gain_second,
    )


def solution(mesh):
    ctx, wsh = mesh.devices.shape
    fine = Mesh(mesh.devices.reshape(ctx // 2, 2, wsh // 2, 2), ("z", "x", "y", "c"))
    rows = P(WSH, ("z", "x"), None)
    marks = P(WSH, ("z", "x"))
    return jax.shard_map(
        shards,
        mesh=fine,
        in_specs=(rows, marks, rows, rows, rows, P(), rows, rows, rows, P(), P(), P()),
        out_specs=(rows, rows, rows, rows, rows, P(), P(), P()),
        check_vma=False,
    )
```

```python
import jax
import jax.numpy as jnp
import numpy as np
from jax import lax
from jax.experimental import pallas as pl
from jax.experimental.pallas import tpu as pltpu
from jax.sharding import Mesh
from jax.sharding import PartitionSpec as P

QH = 16
KVH = 8
HD = 64
STEP = 7

EPS_NORM = 1e-05
THETA = 10000.0
BETA_ONE = 0.5
BETA_TWO = 0.6
ADAM_EPS = 1e-08
DECAY = 0.1
GAIN_RATE = 0.3
NEG_BIG = -1e30
PLANE = ("x", "y", "c")
WSH = ("y", "c")
BF = jnp.bfloat16
F32 = jnp.float32


def swap(value, axis):
    return lax.ppermute(value, axis, [(0, 1), (1, 0)])


def shift(value, by):
    count = lax.axis_size("z")
    pairs = [(i, i + by) for i in range(count) if 0 <= i + by < count]
    return lax.ppermute(value, "z", pairs)


def took(us):
    return pl.CostEstimate(flops=int(us * 1e9), bytes_accessed=2**20, transcendentals=0)


def vmem(mib):
    return pltpu.CompilerParams(vmem_limit_bytes=mib * 2**20)


def whole(shape):
    return pl.BlockSpec(shape, lambda *_: (0,) * len(shape))


def half_specs(block, width, rows, at):
    low = pl.BlockSpec((block, width), lambda *g: (jnp.minimum(at(*g), rows // 2 // block - 1), 0))
    high = pl.BlockSpec((block, width), lambda *g: (jnp.maximum(at(*g) - rows // 2 // block, 0), 0))
    return [low, high]


def together(*values):
    return lax.optimization_barrier(values)


def after(value, *first):
    return lax.optimization_barrier((value, *first))[0]


def stack_kernel(*refs):
    at = 0
    for ref in refs[:-1]:
        refs[-1][at : at + ref.shape[0]] = ref[...]
        at += ref.shape[0]


def stack(pieces):
    shape = (sum(piece.shape[0] for piece in pieces), pieces[0].shape[1])
    return pl.pallas_call(
        stack_kernel,
        grid=(1,),
        in_specs=[whole(piece.shape) for piece in pieces],
        out_specs=whole(shape),
        out_shape=jax.ShapeDtypeStruct(shape, BF),
        cost_estimate=took(2),
        compiler_params=vmem(12),
    )(*pieces)


def plane_gather(rows, wait=lambda value: value, last=lambda value: value):
    half = rows.shape[0] // 2
    over_x = swap(rows, "x")
    over_y = swap(rows, "y")
    first, second = wait((over_x[:half], over_y[half:]))
    corner_top = swap(first, "y")
    corner_low = swap(second, "x")
    mine = stack([rows, over_x, over_y, corner_top, corner_low])
    return mine, swap(last(mine), "c")


def corner_kernel(kept_ref, got_ref, out_ref):
    out_ref[...] = (kept_ref[...].astype(F32) + got_ref[...].astype(F32)).astype(BF)


def corner_rows(kept, got):
    rows, width = kept.shape
    spec = pl.BlockSpec((rows // 4, width), lambda i: (3, 0))
    return pl.pallas_call(
        corner_kernel,
        grid=(1,),
        in_specs=[spec, spec],
        out_specs=whole((rows // 4, width)),
        out_shape=jax.ShapeDtypeStruct((rows // 4, width), BF),
        cost_estimate=took(1),
        compiler_params=vmem(8),
    )(kept, got)


def edge_kernel(kx_ref, gx_ref, ky_ref, gy_ref, fx_ref, fy_ref, x_ref, y_ref):
    half = fx_ref.shape[0]
    for kept, got, extra, out_ref, at in ((kx_ref, gx_ref, fx_ref, x_ref, 0), (ky_ref, gy_ref, fy_ref, y_ref, 1)):
        total = kept[...].astype(F32) + got[...].astype(F32)
        mine, rest = slice(at * half, (at + 1) * half), slice((1 - at) * half, (2 - at) * half)
        out_ref[mine] = (total[mine] + extra[...].astype(F32)).astype(BF)
        out_ref[rest] = total[rest].astype(BF)


def edge_rows(kept, got, for_x, for_y):
    rows, width = kept.shape
    step = rows // 4
    one, two = (pl.BlockSpec((step, width), lambda i, b=b: (b, 0)) for b in (1, 2))
    half = whole((step // 2, width))
    return pl.pallas_call(
        edge_kernel,
        grid=(1,),
        in_specs=[one, one, two, two, half, half],
        out_specs=[whole((step, width))] * 2,
        out_shape=[jax.ShapeDtypeStruct((step, width), BF)] * 2,
        cost_estimate=took(2),
        compiler_params=vmem(12),
    )(kept, got, kept, got, for_x, for_y)


def plane_reduce(kept, sent, waits=(None, None, None)):
    hold = [wait or (lambda value: value) for wait in waits]
    step = kept.shape[0] // 4
    half = step // 2
    got = swap(hold[0](sent), "c")
    corner = hold[1](corner_rows(kept, got))
    for_x = swap(corner[:half], "y")
    for_y = swap(corner[half:], "x")
    to_x, to_y = hold[2](edge_rows(kept, got, for_x, for_y))
    own = kept[:step].astype(F32) + got[:step].astype(F32)
    return own + swap(to_x, "x").astype(F32) + swap(to_y, "y").astype(F32)


def norm_scale(values):
    return lax.rsqrt(jnp.mean(values * values, axis=-1, keepdims=True) + EPS_NORM)


def norm_back(values, scale_row, gain_row, grad_out):
    weighted = grad_out * gain_row
    grad_in = scale_row * weighted - values * scale_row**3 * jnp.mean(
        values * weighted, axis=-1, keepdims=True
    )
    return grad_in


def kind_rates(width, hidden):
    base_rate = 0.5 * width ** (-0.5)
    return [
        base_rate,
        base_rate,
        base_rate,
        2.0 * (2 * hidden) ** (-0.5),
        base_rate,
        base_rate,
        3.0 * hidden ** (-0.5),
        base_rate,
    ]


def adamw(weight, first, second, grad, rate, decay):
    first_new = BETA_ONE * first + (1.0 - BETA_ONE) * grad
    second_new = BETA_TWO * second + (1.0 - BETA_TWO) * grad * grad
    first_hat = first_new / (1.0 - BETA_ONE**STEP)
    second_hat = second_new / (1.0 - BETA_TWO**STEP)
    weight_new = weight - rate * (first_hat / (jnp.sqrt(second_hat) + ADAM_EPS) + decay * weight)
    return (weight_new, first_new, second_new)


def dot_nn(left, right):
    return lax.dot_general(left, right, (((1,), (0,)), ((), ())), preferred_element_type=F32)


def dot_nt(left, right):
    return lax.dot_general(left, right, (((1,), (1,)), ((), ())), preferred_element_type=F32)


def dot_tn(left, right):
    return lax.dot_general(left, right, (((0,), (0,)), ((), ())), preferred_element_type=F32)


def turn(value, lane):
    low = (lane % HD) < (HD // 2)
    return jnp.where(
        low, -pltpu.roll(value, 2 * HD - HD // 2, 1), pltpu.roll(value, HD // 2, 1)
    )

def choose(early, low_ref, high_ref):
    return jnp.where(early, low_ref[...], high_ref[...])


def attn_send_kernel(at_ref, ok_ref, *refs):
    mats, out_ref = refs[:6], refs[6]

    def read(m):
        return jnp.where(ok_ref[m] == 1, mats[m][0], 0.0).astype(BF)

    part = out_ref.shape[3]
    for side in range(2):
        for kind, m in ((0, side), (2, 4 + side)):
            mat = read(m)
            for j in range(4):
                out_ref[4 * side + j, kind] = mat[:, j * part : (j + 1) * part]
    keys, values = read(2), read(3)
    for h in range(8):
        both = (keys[:, h * HD : (h + 1) * HD], values[:, h * HD : (h + 1) * HD])
        out_ref[h, 1] = jnp.concatenate(both, axis=1)


def attn_send(masters, at, ok):
    _, rows, hidden = masters.shape
    part = hidden // 4
    specs = [pl.BlockSpec((1, rows, hidden), lambda i, at, ok, m=m: (at[m], 0, 0)) for m in range(6)]
    return pl.pallas_call(
        attn_send_kernel,
        grid_spec=pltpu.PrefetchScalarGridSpec(
            num_scalar_prefetch=2,
            grid=(1,),
            in_specs=specs,
            out_specs=pl.BlockSpec((8, 3, rows, part), lambda i, at, ok: (0, 0, 0, 0)),
        ),
        out_shape=jax.ShapeDtypeStruct((8, 3, rows, part), BF),
        cost_estimate=took(3),
        compiler_params=vmem(62),
    )(at, ok, *([masters] * 6))


def bulk_send_kernel(info_ref, in_ref, *outs):
    part = outs[0].shape[2]
    for d, out_ref in enumerate(outs):
        start = pl.multiple_of((info_ref[1] ^ d) * part, part)
        out_ref[...] = in_ref[:, :, pl.ds(start, part)].astype(BF)


def bulk_send(info, masters):
    slots, rows, hidden = masters.shape
    step, part = 5 if slots % 5 == 0 else 1, hidden // 4
    return pl.pallas_call(
        bulk_send_kernel,
        grid=(slots // step,),
        in_specs=[
            pl.BlockSpec(memory_space=pltpu.SMEM),
            pl.BlockSpec((step, rows, hidden), lambda i: (i, 0, 0)),
        ],
        out_specs=[pl.BlockSpec((step, rows, part), lambda i: (i, 0, 0))] * 4,
        out_shape=[jax.ShapeDtypeStruct((slots, rows, part), BF)] * 4,
        cost_estimate=took(4),
        compiler_params=vmem(62),
    )(info, masters)


def over_wsh(arrays):
    across = [(i, i ^ 3) for i in range(4)]
    return [arrays[0], swap(arrays[1], "c"), swap(arrays[2], "y"), lax.ppermute(arrays[3], WSH, across)]


def pick_kernel(at_ref, *refs):
    slots, outs, held = refs[:4], refs[4:-1], refs[-1]
    count = slots[0].shape[0]
    part = held.shape[2]
    for d in range(4):
        held[d * count : (d + 1) * count] = slots[d][...]
    for i, out_ref in enumerate(outs):
        number = out_ref.shape[1] // part
        for k in range(number):
            out_ref[:, k * part : (k + 1) * part] = held[at_ref[i * number + k]]


def pick(places, slots, parts):
    count, rows, part = slots[0].shape
    wide = (rows, places.shape[0] // parts * part)
    return pl.pallas_call(
        pick_kernel,
        grid_spec=pltpu.PrefetchScalarGridSpec(
            num_scalar_prefetch=1,
            grid=(1,),
            in_specs=[pl.BlockSpec((count, rows, part), lambda i, a: (0, 0, 0))] * 4,
            out_specs=[pl.BlockSpec(wide, lambda i, a: (0, 0))] * parts,
            scratch_shapes=[pltpu.VMEM((4 * count, rows, part), BF)],
        ),
        out_shape=[jax.ShapeDtypeStruct(wide, BF)] * parts,
        cost_estimate=took(3),
        compiler_params=vmem(24),
    )(places, *slots)


def join_kernel(info_ref, *refs):
    count = len(refs) // 2
    keeps, gots, out_ref = refs[:count], refs[count:-1], refs[-1]
    rows, wide = keeps[0].shape
    first = info_ref[0] == 0
    for i in range(count):
        keep, got, lanes = keeps[i][...], gots[i][...], slice(i * wide, (i + 1) * wide)
        out_ref[:rows, lanes] = jnp.where(first, keep, got)
        out_ref[rows:, lanes] = jnp.where(first, got, keep)


def join(info, keeps, gots):
    rows, wide = keeps[0].shape
    shape = (2 * rows, wide * len(keeps))
    return pl.pallas_call(
        join_kernel,
        grid=(1,),
        in_specs=[pl.BlockSpec(memory_space=pltpu.SMEM)] + [whole((rows, wide))] * (2 * len(keeps)),
        out_specs=whole(shape),
        out_shape=jax.ShapeDtypeStruct(shape, BF),
        cost_estimate=took(1.5),
        compiler_params=vmem(12),
    )(info, *keeps, *gots)


def pack_kernel(place_ref, side_ref, info_ref, *refs):
    totals, gots, outs, held = refs[:2], refs[2:4], refs[4:-1], refs[-1]
    count, rows, part = outs[0].shape
    full = gots[0].shape[0]
    mine = pl.ds(pl.multiple_of(info_ref[0] * full, full), full)
    for c in range(2):
        held[c * full : (c + 1) * full] = totals[c][mine]
        held[(2 + c) * full : (3 + c) * full] = gots[c][...]
    held[4 * full :] = jnp.zeros((full, held.shape[1]), BF)
    for d in range(4):

        def one(j, carry):
            s = (info_ref[1] ^ d) * count + j
            lanes = pl.ds(pl.multiple_of(place_ref[s] * part, part), part)
            for h, out_ref in enumerate(outs[d::4]):
                start = pl.multiple_of(side_ref[s] * full + h * rows, rows)
                out_ref[j] = held[pl.ds(start, rows), lanes]
            return carry

        lax.fori_loop(0, count, one, 0)


def pack(place, side, info, totals, gots, part, halves):
    rows, wide = gots[0].shape
    shape = (place.shape[0] // 4, rows // halves, part)
    outs = pl.pallas_call(
        pack_kernel,
        grid_spec=pltpu.PrefetchScalarGridSpec(
            num_scalar_prefetch=3,
            grid=(1,),
            in_specs=[
                *[pl.BlockSpec((2 * rows, wide), lambda i, a, b, c: (0, 0))] * 2,
                *[pl.BlockSpec((rows, wide), lambda i, a, b, c: (0, 0))] * 2,
            ],
            out_specs=[pl.BlockSpec(shape, lambda i, a, b, c: (0, 0, 0))] * (4 * halves),
            scratch_shapes=[pltpu.VMEM((5 * rows, wide), BF)],
        ),
        out_shape=[jax.ShapeDtypeStruct(shape, BF)] * (4 * halves),
        cost_estimate=took(3),
        compiler_params=vmem(16),
    )(place, side, info, *totals, *gots)
    return [outs[4 * h : 4 * h + 4] for h in range(halves)]


def update_kernel(info_ref, rate_ref, *refs):
    grads, (w_ref, m_ref, v_ref, w_out, m_out, v_out) = refs[:-6], refs[-6:]
    part = grads[0].shape[2]
    rows = grads[0].shape[1]

    def one(s, carry):
        rate = rate_ref[pl.program_id(0) * w_ref.shape[0] + s]
        for i, grad_ref in enumerate(grads):
            lanes = pl.ds(pl.multiple_of((info_ref[1] ^ (i % 4)) * part, part), part)
            at = slice((i // 4) * rows, (i // 4 + 1) * rows)
            w_out[s, at, lanes], m_out[s, at, lanes], v_out[s, at, lanes] = adamw(
                w_ref[s, at, lanes],
                m_ref[s, at, lanes],
                v_ref[s, at, lanes],
                grad_ref[s].astype(F32),
                rate,
                DECAY,
            )
        return carry

    lax.fori_loop(0, w_ref.shape[0], one, 0)


def update(info, rates, grads, masters, first, second):
    slots, rows, hidden = masters.shape
    step = 4 if slots % 4 == 0 else 1
    smem = pl.BlockSpec(memory_space=pltpu.SMEM)
    spec = pl.BlockSpec((step, rows, hidden), lambda i: (i, 0, 0))
    grad_spec = pl.BlockSpec((step, *grads[0].shape[1:]), lambda i: (i, 0, 0))
    return pl.pallas_call(
        update_kernel,
        grid=(slots // step,),
        in_specs=[smem, smem] + [grad_spec] * len(grads) + [spec] * 3,
        out_specs=[spec] * 3,
        out_shape=[jax.ShapeDtypeStruct(masters.shape, F32)] * 3,
        cost_estimate=took(6),
        compiler_params=vmem(62),
    )(info, rates, *grads, masters, first, second)


def update_attn_kernel(slot_ref, held_ref, rate_ref, attn_ref, *refs):
    (w_ref, m_ref, v_ref), olds, news = refs[:3], refs[3:6], refs[6:]
    step = pl.program_id(0)
    held = held_ref[step]
    rate = rate_ref[step]
    part = w_ref.shape[2] // 4

    def write(j, grad):
        lanes = slice(j * part, (j + 1) * part)
        results = adamw(
            w_ref[0, :, lanes], m_ref[0, :, lanes], v_ref[0, :, lanes], grad.astype(F32), rate, DECAY
        )
        for new_ref, result in zip(news, results):
            new_ref[0, :, lanes] = result

    @pl.when(held < 0)
    def _():
        for old_ref, new_ref in zip(olds, news):
            new_ref[...] = old_ref[...]

    for m, side, kind in ((0, 0, 0), (1, 1, 0), (4, 0, 2), (5, 1, 2)):

        @pl.when(held == m)
        def _():
            for j in range(4):
                write(j, attn_ref[4 * side + j, :, kind * part : (kind + 1) * part])

    for m, start in ((2, part), (3, part + HD)):

        @pl.when(held == m)
        def _():
            for j in range(4):
                pieces = [attn_ref[2 * j + i, :, start : start + HD] for i in range(2)]
                write(j, jnp.concatenate(pieces, axis=1))


def update_attn(slots, held, rates, attn_back, masters, first, second, new):
    _, rows, hidden = masters.shape
    spec = pl.BlockSpec((1, rows, hidden), lambda i, at, held: (at[i], 0, 0))
    return pl.pallas_call(
        update_attn_kernel,
        grid_spec=pltpu.PrefetchScalarGridSpec(
            num_scalar_prefetch=2,
            grid=(slots.shape[0],),
            in_specs=[
                pl.BlockSpec(memory_space=pltpu.SMEM),
                pl.BlockSpec(attn_back.shape, lambda i, at, held: (0, 0, 0)),
                *[spec] * 6,
            ],
            out_specs=[spec] * 3,
        ),
        out_shape=[jax.ShapeDtypeStruct(masters.shape, F32)] * 3,
        input_output_aliases={7: 0, 8: 1, 9: 2},
        cost_estimate=took(5),
        compiler_params=vmem(62),
    )(slots, held, rates, attn_back, masters, first, second, *new)


def project_kernel(low_ref, high_ref, w_ref, cos_ref, sin_ref, q_ref, kv_ref):
    early = pl.program_id(0) < pl.num_programs(0) // 2
    both = dot_nn(choose(early, low_ref, high_ref), w_ref[...])
    cosine = cos_ref[0]
    sine = sin_ref[0]
    lane = lax.broadcasted_iota(jnp.int32, cosine.shape, 1)
    query = both[:, : 2 * HD]
    pair = both[:, 2 * HD :]
    q_ref[...] = (query * cosine + turn(query, lane) * sine).astype(BF)
    turned = pair * cosine + turn(pair, lane) * sine
    kv_ref[...] = jnp.where(lane < HD, turned, pair).astype(BF)


def project(x_low, x_high, weights, cosine, sine, block):
    rows = 2 * x_low.shape[0]
    width = weights.shape[0]
    table = pl.BlockSpec((1, block, 2 * HD), lambda i: (i % 2, 0, 0))
    return pl.pallas_call(
        project_kernel,
        grid=(rows // block,),
        in_specs=[
            *half_specs(block, width, rows, lambda i: i),
            pl.BlockSpec((width, 4 * HD), lambda i: (0, 0)),
            table,
            table,
        ],
        out_specs=[pl.BlockSpec((block, 2 * HD), lambda i: (i, 0))] * 2,
        out_shape=[jax.ShapeDtypeStruct((rows, 2 * HD), BF)] * 2,
        cost_estimate=took(6),
        compiler_params=vmem(20),
    )(x_low, x_high, weights, cosine, sine)


def head_rows(rows, head, lane, high):
    if (head == 1) != high:
        rows = pltpu.roll(rows, HD, 1)
    keep = (lane >= HD) if high else (lane < HD)
    return jnp.where(keep, rows, jnp.zeros_like(rows))


def masks(info_ref, qseg_ref, kseg, block, span):
    flip = info_ref[0]
    chunk = pl.program_id(1)
    key_at = lax.broadcasted_iota(jnp.int32, (span, 1), 0)
    query_at = lax.broadcasted_iota(jnp.int32, (1, block), 1)
    swapped = jnp.where(flip == 1, key_at ^ block, key_at)
    key_pos = jnp.where(key_at < 2 * block, swapped, -1)
    query_pos = query_at + block * jnp.where(flip == 1, 1 - chunk, chunk)
    return (key_pos <= query_pos) & (kseg == qseg_ref[0])


def load_pairs(refs, tails, kv_all, kv_turned, marks, kseg, reach):
    third = kv_all.shape[0] // 3
    for i, (ref, tail) in enumerate(zip(refs, tails)):
        kv_all[i * third : (i + 1) * third] = ref[...]
        marks[i] = tail[...].astype(F32).reshape(marks.shape[1:])
        columns = marks[i, pl.program_id(0)].T
        for j in range(third // 128):
            at = i * third + j * 128
            kseg[at : at + 128] = columns[:, j : j + 1]
    kv_turned[...] = kv_all[...].T
    seq = pl.program_id(0)
    least = jnp.min(marks[0, seq][: third // 128])
    far = jnp.max(marks[2, seq]) >= least
    near = jnp.max(marks[1, seq]) >= least
    reach[0] = jnp.where(far, 3, jnp.where(near, 2, 1)).astype(jnp.int32)


def attend_kernel(info_ref, q_ref, k0_ref, k1_ref, k2_ref, t0_ref, t1_ref, t2_ref, qseg_ref,
                  w_ref, mix_ref, stat_ref, low_ref, high_ref, kv_all, kv_turned, marks, kseg, reach):
    block = q_ref.shape[0]
    span = kv_all.shape[0]

    @pl.when(pl.program_id(1) == 0)
    def _():
        load_pairs((k0_ref, k1_ref, k2_ref), (t0_ref, t1_ref, t2_ref), kv_all, kv_turned, marks, kseg, reach)

    lane = lax.broadcasted_iota(jnp.int32, (block, 2 * HD), 1)
    query = q_ref[...] * jnp.asarray(HD**-0.5, BF)

    def attend_to(keys):
        allowed = masks(info_ref, qseg_ref, kseg[:keys], block, keys)
        mixed = []
        for head in range(2):
            scores = dot_nt(kv_all[:keys], head_rows(query, head, lane, False))
            scores = jnp.where(allowed, scores, NEG_BIG)
            top = jnp.max(scores, axis=0, keepdims=True)
            powers = jnp.exp(scores - top)
            total = jnp.sum(powers, axis=0, keepdims=True)
            stat_ref[0, 0, head : head + 1, :] = top + jnp.log(total)
            probs = (powers * (1.0 / total)).astype(BF)
            mixed.append(dot_nn(kv_turned[:, :keys], probs)[HD:])
        mix_ref[...] = jnp.concatenate(mixed, axis=0).T.astype(BF)

    for blocks in range(1, 4):

        @pl.when(reach[0] == blocks)
        def _():
            attend_to(blocks * span // 3)

    mix = mix_ref[...]
    out = dot_nt(mix, w_ref[...]).astype(BF)
    early = pl.program_id(0) < pl.num_programs(0) // 2

    @pl.when(early)
    def _():
        low_ref[...] = out

    @pl.when(jnp.logical_not(early))
    def _():
        high_ref[...] = out


def attend(info, query, kv, qseg, weights, block):
    rows = query.shape[0]
    seqs = rows // (2 * block)
    width = weights.shape[0]
    row_spec = pl.BlockSpec((block, 2 * HD), lambda s, i: (2 * s + i, 0))
    kv_spec = pl.BlockSpec((2 * block, 2 * HD), lambda s, i: (s, 0))
    tail_spec = pl.BlockSpec((8 * seqs, 2 * HD), lambda s, i: (rows // (8 * seqs), 0))
    return pl.pallas_call(
        attend_kernel,
        grid=(seqs, 2),
        in_specs=[
            pl.BlockSpec(memory_space=pltpu.SMEM),
            row_spec,
            kv_spec,
            kv_spec,
            kv_spec,
            tail_spec,
            tail_spec,
            tail_spec,
            pl.BlockSpec((1, 1, block), lambda s, i: (2 * s + i, 0, 0)),
            pl.BlockSpec((width, 2 * HD), lambda s, i: (0, 2)),
        ],
        out_specs=[
            row_spec,
            pl.BlockSpec((1, 1, 2, block), lambda s, i: (s, i, 0, 0)),
            *half_specs(block, width, rows, lambda s, i: 2 * s + i),
        ],
        out_shape=[
            jax.ShapeDtypeStruct((rows, 2 * HD), BF),
            jax.ShapeDtypeStruct((seqs, 2, 2, block), F32),
            *[jax.ShapeDtypeStruct((rows // 2, width), BF)] * 2,
        ],
        scratch_shapes=[
            pltpu.VMEM((6 * block, 2 * HD), BF),
            pltpu.VMEM((2 * HD, 6 * block), BF),
            pltpu.VMEM((3, seqs, 8, 128), F32),
            pltpu.VMEM((6 * block, 1), F32),
            pltpu.SMEM((1,), jnp.int32),
        ],
        cost_estimate=took(24),
        compiler_params=vmem(32),
    )(info, query, *kv, *kv, qseg, weights)


def attend_back_kernel(info_ref, q_ref, k0_ref, k1_ref, k2_ref, t0_ref, t1_ref, t2_ref, qseg_ref,
                       stat_ref, dy_low, dy_high, mix_ref, w_ref, cos_ref, sin_ref,
                       dq_ref, dk0_ref, dk1_ref, dk2_ref, dw_ref,
                       kv_all, kv_turned, marks, kseg, reach, sums, dw_sum, turned_sum):
    block = q_ref.shape[0]
    span = kv_all.shape[0]
    third = span // 3
    seq = pl.program_id(0)
    chunk = pl.program_id(1)

    @pl.when((chunk == 0) & (seq == 0))
    def _():
        dw_sum[...] = jnp.zeros_like(dw_sum)

    @pl.when(chunk == 0)
    def _():
        sums[...] = jnp.zeros_like(sums)
        load_pairs((k0_ref, k1_ref, k2_ref), (t0_ref, t1_ref, t2_ref), kv_all, kv_turned, marks, kseg, reach)

    lane = lax.broadcasted_iota(jnp.int32, (block, 2 * HD), 1)
    query = q_ref[...] * jnp.asarray(HD**-0.5, BF)
    grad_rows = choose(seq < pl.num_programs(0) // 2, dy_low, dy_high)
    dw_sum[...] += dot_tn(mix_ref[...], grad_rows)
    grad_mix = dot_nn(grad_rows, w_ref[...]).astype(BF)

    def attend_to(keys):
        allowed = masks(info_ref, qseg_ref, kseg[:keys], block, keys)
        grad_query = []
        for head in range(2):
            q_low = head_rows(query, head, lane, False)
            g_high = head_rows(grad_mix, head, lane, True)
            scores = dot_nt(kv_all[:keys], q_low)
            stat = stat_ref[0, 0, head : head + 1, :]
            probs = jnp.where(allowed, jnp.exp(scores - stat), 0.0)
            grad_probs = dot_nt(kv_all[:keys], g_high)
            delta = jnp.sum(probs * grad_probs, axis=0, keepdims=True)
            grad_scores = (probs * (grad_probs - delta)).astype(BF)
            sums[:keys] += dot_nn(grad_scores, q_low) + dot_nn(probs.astype(BF), g_high)
            grad_query.append(dot_nn(kv_turned[:, :keys], grad_scores)[:HD])
        turned_sum[...] = jnp.concatenate(grad_query, axis=0)

    for blocks in range(1, 4):

        @pl.when(reach[0] == blocks)
        def _():
            attend_to(blocks * span // 3)

    grad_q = turned_sum[...].T * HD**-0.5
    dq_ref[...] = (grad_q * cos_ref[0] - turn(grad_q * sin_ref[0], lane)).astype(BF)

    @pl.when(chunk == 1)
    def _():
        dk0_ref[...] = sums[:third]
        dk1_ref[...] = sums[third : 2 * third]
        dk2_ref[...] = sums[2 * third :].astype(BF)

    @pl.when((chunk == 1) & (seq == pl.num_programs(0) - 1))
    def _():
        dw_ref[...] = dw_sum[...].T.astype(BF)


def attend_back(info, query, kv, qseg, stat, grad_rows, mix, weights, cosine, sine, block):
    rows = query.shape[0]
    seqs = rows // (2 * block)
    width = weights.shape[0]
    row_spec = pl.BlockSpec((block, 2 * HD), lambda s, i: (2 * s + i, 0))
    kv_spec = pl.BlockSpec((2 * block, 2 * HD), lambda s, i: (s, 0))
    tail_spec = pl.BlockSpec((8 * seqs, 2 * HD), lambda s, i: (rows // (8 * seqs), 0))
    table = pl.BlockSpec((1, block, 2 * HD), lambda s, i: (i, 0, 0))
    return pl.pallas_call(
        attend_back_kernel,
        grid=(seqs, 2),
        in_specs=[
            pl.BlockSpec(memory_space=pltpu.SMEM),
            row_spec,
            kv_spec,
            kv_spec,
            kv_spec,
            tail_spec,
            tail_spec,
            tail_spec,
            pl.BlockSpec((1, 1, block), lambda s, i: (2 * s + i, 0, 0)),
            pl.BlockSpec((1, 1, 2, block), lambda s, i: (s, i, 0, 0)),
            *half_specs(block, width, rows, lambda s, i: 2 * s + i),
            row_spec,
            pl.BlockSpec((width, 2 * HD), lambda s, i: (0, 2)),
            table,
            table,
        ],
        out_specs=[row_spec, kv_spec, kv_spec, kv_spec, whole((width, 2 * HD))],
        out_shape=[
            jax.ShapeDtypeStruct((rows, 2 * HD), BF),
            jax.ShapeDtypeStruct((rows, 2 * HD), F32),
            jax.ShapeDtypeStruct((rows, 2 * HD), F32),
            jax.ShapeDtypeStruct((rows, 2 * HD), BF),
            jax.ShapeDtypeStruct((width, 2 * HD), BF),
        ],
        scratch_shapes=[
            pltpu.VMEM((6 * block, 2 * HD), BF),
            pltpu.VMEM((2 * HD, 6 * block), BF),
            pltpu.VMEM((3, seqs, 8, 128), F32),
            pltpu.VMEM((6 * block, 1), F32),
            pltpu.SMEM((1,), jnp.int32),
            pltpu.VMEM((6 * block, 2 * HD), F32),
            pltpu.VMEM((2 * HD, width), F32),
            pltpu.VMEM((2 * HD, block), F32),
        ],
        cost_estimate=took(12),
        compiler_params=vmem(36),
    )(info, query, *kv, *kv, qseg, stat, *grad_rows, mix, weights, cosine, sine)


def project_back_kernel(dq_ref, a_ref, b_ref, x_low, x_high, w_ref, cos_ref, sin_ref, dout_ref,
                        low_ref, high_ref, dw_ref, gain_ref, dw_sum):
    step = pl.program_id(0)

    @pl.when(step == 0)
    def _():
        dw_sum[...] = jnp.zeros_like(dw_sum)
        gain_ref[...] = jnp.zeros_like(gain_ref)

    grad = a_ref[...] + b_ref[...].astype(F32)
    lane = lax.broadcasted_iota(jnp.int32, grad.shape, 1)
    turned = grad * cos_ref[0] - turn(grad * sin_ref[0], lane)
    pair = jnp.where(lane < HD, turned, grad).astype(BF)
    both = jnp.concatenate([dq_ref[...], pair], axis=1)
    grad_in = dot_nt(both, w_ref[...])
    early = step < pl.num_programs(0) // 2

    @pl.when(early)
    def _():
        low_ref[...] = grad_in.astype(BF)

    @pl.when(jnp.logical_not(early))
    def _():
        high_ref[...] = grad_in.astype(BF)

    x_rows = choose(early, x_low, x_high)
    dw_sum[...] += dot_tn(both, x_rows)
    weighted = grad_in * x_rows.astype(F32)
    gain_ref[...] += jnp.sum(weighted.reshape(-1, 8, weighted.shape[1]), axis=0)

    @pl.when(step == pl.num_programs(0) - 1)
    def _():
        dw_ref[:, : 4 * HD] = dw_sum[...].T.astype(BF)
        dw_ref[:, 4 * HD :] = dout_ref[...]


def project_back(grad_q, here, arrived, x_rows, weights, cosine, sine, grad_out, block):
    rows = here.shape[0]
    width, cols = weights.shape[0], 4 * HD
    spec = pl.BlockSpec((block, 2 * HD), lambda i: (i, 0))
    table = pl.BlockSpec((1, block, 2 * HD), lambda i: (i % 2, 0, 0))
    return pl.pallas_call(
        project_back_kernel,
        grid=(rows // block,),
        in_specs=[
            *[spec] * 3,
            *half_specs(block, width, rows, lambda i: i),
            pl.BlockSpec((width, cols), lambda i: (0, 0)),
            table,
            table,
            whole(grad_out.shape),
        ],
        out_specs=[
            *half_specs(block, width, rows, lambda i: i),
            whole((width, 6 * HD)),
            whole((8, width)),
        ],
        out_shape=[
            *[jax.ShapeDtypeStruct((rows // 2, width), BF)] * 2,
            jax.ShapeDtypeStruct((width, 6 * HD), BF),
            jax.ShapeDtypeStruct((8, width), F32),
        ],
        scratch_shapes=[pltpu.VMEM((cols, width), F32)],
        cost_estimate=took(10),
        compiler_params=vmem(20),
    )(grad_q, here, arrived, *x_rows, weights, cosine, sine, grad_out)


def expert_kernel(part, start, more, e_low, e_high, g_low, g_high, gate_ref, w_ref, *refs):
    before, (low_ref, high_ref, hidden_ref, grads_ref), (e_ref, g_ref, act_ref, sums) = (
        refs[:more],
        refs[more : more + 4],
        refs[more + 4 :],
    )
    rows = e_ref.shape[0]
    step_id = pl.program_id(0)
    last = pl.num_programs(0) - 1
    early = step_id < pl.num_programs(0) // 2
    e_ref[...] = choose(early, e_low, e_high)
    g_ref[...] = choose(early, g_low, g_high)
    cols = w_ref.shape[1] // 3
    step = 2 * part
    lane = lax.broadcasted_iota(jnp.int32, (rows, step), 1)
    for j in range(cols // step):
        at = j * step
        first = start + 2 * j
        gate = jnp.where(lane < part, gate_ref[:, first : first + 1], gate_ref[:, first + 1 : first + 2])
        pre = dot_nn(e_ref[...], w_ref[:, at : at + step])
        up = dot_nn(e_ref[...], w_ref[:, cols + at : cols + at + step])
        grad = dot_nn(g_ref[...], w_ref[:, 2 * cols + at : 2 * cols + at + step]) * gate
        logistic = 1.0 / (1.0 + jnp.exp(-pre))
        active = pre * logistic
        act_ref[:, at : at + step] = (
            grad * up * logistic * (1.0 + pre * (1.0 - logistic))
        ).astype(BF)
        act_ref[:, cols + at : cols + at + step] = (grad * active).astype(BF)
        act_ref[:, 2 * cols + at : 2 * cols + at + step] = (active * up * gate).astype(BF)
    hidden_ref[...] = act_ref[:, 2 * cols :]
    dx = dot_nt(act_ref[:, : 2 * cols], w_ref[:, : 2 * cols])
    if more:
        dx = dx + choose(early, *before).astype(F32)

    @pl.when(early)
    def _():
        low_ref[...] = dx.astype(BF)

    @pl.when(jnp.logical_not(early))
    def _():
        high_ref[...] = dx.astype(BF)

    e_turned = e_ref[...].T
    g_turned = g_ref[...].T
    chunk = 2 * step

    def part_sum(at):
        left = e_turned if at < 2 * cols else g_turned
        return dot_nn(left, act_ref[:, at : at + chunk])

    @pl.when(step_id == 0)
    def _():
        for at in range(0, 3 * cols, chunk):
            sums[:, at : at + chunk] = part_sum(at)

    @pl.when((step_id > 0) & (step_id < last))
    def _():
        for at in range(0, 3 * cols, chunk):
            sums[:, at : at + chunk] += part_sum(at)

    @pl.when(step_id == last)
    def _():
        for at in range(0, 3 * cols, chunk):
            grads_ref[:, at : at + chunk] = (sums[:, at : at + chunk] + part_sum(at)).astype(BF)


def expert_rows(e_rows, g_rows, gates, weights, part, start, before, block):
    rows, width = 2 * e_rows[0].shape[0], e_rows[0].shape[1]
    wide = weights.shape[1] // 2
    once = pl.Buffered(1)
    column = 1 if before else 0
    return pl.pallas_call(
        lambda *refs: expert_kernel(part, start, len(before), *refs),
        grid=(rows // block,),
        in_specs=[
            *half_specs(block, width, rows, lambda i: i) * 2,
            pl.BlockSpec((block, gates.shape[1]), lambda i: (i, 0)),
            pl.BlockSpec((width, wide), lambda i: (0, column), pipeline_mode=once),
            *half_specs(block, width, rows, lambda i: i)[: len(before)],
        ],
        out_specs=[
            *half_specs(block, width, rows, lambda i: i),
            pl.BlockSpec((block, wide // 3), lambda i: (i, 0)),
            pl.BlockSpec((width, wide), lambda i: (0, 0), pipeline_mode=once),
        ],
        out_shape=[
            *[jax.ShapeDtypeStruct((rows // 2, width), BF)] * 2,
            jax.ShapeDtypeStruct((rows, wide // 3), BF),
            jax.ShapeDtypeStruct((width, wide), BF),
        ],
        scratch_shapes=[
            *[pltpu.VMEM((block, width), BF)] * 2,
            pltpu.VMEM((block, wide), BF),
            pltpu.VMEM((width, wide), F32),
        ],
        cost_estimate=took(0.01),
        compiler_params=vmem(62),
    )(*e_rows, *g_rows, gates, weights, *before)


def expert_out_kernel(h0_ref, h1_ref, w0_ref, w1_ref, low_ref, high_ref):
    out = (dot_nt(h0_ref[...], w0_ref[...]) + dot_nt(h1_ref[...], w1_ref[...])).astype(BF)
    early = pl.program_id(0) < pl.num_programs(0) // 2

    @pl.when(early)
    def _():
        low_ref[...] = out

    @pl.when(jnp.logical_not(early))
    def _():
        high_ref[...] = out


def expert_out(hidden, weights, block):
    rows, cols = hidden[0].shape
    width = weights.shape[0]
    return pl.pallas_call(
        expert_out_kernel,
        grid=(rows // block,),
        in_specs=[
            *[pl.BlockSpec((block, cols), lambda i: (i, 0))] * 2,
            pl.BlockSpec((width, cols), lambda i: (0, 2)),
            pl.BlockSpec((width, cols), lambda i: (0, 5)),
        ],
        out_specs=half_specs(block, width, rows, lambda i: i),
        out_shape=[jax.ShapeDtypeStruct((rows // 2, width), BF)] * 2,
        cost_estimate=took(2),
        compiler_params=vmem(24),
    )(*hidden, weights, weights)


def shards(
    tokens,
    segments,
    routes,
    gate_weights,
    cotangent,
    owners,
    masters,
    first_moments,
    second_moments,
    norm_gains,
    gain_first,
    gain_second,
):
    z_index = lax.axis_index("z")
    x_index = lax.axis_index("x")
    w_index = lax.axis_index("y") * 2 + lax.axis_index("c")
    slot_count, row_count, hidden = masters.shape
    slot_total = slot_count * 4
    seg_len = tokens.shape[1]
    width = tokens.shape[2]
    ctx_count = width // row_count
    matrix_count = owners.shape[0]
    experts = (matrix_count - 6) // 3
    group = experts // 2
    part = hidden // 4
    halves = 2 if row_count % 32 == 0 else 1
    team = group // 2
    x_even = x_index == 0
    info = jnp.stack([x_index, w_index]).astype(jnp.int32)

    slot_ids = jnp.arange(slot_total, dtype=jnp.int32)
    hits = owners[None, :] == slot_ids[:, None]
    held = jnp.sum(hits * (jnp.arange(matrix_count, dtype=jnp.int32) + 1)[None, :], axis=1) - 1

    local_at = owners[:6] - slot_count * w_index
    local_ok = (local_at >= 0) & (local_at < slot_count)
    attn_sent = attn_send(masters, jnp.clip(local_at, 0, slot_count - 1), local_ok.astype(jnp.int32))
    bulk = bulk_send(info, masters)
    attn_got = lax.all_to_all(attn_sent, PLANE, split_axis=0, concat_axis=0, tiled=True)
    attn_got, *bulk = together(attn_got, *bulk)
    attn_mine = jnp.sum(attn_got.reshape(2, 4, 3, row_count, part).astype(F32), axis=1).astype(BF)
    attn_mine = jnp.transpose(attn_mine, (0, 2, 1, 3)).reshape(2 * row_count, 3 * part)

    order = np.array(
        [
            [6 + 3 * (group * g + team * c + e) + k for c in range(2) for k in range(3) for e in range(team)]
            for g in range(2)
        ]
    )
    picks = jnp.take(owners, jnp.asarray(order))
    picks = jnp.stack([jnp.where(x_even, picks[0], picks[1]), jnp.where(x_even, picks[1], picks[0])])
    places = ((picks // slot_count) ^ w_index) * slot_count + picks % slot_count

    gains = norm_gains
    tokens_f = tokens[0].astype(F32)
    cot_low = cotangent[0]
    scale_one = norm_scale(tokens_f)
    attn_in = (tokens_f * scale_one * gains[0]).astype(BF)
    expert_ids = jnp.arange(experts, dtype=jnp.int32)
    gates = jnp.sum(
        jnp.where(routes[0][:, :, None] == expert_ids[None, None, :], gate_weights[0][:, :, None], 0.0),
        axis=1,
    )
    gates_high = gates.astype(BF)
    gates_low = (gates - gates_high.astype(F32)).astype(BF)
    marks = (segments[0] + 1).astype(BF)[:, None]
    spare = jnp.zeros((seg_len, 128 - 2 * experts - 1), BF)
    packed = jnp.concatenate([attn_in, gates_high, gates_low, marks, spare], axis=1)

    across = [(i, i ^ 3) for i in range(4)]
    half = seg_len // 2
    packed = after(packed, attn_got)
    over_x, over_y, from_y, attn_w = together(
        swap(packed, "x"),
        swap(packed, "y"),
        swap(bulk[2], "y"),
        lax.all_gather(attn_mine, "z", axis=0, tiled=True),
    )
    corner, from_c, from_corner = together(
        swap(over_y, "x"),
        swap(bulk[1], "c"),
        lax.ppermute(after(bulk[3], from_y), WSH, across),
    )
    mine = stack([packed, over_x, over_y, corner])
    other, *picked = together(
        swap(mine, "c"), *pick(places.reshape(-1), [bulk[0], from_c, from_y, from_corner], 2)
    )
    packed_all = (mine, other)
    extras = jnp.concatenate([rows[:, width:] for rows in packed_all], axis=0)
    gates_all = extras[:, :experts].astype(F32) + extras[:, experts : 2 * experts].astype(F32)
    my_gates = jnp.where(x_even, gates_all[:, :group], gates_all[:, group:])
    seqs = 4
    rows_all = seqs * 2 * seg_len
    marks_all = extras[:, 2 * experts].reshape(seqs, -1, 128)
    marks_tail = jnp.pad(marks_all, ((0, 0), (0, 8 - marks_all.shape[1]), (0, 0))).reshape(-1, 128)

    inverse = THETA ** (-(jnp.arange(HD // 2, dtype=F32) * 2.0 / HD))
    at = jnp.arange(seg_len, dtype=jnp.int32)
    first_pos = z_index * 2 * seg_len + x_index * seg_len + at
    second_pos = z_index * 2 * seg_len + (1 - x_index) * seg_len + at
    positions = jnp.stack([first_pos, second_pos])
    angles = positions.astype(F32)[:, :, None] * inverse[None, None, :]
    cosine = jnp.tile(jnp.cos(angles), (1, 1, 4))
    sine = jnp.tile(jnp.sin(angles), (1, 1, 4))

    query, kv_low = project(*packed_all, attn_w, cosine, sine, seg_len)
    kv_zero = jnp.concatenate([kv_low, marks_tail], axis=0)
    kv_one = shift(kv_zero, 1)
    joined = join(info, picked[:1], [swap(picked[1], "x")])
    expert_w = lax.all_gather(joined, "z", axis=0, tiled=True)
    kv_two = shift(after(kv_one, joined), 1)
    g_all = plane_gather(after(cot_low, joined))
    kv = (kv_zero, kv_one, kv_two)
    qseg = marks_all.astype(F32).reshape(2 * seqs, 1, seg_len)
    attn_mix, stat, out_low, out_high = attend(
        info, query, kv, qseg, attn_w, seg_len
    )
    resid_one = tokens_f + plane_reduce(out_low, out_high)
    scale_two = norm_scale(resid_one)
    expert_in = (resid_one * scale_two * gains[1]).astype(BF)
    e_all = plane_gather(expert_in)

    held, local_at, local_ok = together(*after((held, local_at, local_ok), expert_in))
    expert_of = (held - 6) // 3
    kind_of = (held - 6) % 3
    place = jnp.where(held >= 6, kind_of * team + expert_of % team, 0)
    side = jnp.where(held >= 6, 2 * ((expert_of // group) ^ x_index) + expert_of % group // team, 4)

    held_mine = lax.dynamic_slice_in_dim(held, w_index * slot_count, slot_count)
    table = jnp.asarray(np.array([7, 0, 0, 1, 2, 3, 3] + [4, 5, 6] * experts, np.int32))
    rates = jnp.take(jnp.asarray(kind_rates(width, hidden), F32), jnp.take(table, held_mine + 1))

    rank = jnp.cumsum(local_ok.astype(jnp.int32)) - 1
    count = rank[5] + 1
    wanted = jnp.minimum(jnp.arange(6, dtype=jnp.int32), count - 1)
    chosen = local_ok[None, :] & (rank[None, :] == wanted[:, None])
    attn_slots = jnp.sum(jnp.where(chosen, local_at[None, :], 0), axis=1)
    attn_held = jnp.sum(jnp.where(chosen, jnp.arange(6, dtype=jnp.int32)[None, :] + 1, 0), axis=1) - 1
    attn_rates = jnp.take(rates, attn_slots)
    e_all, place, side, rates, attn_slots, attn_held, attn_rates = together(
        e_all, place, side, rates, attn_slots, attn_held, attn_rates
    )

    before = ()
    hidden_all = []
    sums = []
    for c in range(2):
        *before, units, grads = expert_rows(
            e_all, g_all, my_gates, expert_w, part, team * c, before, 2 * seg_len
        )
        hidden_all.append(units)
        sums.append(lax.psum_scatter(after(grads, *sums), "z", scatter_dimension=0, tiled=True))
    grad_expert_in = plane_reduce(*before)

    cot_rows = cot_low.astype(F32)
    norm_grad_two = norm_back(resid_one, scale_two, gains[1], grad_expert_in)
    gain_grad_two = jnp.sum(grad_expert_in * resid_one * scale_two, axis=0)
    grad_resid = cot_rows + norm_grad_two
    def over(total):
        give = lax.dynamic_slice_in_dim(total, (1 - x_index) * row_count, row_count, axis=0)
        return swap(give, "x")

    dy = after(grad_resid.astype(BF), sums[0])
    over_x, over_y, moe = together(
        swap(dy, "x"), swap(dy, "y"), expert_out([after(units, dy) for units in hidden_all], expert_w, 2 * seg_len)
    )
    corner_top, corner_low, moe_got = together(
        swap(over_x[:half], "y"), swap(over_y[half:], "x"), swap(moe[1], "c")
    )
    dy_mine = stack([dy, over_x, over_y, corner_top, corner_low])
    dy_other, moe_corner = together(swap(dy_mine, "c"), corner_rows(moe[0], moe_got))
    dy_all = (dy_mine, dy_other)
    back = attend_back(info, query, kv, qseg, stat, dy_all, attn_mix, attn_w, cosine, sine, seg_len)
    (grad_q_low, dkv_zero, dkv_one, dkv_two, grad_w_out), got_one, moe_x, moe_y = together(
        back, over(sums[0]), swap(moe_corner[:half], "y"), swap(moe_corner[half:], "x")
    )
    to_x, to_y = edge_rows(moe[0], moe_got, moe_x, moe_y)

    passed_one, got_two, out_y = together(
        shift(dkv_two, -1), over(after(sums[1], grad_q_low)), swap(to_y, "y")
    )
    passing = (dkv_one + passed_one.astype(F32)).astype(BF)
    first_half, *second_half = pack(place, side, info, sums, [got_one, got_two], part, halves)
    passed, slot_grads, out_x = together(shift(passing, -1), over_wsh(first_half), swap(to_x, "x"))
    *grads, attn_grads, gain_part = project_back(
        grad_q_low, dkv_zero, passed, packed_all, attn_w, cosine, sine, grad_w_out, seg_len
    )
    attn_sum = lax.psum_scatter(attn_grads, "z", scatter_dimension=0, tiled=True)
    (grad_low, grad_high), *more = together(
        grads,
        *[over_wsh([after(array, passed) for array in arrays]) for arrays in second_half],
    )
    slot_grads = sum(more, slot_grads)

    hops = [("x", 1), ("z", 0), *[("z", k) for k in range(1, lax.axis_size("z").bit_length() - 1)], ("y", 1), ("c", 1)]

    def hop(value, at):
        axis, k = hops[at]
        if axis != "z":
            return value + swap(value, axis)
        return value + lax.ppermute(value, "z", [(i, i ^ (1 << k)) for i in range(lax.axis_size("z"))])

    gain_grad = jnp.stack([jnp.sum(gain_part, axis=0) / gains[0], gain_grad_two])
    grad_got = swap(grad_high, "c")
    grad_corner = corner_rows(grad_low, grad_got)
    grad_x, grad_y, gain_grad = together(
        swap(grad_corner[:half], "y"),
        swap(grad_corner[half:], "x"),
        hop(after(gain_grad, grad_corner), 0),
    )
    to_x, to_y = edge_rows(grad_low, grad_got, grad_x, grad_y)
    attn_sum, last_x, last_y, gain_grad, new = together(
        attn_sum,
        swap(to_x, "x"),
        swap(to_y, "y"),
        hop(gain_grad, 1),
        update(after(info, to_x), rates, slot_grads, masters, first_moments, second_moments),
    )

    attn_rows = jnp.broadcast_to(
        attn_sum.reshape(2, 1, row_count, 3 * part), (2, 4, row_count, 3 * part)
    ).reshape(8, row_count, 3 * part)
    attn_back, gain_grad = together(
        lax.all_to_all(attn_rows, PLANE, split_axis=0, concat_axis=0, tiled=True),
        hop(gain_grad, 2),
    )
    for at in range(3, len(hops)):
        gain_grad = hop(gain_grad, at)

    def own(kept, got, *rest):
        total = kept[:seg_len].astype(F32) + got[:seg_len].astype(F32)
        return total + sum(value.astype(F32) for value in rest)

    output = (resid_one + own(moe[0], moe_got, out_x, out_y)).astype(BF)
    grad_in_one = own(grad_low, grad_got, last_x, last_y)
    input_grad = grad_resid + norm_back(tokens_f, scale_one, gains[0], grad_in_one)
    new_masters, new_first, new_second = update_attn(
        attn_slots, attn_held, attn_rates, attn_back, masters, first_moments, second_moments, new
    )
    new_gains, new_gain_first, new_gain_second = adamw(
        norm_gains, gain_first, gain_second, gain_grad, GAIN_RATE, 0.0
    )
    return (
        output[None],
        input_grad[None],
        new_masters,
        new_first,
        new_second,
        new_gains,
        new_gain_first,
        new_gain_second,
    )


def solution(mesh):
    ctx, wsh = mesh.devices.shape
    fine = Mesh(mesh.devices.reshape(ctx // 2, 2, wsh // 2, 2), ("z", "x", "y", "c"))
    rows = P(WSH, ("z", "x"), None)
    marks = P(WSH, ("z", "x"))
    return jax.shard_map(
        shards,
        mesh=fine,
        in_specs=(rows, marks, rows, rows, rows, P(), rows, rows, rows, P(), P(), P()),
        out_specs=(rows, rows, rows, rows, rows, P(), P(), P()),
        check_vma=False,
    )
```
